512 devices in a mesh: curve: 32 (over z, x_lo), head: 16 (over x_hi, y, core).
Axes of the slice: x: 4 (x_hi: 2, x_lo: 2; x = x_hi * 2 + x_lo), y: 4, z: 16, core: 2. Of those that a mesh axis runs over, the one named last changes fastest.
Arguments:
- points: bfloat16 [65536, 1024], P(('curve', 'head')), may hold values from -6 to 6
- order: int32 [512, 128], P(('curve', 'head')), may hold values from 0 to 127, each once within a row
- scan_ids: int32 [65536], P(('curve', 'head')), may hold values from 0 to 3
- ln_gain: float32 [2, 1024], replicated, may hold values from 0.25 to 1.75
- w_qkv: bfloat16 [2, 1024, 3072], P(None, None, 'head'), may hold values from -7 to 7, as said below
- w_out: bfloat16 [2, 1024, 1024], P(None, 'head'), may hold values from -0.1875 to 0.1875
Outputs:
- refined: bfloat16 [65536, 1024], P(('curve', 'head'))
The draws below stay inside these ranges and needn't reach their ends.
Inputs may be any that keep to these rules, and one draw needn't show every extreme that they name: `order`: row b is a permutation of the 128 rows of block b. `w_qkv`: columns ordered by head, then query, key, value, then entry.
All inputs are finite; a program needn't handle non-finite values.
Results may differ from the reference program's by a relative error of at most 0.01.
Values may be sent and summed in bfloat16 or wider, within the bound.
No kernel may reach another device: no remote copies, remote signals or barrier semaphores. Data moves between devices by JAX's collectives and lax.ppermute only.
A program may use at most 64 MiB of HBM per device.

```python
import jax
import jax.numpy as jnp
from jax import lax

D = 1024
HEADS = 16
HEAD_DIM = 64
PATCH = 1024
SCANS = 4
TOK_DEV = 128
TOKENS = 65536
DEVICES = 512


def draw_w_qkv(key, part):
    base = jnp.clip(jax.random.normal(key, (2, D, HEADS, 3, HEAD_DIM), jnp.float32), -5.0, 5.0) * D ** (-0.5)
    return base.reshape(2, D, HEADS * 3 * HEAD_DIM).astype(jnp.bfloat16)


def touch_ends(values, own_key, smallest, largest):
    longest = values.shape.index(max(values.shape))
    spots = []
    for shift in (0, 1):
        where = [jax.random.randint(jax.random.fold_in(own_key, axis), (), 0, length) for axis, length in enumerate(values.shape)]
        where[longest] = (where[longest] + shift) % values.shape[longest]
        spots.append(tuple(where))
    return values.at[spots[0]].set(smallest).at[spots[1]].set(largest)


def level_of(own_key, extent, pieces, smallest, largest):
    def one(axis_at, blocks):
        heights = jax.random.uniform(jax.random.fold_in(jax.random.fold_in(own_key, 6), axis_at), (blocks,), jnp.float32, smallest / len(pieces), largest / len(pieces))
        return jnp.repeat(jnp.exp(heights), extent[axis_at] // blocks).reshape((-1,) + (1,) * (len(extent) - axis_at - 1))

    factor_of = one(*pieces[0])
    for cut in pieces[1:]:
        factor_of = factor_of * one(*cut)
    return factor_of


def normal_values(rng, extent, scale, most, split=(), held_as=jnp.bfloat16):
    level = level_of(rng, extent, split, -0.22, 0.18) if split else 1.0
    result = jax.random.normal(rng, extent, jnp.float32) * scale * level
    return jnp.minimum(jnp.maximum(result, -most), most).astype(held_as)


def setup_inputs(seed: int = 0) -> dict:
    splits = jax.random.split(jax.random.key(seed), 7)
    return {
        "points": normal_values(splits[0], (TOKENS, D), 1.0, 6.0, ((0, 512),)),
        "order": jax.vmap(lambda own: jax.random.permutation(own, TOK_DEV))(jax.random.split(splits[1], DEVICES)).reshape((DEVICES, TOK_DEV)).astype(jnp.int32),
        "scan_ids": touch_ends(jax.random.randint(splits[2], (TOKENS,), 0, SCANS), jax.random.fold_in(splits[2], 1), 0, SCANS - 1).astype(jnp.int32),
        "ln_gain": jnp.clip(1.0 + 0.15 * jax.random.normal(splits[3], (2, D), jnp.float32), 0.25, 1.75),
        "w_qkv": draw_w_qkv(jax.random.fold_in(splits[6], 71), 0),
        "w_out": normal_values(splits[5], (2, D, D), D ** -0.5, 0.1875, ((1, 16),)),
    }


EPSILON = 1e-05

def layer_norm(rows, gain):
    values = rows.astype(jnp.float32)
    center = values - lax.optimization_barrier(jnp.mean(values, axis=-1, keepdims=True))
    spread = lax.optimization_barrier(jnp.mean(center * center, axis=-1, keepdims=True))
    return (center * lax.rsqrt(spread + EPSILON) * gain.astype(jnp.float32)).astype(jnp.bfloat16)

def window_attention(qkv_all, tags, offset):
    length = qkv_all.shape[0]
    rolled = jnp.roll(qkv_all, -offset, axis=0)
    rolled_tags = jnp.roll(tags, -offset, axis=0)
    windows = length // PATCH
    parts = rolled.reshape(windows, PATCH, HEADS, 3, HEAD_DIM)
    part_tags = rolled_tags.reshape(windows, PATCH)

    def one_window(inputs):
        piece, piece_tags = inputs
        queries = piece[:, :, 0].astype(jnp.float32)
        keys = piece[:, :, 1].astype(jnp.float32)
        values = piece[:, :, 2].astype(jnp.float32)
        scores = jnp.einsum('qhd,khd->hqk', queries, keys) * HEAD_DIM ** (-0.5)
        allowed = piece_tags[:, None] == piece_tags[None, :]
        scores = jnp.where(allowed[None], scores, -jnp.inf)
        row_max = lax.optimization_barrier(jnp.max(scores, axis=-1, keepdims=True))
        expo = jnp.exp(scores - row_max)
        probs = (expo / lax.optimization_barrier(jnp.sum(expo, axis=-1, keepdims=True))).astype(jnp.bfloat16)
        heads = jnp.einsum('hqk,khd->qhd', probs.astype(jnp.float32), values)
        return heads.astype(jnp.bfloat16)
    outputs = lax.map(one_window, (parts, part_tags))
    return jnp.roll(outputs.reshape(length, HEADS * HEAD_DIM), offset, axis=0)

def reference(points, order, scan_ids, ln_gain, w_qkv, w_out):
    blocks = points.reshape(-1, TOK_DEV, D)
    stream = jax.vmap(lambda block, picks: block[picks])(blocks, order.astype(jnp.int32)).reshape(-1, D)
    for layer_index in range(2):
        normed = layer_norm(stream, ln_gain[layer_index])
        qkv_all = jnp.dot(normed, w_qkv[layer_index], preferred_element_type=jnp.float32).astype(jnp.bfloat16)
        heads = window_attention(qkv_all, scan_ids, layer_index * (PATCH // 2))
        update = jnp.dot(heads, w_out[layer_index], preferred_element_type=jnp.float32)
        stream = (stream.astype(jnp.float32) + update).astype(jnp.bfloat16)
    return stream
```

```python
import jax
import jax.numpy as jnp
import numpy as np
from jax import lax
from jax.experimental import pallas as pl
from jax.experimental.pallas import tpu as pltpu
from jax.sharding import Mesh
from jax.sharding import PartitionSpec as P

HEAD_DIM = 64
D = 1024
ROWS = 128
PATCH = 1024
HALF = 512
LANES = 128
BLOCKS = D // LANES
EXT = D + 16
EPSILON = 1e-05
FAR = -1e30
AXES = ("z", "xl", "xh", "y", "c")
F32 = jnp.float32
BF16 = jnp.bfloat16


def pairs(shape, move):
    result = []
    for i in range(int(np.prod(shape))):
        place = tuple(int(v) for v in np.unravel_index(i, shape))
        result.append((i, int(np.ravel_multi_index(move(*place), shape))))
    return result


def dot(a, b):
    return lax.dot_general(a, b, (((1,), (0,)), ((), ())), preferred_element_type=F32)


def dot_nt(a, b):
    return lax.dot_general(a, b, (((1,), (1,)), ((), ())), preferred_element_type=F32)


def layer_norm(values, gain):
    center = values - jnp.mean(values, axis=-1, keepdims=True)
    spread = jnp.mean(center * center, axis=-1, keepdims=True)
    return (center * lax.rsqrt(spread + EPSILON) * gain).astype(BF16)


def side_by_side(ref, index):
    return jnp.concatenate([ref[index, b * LANES : (b + 1) * LANES, :] for b in range(BLOCKS)], axis=1)


def tag_columns(rows):
    return jnp.transpose(jnp.concatenate(rows, axis=0))


def one_hot(columns, block):
    lane = lax.broadcasted_iota(jnp.int32, (ROWS, LANES), 1).astype(F32)
    return columns[:, block : block + 1] == lane


def attend(queries, hot, keys_ref, values_ref):
    lane = lax.broadcasted_iota(jnp.int32, queries.shape, 1)
    results = []
    for head in range(2):
        own = jnp.where(lane // HEAD_DIM == head, queries, jnp.zeros_like(queries))
        scores = dot_nt(keys_ref[...], jnp.concatenate([own, hot], axis=1))
        top = jnp.max(scores, axis=0, keepdims=True)
        probs = jnp.exp(scores - top).astype(BF16)
        sums = dot(values_ref[head], probs)
        results.append(sums[:HEAD_DIM] / sums[HEAD_DIM : HEAD_DIM + 1])
    return jnp.transpose(jnp.concatenate(results, axis=0)).astype(BF16)


def put_values(values_ref, values):
    turned = jnp.transpose(values.astype(F32)).astype(BF16)
    for head in range(2):
        values_ref[head, :HEAD_DIM, :] = turned[head * HEAD_DIM : (head + 1) * HEAD_DIM]
        values_ref[head, HEAD_DIM:, :] = jnp.ones((16, PATCH), BF16)


def order_kernel(points, order, tags, out):
    row = lax.broadcasted_iota(jnp.int32, (ROWS, ROWS), 0)
    picks = jnp.transpose((row == order[...]).astype(F32)).astype(BF16)
    ordered = dot(picks, points[...]).astype(BF16)
    tag_rows = jnp.broadcast_to(tags[...].astype(F32), (16, LANES)).astype(BF16)
    for copy in range(4):
        for b in range(BLOCKS):
            out[copy, b * LANES : (b + 1) * LANES, :] = ordered[:, b * LANES : (b + 1) * LANES]
        out[copy, D:, :] = tag_rows


def first_kernel(near, far, gain, weights, out, normed, queries, keys, values, hots):
    rows = []
    for s, ref in enumerate((near, far)):
        for y in range(4):
            block = s * 4 + y
            normed[block * ROWS : (block + 1) * ROWS, :] = layer_norm(
                side_by_side(ref, y).astype(F32), gain[...]
            )
            rows.append(ref[y, D:, :].astype(F32)[:1])
    columns = tag_columns(rows)
    qkv = dot(normed[...], weights[...]).astype(BF16)
    queries[...] = qkv[:, :LANES] * jnp.asarray(HEAD_DIM**-0.5, BF16)
    keys[:, :LANES] = qkv[:, LANES : 2 * LANES]
    put_values(values, qkv[:, 2 * LANES :])
    for block in range(8):
        hot = one_hot(columns, block)
        span = slice(block * ROWS, (block + 1) * ROWS)
        hots[span, :] = jnp.where(hot, 1.0, 0.0).astype(BF16)
        keys[span, LANES:] = jnp.where(hot, 0.0, FAR).astype(BF16)
    for part in range(4):
        span = slice(part * 256, (part + 1) * 256)
        result = attend(queries[span, :], hots[span, :], keys, values)
        for copy in range(4):
            out[copy, span, :] = result


def middle_kernel(
    near, far, o_near, o_far, w_near, w_far, gain, weights,
    q_out, kv_p, kv_q, st_out, heads, update, normed,
):
    xh, my_y = lax.axis_index("xh"), lax.axis_index("y")
    for part, kv in enumerate((kv_p, kv_q)):
        half = 1 - xh if part == 0 else xh
        for s in range(2):
            for yy in range(2):
                y = half * 2 + yy
                span = slice((s * 2 + yy) * ROWS, (s * 2 + yy + 1) * ROWS)
                at_near = pl.ds(pl.multiple_of((s * 4 + y) * ROWS, ROWS), ROWS)
                at_far = pl.ds(pl.multiple_of(((1 - s) * 4 + y) * ROWS, ROWS), ROWS)
                for g in range(4):
                    heads[span, g * LANES : (g + 1) * LANES] = o_near[g, at_near, :]
                    heads[span, (g + 4) * LANES : (g + 5) * LANES] = o_far[g, at_far, :]
        update[...] = dot(heads[:, :HALF], w_near[...]) + dot(heads[:, HALF:], w_far[...])
        rows = []
        for s, ref in enumerate((near, far)):
            for yy in range(2):
                y = half * 2 + yy
                span = slice((s * 2 + yy) * ROWS, (s * 2 + yy + 1) * ROWS)
                stream = (side_by_side(ref, y).astype(F32) + update[span, :]).astype(BF16)
                normed[span, :] = layer_norm(stream.astype(F32), gain[...])
                rows.append(ref[y, D:, :].astype(F32)[:1])
                if s == 0:

                    @pl.when(y == my_y)
                    def _(stream=stream):
                        st_out[...] = stream

        qkv = dot(normed[...], weights[...]).astype(BF16)
        q_out[part] = qkv[:, :LANES] * jnp.asarray(HEAD_DIM**-0.5, BF16)
        kv[:HALF, :] = qkv[:, LANES : 2 * LANES]
        kv[HALF:D, :] = qkv[:, 2 * LANES :]
        kv[D:, :] = jnp.concatenate(rows + [jnp.zeros((12, LANES), F32)], axis=0).astype(BF16)


def second_kernel(queries, kv_p, kv_q, halo_p, halo_q, out, keys, values, hots):
    xh, c = lax.axis_index("xh"), lax.axis_index("c")
    for part, (mine, other) in enumerate(((kv_p, halo_p), (kv_q, halo_q))):
        half = 1 - xh if part == 0 else xh
        keys[:HALF, :LANES] = mine[:HALF, :]
        keys[HALF:, :LANES] = other[:HALF, :]
        put_values(values, jnp.concatenate([mine[HALF:D, :], other[HALF:D, :]], axis=0))
        columns = tag_columns([mine[D:, :].astype(F32)[:4], other[D:, :].astype(F32)[:4]])
        for block in range(8):
            hot = one_hot(columns, block)
            span = slice(block * ROWS, (block + 1) * ROWS)
            if block < 4:
                hots[span, :] = jnp.where(hot, 1.0, 0.0).astype(BF16)
            keys[span, LANES:] = jnp.where(hot, 0.0, FAR).astype(BF16)
        for s in range(2):
            span = slice(s * 256, (s + 1) * 256)
            result = attend(queries[part, span, :], hots[span, :], keys, values)
            core = c if s == 0 else 1 - c
            for yy in range(2):
                out[(half * 2 + yy) * 2 + core] = result[yy * ROWS : (yy + 1) * ROWS]


def last_kernel(parts, w_near, w_far, stream, out, heads):
    c = lax.axis_index("c")
    for s in range(2):
        core = c if s == 0 else 1 - c
        for y in range(4):
            heads[:, (s * 4 + y) * LANES : (s * 4 + y + 1) * LANES] = parts[y * 2 + core]
    update = dot(heads[:, :HALF], w_near[...]) + dot(heads[:, HALF:], w_far[...])
    out[...] = (stream[...].astype(F32) + update).astype(BF16)


def call(kernel, outs, scratch, *args):
    return pl.pallas_call(
        kernel,
        out_shape=[jax.ShapeDtypeStruct(shape, BF16) for shape in outs],
        in_specs=[pl.BlockSpec(memory_space=pltpu.VMEM)] * len(args),
        out_specs=[pl.BlockSpec(memory_space=pltpu.VMEM)] * len(outs),
        scratch_shapes=[pltpu.VMEM(shape, dtype) for shape, dtype in scratch],
        compiler_params=pltpu.CompilerParams(vmem_limit_bytes=32 * 1024 * 1024),
    )(*args)


def after(value, *others):
    return lax.optimization_barrier((value, *others))[0]


def solution(mesh):
    curve, heads = mesh.shape["curve"], mesh.shape["head"]
    shape = (curve // 2, 2, 2, heads // 4, 2)
    deep = shape[0]
    other_core = pairs(shape, lambda z, xl, xh, y, c: (z, xl, xh, y, 1 - c))
    mirror = pairs(shape, lambda z, xl, xh, y, c: (z, 1 - xl, 1 - xh, y, c))
    inner = pairs(shape, lambda z, xl, xh, y, c: (z, xl, 1 - xh, y, c))

    def across(z, xl, xh, y, c):
        here = z * 2 + xl
        there = (here + (1 if xh else -1)) % (2 * deep)
        return there // 2, there % 2, 1 - xh, y, c

    outer = pairs(shape, across)

    def by_head(own, mirrored):
        first = lax.axis_index("xh") == 0
        return jnp.where(first, own, mirrored), jnp.where(first, mirrored, own)

    def over_y(copies):
        return lax.all_to_all(copies, "y", 0, 0, tiled=True)

    def swapped(array):
        return lax.ppermute(array, AXES, other_core)

    def projections(own, mirrored):
        low, high = by_head(own, mirrored)
        picks = []
        for kind in range(3):
            cut = slice(kind * HEAD_DIM, (kind + 1) * HEAD_DIM)
            picks += [low[:, cut], high[:, cut]]
        return jnp.concatenate(picks, axis=1)

    def on_device(points, order, scan_ids, ln_gain, w_qkv, w_out):
        (copies,) = call(
            order_kernel, [(4, EXT, LANES)], [], points, order, scan_ids.reshape(1, ROWS)
        )
        w_qkv_far = [lax.ppermute(w_qkv[l], AXES, mirror) for l in range(2)]
        w_out_far = lax.ppermute(w_out, AXES, mirror)
        x_near = over_y(copies)
        x_far = swapped(x_near)
        weights = [projections(w_qkv[l], w_qkv_far[l]) for l in range(2)]
        outs = jnp.concatenate(by_head(w_out, w_out_far), axis=1)
        out_near, out_far = [], []
        for l in range(2):
            got = over_y(jnp.broadcast_to(outs[l], (4, ROWS, D)))
            out_near.append(got.reshape(HALF, D))
            out_far.append(swapped(got).reshape(HALF, D))
        (o_copies,) = call(
            first_kernel,
            [(4, PATCH, LANES)],
            [
                ((PATCH, D), BF16),
                ((PATCH, LANES), BF16),
                ((PATCH, 2 * LANES), BF16),
                ((2, HEAD_DIM + 16, PATCH), BF16),
                ((PATCH, LANES), BF16),
            ],
            x_near, x_far, ln_gain[0:1], weights[0],
        )
        o_near = over_y(o_copies)
        o_far = swapped(o_near)
        queries, kv_p, kv_q, stream = call(
            middle_kernel,
            [(2, HALF, LANES), (EXT, LANES), (EXT, LANES), (ROWS, D)],
            [((HALF, D), BF16), ((HALF, D), F32), ((HALF, D), BF16)],
            x_near, x_far, o_near, o_far, out_near[0], out_far[0], ln_gain[1:2], weights[1],
        )
        halo_p = lax.ppermute(kv_p, AXES, inner)
        halo_q = lax.ppermute(kv_q, AXES, outer)
        (parts,) = call(
            second_kernel,
            [(8, ROWS, LANES)],
            [
                ((PATCH, 2 * LANES), BF16),
                ((2, HEAD_DIM + 16, PATCH), BF16),
                ((HALF, LANES), BF16),
            ],
            queries, kv_p, kv_q, halo_p, halo_q,
        )
        parts = lax.all_to_all(parts, ("y", "c"), 0, 0, tiled=True)
        (result,) = call(
            last_kernel, [(ROWS, D)], [((ROWS, D), BF16)], parts, out_near[1], out_far[1], stream
        )
        return result

    curve_axes, head_axes = ("z", "xl"), ("xh", "y", "c")
    every = curve_axes + head_axes
    return jax.shard_map(
        on_device,
        mesh=Mesh(mesh.devices.reshape(shape), AXES),
        in_specs=(P(every, None), P(every, None), P(every), P(), P(None, None, head_axes), P(None, head_axes, None)),
        out_specs=P(every, None),
        check_vma=False,
    )
```

```python
import functools

import jax
import jax.numpy as jnp
import numpy as np
from jax import lax
from jax.experimental import pallas as pl
from jax.experimental.pallas import tpu as pltpu
from jax.sharding import Mesh
from jax.sharding import PartitionSpec as P

HEAD_DIM = 64
D = 1024
ROWS = 128
PATCH = 1024
HALF = 512
LANES = 128
BLOCKS = D // LANES
EXT = D + 16
EPSILON = 1e-05
FAR = -1e30
AXES = ("z", "xl", "xh", "y", "c")
F32 = jnp.float32
BF16 = jnp.bfloat16


def pairs(shape, move):
    result = []
    for i in range(int(np.prod(shape))):
        place = tuple(int(v) for v in np.unravel_index(i, shape))
        result.append((i, int(np.ravel_multi_index(move(*place), shape))))
    return result


def dot(a, b):
    return lax.dot_general(a, b, (((1,), (0,)), ((), ())), preferred_element_type=F32)


def dot_nt(a, b):
    return lax.dot_general(a, b, (((1,), (1,)), ((), ())), preferred_element_type=F32)


def layer_norm(values, gain):
    center = values - jnp.mean(values, axis=-1, keepdims=True)
    spread = jnp.mean(center * center, axis=-1, keepdims=True)
    return (center * lax.rsqrt(spread + EPSILON) * gain).astype(BF16)


def side_by_side(ref, index):
    return jnp.concatenate([ref[index, b * LANES : (b + 1) * LANES, :] for b in range(BLOCKS)], axis=1)


def tag_columns(rows):
    return jnp.transpose(jnp.concatenate(rows, axis=0))


def one_hot(columns, block):
    lane = lax.broadcasted_iota(jnp.int32, (ROWS, LANES), 1).astype(F32)
    return columns[:, block : block + 1] == lane


def attend(queries, hot, keys_ref, values_ref):
    lane = lax.broadcasted_iota(jnp.int32, queries.shape, 1)
    results = []
    for head in range(2):
        own = jnp.where(lane // HEAD_DIM == head, queries, jnp.zeros_like(queries))
        scores = dot_nt(keys_ref[...], jnp.concatenate([own, hot], axis=1))
        top = jnp.max(scores, axis=0, keepdims=True)
        probs = jnp.exp(scores - top).astype(BF16)
        sums = dot(values_ref[head], probs)
        results.append(sums[:HEAD_DIM] / sums[HEAD_DIM : HEAD_DIM + 1])
    return jnp.transpose(jnp.concatenate(results, axis=0)).astype(BF16)


def order_kernel(points, order, tags, out):
    row = lax.broadcasted_iota(jnp.int32, (ROWS, ROWS), 0)
    picks = jnp.transpose((row == order[...]).astype(F32)).astype(BF16)
    ordered = dot(picks, points[...]).astype(BF16)
    tag_rows = jnp.broadcast_to(tags[...].astype(F32), (16, LANES)).astype(BF16)
    for copy in range(4):
        for b in range(BLOCKS):
            out[copy, b * LANES : (b + 1) * LANES, :] = ordered[:, b * LANES : (b + 1) * LANES]
        out[copy, D:, :] = tag_rows


def joined(own, mirrored, kind):
    cut = slice(kind * HEAD_DIM, (kind + 1) * HEAD_DIM)
    return jnp.concatenate([own[cut, :], mirrored[cut, :]], axis=0)


def project(normed, own, mirrored, queries, keys, turned):
    both = jnp.concatenate([joined(own, mirrored, 0), joined(own, mirrored, 1)], axis=0)
    found = dot_nt(normed[...], both).astype(BF16)
    queries[...] = found[:, :LANES] * jnp.asarray(HEAD_DIM**-0.5, BF16)
    keys[...] = found[:, LANES:]
    turned[...] = dot_nt(joined(own, mirrored, 2), normed[...]).astype(BF16)


def put_values(values_ref, span, turned, swap):
    for head in range(2):
        from_head = 1 - head if swap else head
        values_ref[head, :HEAD_DIM, span] = turned[from_head * HEAD_DIM : (from_head + 1) * HEAD_DIM]


def first_kernel(near, far, gain, own, mirrored, out, normed, queries, keys, turned, values, hots):
    rows = []
    for s, ref in enumerate((near, far)):
        for y in range(4):
            block = s * 4 + y
            normed[block * ROWS : (block + 1) * ROWS, :] = layer_norm(
                side_by_side(ref, y).astype(F32), gain[...]
            )
            rows.append(ref[y, D:, :].astype(F32)[:1])
    columns = tag_columns(rows)
    project(normed, own, mirrored, queries, keys.at[:, :LANES], turned)
    put_values(values, slice(0, PATCH), turned, False)
    values[:, HEAD_DIM:, :] = jnp.ones((2, 16, PATCH), BF16)
    for block in range(8):
        hot = one_hot(columns, block)
        span = slice(block * ROWS, (block + 1) * ROWS)
        hots[span, :] = jnp.where(hot, 1.0, 0.0).astype(BF16)
        keys[span, LANES:] = jnp.where(hot, 0.0, FAR).astype(BF16)
    for part in range(4):
        span = slice(part * 256, (part + 1) * 256)
        result = attend(queries[span, :], hots[span, :], keys, values)
        for copy in range(4):
            out[copy, span, :] = result


def half_of(part):
    xh = lax.axis_index("xh")
    return xh if part else 1 - xh


def middle_kernel(
    part, near, far, o_near, o_far, w_near, w_far, gain, own, mirrored,
    q_out, kv, st_out, heads, update, normed, turned,
):
    my_y, half = lax.axis_index("y"), half_of(part)
    for s in range(2):
        for yy in range(2):
            y = half * 2 + yy
            span = slice((s * 2 + yy) * ROWS, (s * 2 + yy + 1) * ROWS)
            at_near = pl.ds(pl.multiple_of((s * 4 + y) * ROWS, ROWS), ROWS)
            at_far = pl.ds(pl.multiple_of(((1 - s) * 4 + y) * ROWS, ROWS), ROWS)
            for g in range(4):
                heads[span, g * LANES : (g + 1) * LANES] = o_near[g, at_near, :]
                heads[span, (g + 4) * LANES : (g + 5) * LANES] = o_far[g, at_far, :]
    update[...] = dot(heads[:, :HALF], w_near[...]) + dot(heads[:, HALF:], w_far[...])
    rows = []
    for s, ref in enumerate((near, far)):
        for yy in range(2):
            y = half * 2 + yy
            span = slice((s * 2 + yy) * ROWS, (s * 2 + yy + 1) * ROWS)
            stream = (side_by_side(ref, y).astype(F32) + update[span, :]).astype(BF16)
            normed[span, :] = layer_norm(stream.astype(F32), gain[...])
            rows.append(ref[y, D:, :].astype(F32)[:1])
            if s == 0:

                @pl.when(y == my_y)
                def _(stream=stream):
                    st_out[...] = stream

    project(normed, own, mirrored, q_out, kv.at[:HALF, :], turned)
    for b in range(4):
        kv[HALF + b * LANES : HALF + (b + 1) * LANES, :] = turned[:, b * LANES : (b + 1) * LANES]
    kv[D:, :] = jnp.concatenate(rows + [jnp.zeros((12, LANES), F32)], axis=0).astype(BF16)


def second_kernel(part, *refs):
    if part:
        queries, mine, other, had, out, keys, values, hots = refs
    else:
        queries, mine, other, out, keys, values, hots = refs
    half, c = half_of(part), lax.axis_index("c")
    keys[:HALF, :LANES] = mine[:HALF, :]
    keys[HALF:, :HEAD_DIM] = other[:HALF, HEAD_DIM:]
    keys[HALF:, HEAD_DIM:LANES] = other[:HALF, :HEAD_DIM]
    for b in range(4):
        cut = slice(HALF + b * LANES, HALF + (b + 1) * LANES)
        put_values(values, slice(b * LANES, (b + 1) * LANES), mine[cut, :], False)
        put_values(values, slice(HALF + b * LANES, HALF + (b + 1) * LANES), other[cut, :], True)
    values[:, HEAD_DIM:, :] = jnp.ones((2, 16, PATCH), BF16)
    columns = tag_columns([mine[D:, :].astype(F32)[:4], other[D:, :].astype(F32)[:4]])
    for block in range(8):
        hot = one_hot(columns, block)
        span = slice(block * ROWS, (block + 1) * ROWS)
        if block < 4:
            hots[span, :] = jnp.where(hot, 1.0, 0.0).astype(BF16)
        keys[span, LANES:] = jnp.where(hot, 0.0, FAR).astype(BF16)
    for s in range(2):
        span = slice(s * 256, (s + 1) * 256)
        result = attend(queries[span, :], hots[span, :], keys, values)
        core = c if s == 0 else 1 - c
        for yy in range(2):
            block = result[yy * ROWS : (yy + 1) * ROWS]
            if part:
                out[(half * 2 + yy) * 2 + core] = block
                out[((1 - half) * 2 + yy) * 2 + core] = had[s * 2 + yy]
            else:
                out[s * 2 + yy] = block


def last_kernel(parts, w_near, w_far, stream_p, stream_q, out, heads):
    c, y_half = lax.axis_index("c"), lax.axis_index("y") // 2
    for s in range(2):
        core = c if s == 0 else 1 - c
        for y in range(4):
            heads[:, (s * 4 + y) * LANES : (s * 4 + y + 1) * LANES] = parts[y * 2 + core]
    update = dot(heads[:, :HALF], w_near[...]) + dot(heads[:, HALF:], w_far[...])

    def put(stream):
        out[...] = (stream[...].astype(F32) + update).astype(BF16)

    pl.when(y_half == half_of(0))(lambda: put(stream_p))
    pl.when(y_half == half_of(1))(lambda: put(stream_q))


def relay_kernel(own, far, ready, out):
    for copy in range(out.shape[0]):
        out[copy, : own.shape[0]] = own[...]
        out[copy, own.shape[0] :] = far[...]


def pass_kernel(array, ready, out):
    out[...] = array[...]


def call(kernel, micros, outs, scratch, *args, wait_for=()):
    vmem, anywhere = pl.BlockSpec(memory_space=pltpu.VMEM), pl.BlockSpec(memory_space=pl.ANY)
    return pl.pallas_call(
        kernel,
        out_shape=[jax.ShapeDtypeStruct(shape, BF16) for shape in outs],
        in_specs=[vmem] * len(args) + [anywhere] * len(wait_for),
        out_specs=[vmem] * len(outs),
        scratch_shapes=[pltpu.VMEM(shape, dtype) for shape, dtype in scratch],
        compiler_params=pltpu.CompilerParams(vmem_limit_bytes=16 * 1024 * 1024),
        cost_estimate=pl.CostEstimate(
            flops=int(micros * 1.1e9), bytes_accessed=0, transcendentals=0
        ),
    )(*args, *wait_for)


def solution(mesh):
    curve, heads = mesh.shape["curve"], mesh.shape["head"]
    shape = (curve // 2, 2, 2, heads // 4, 2)
    deep = shape[0]
    other_core = pairs(shape, lambda z, xl, xh, y, c: (z, xl, xh, y, 1 - c))
    mirror = pairs(shape, lambda z, xl, xh, y, c: (z, 1 - xl, 1 - xh, y, c))
    inner = pairs(shape, lambda z, xl, xh, y, c: (z, xl, 1 - xh, y, c))

    def across(z, xl, xh, y, c):
        here = z * 2 + xl
        there = (here + (1 if xh else -1)) % (2 * deep)
        return there // 2, there % 2, 1 - xh, y, c

    outer = pairs(shape, across)

    def over_y(copies):
        return lax.all_to_all(copies, "y", 0, 0, tiled=True)

    def swapped(array):
        return lax.ppermute(array, AXES, other_core)

    def on_device(points, order, scan_ids, ln_gain, w_qkv, w_out):
        w_turned = jnp.swapaxes(w_qkv, 1, 2)
        (copies,) = call(
            order_kernel, 1.2, [(4, EXT, LANES)], [], points, order, scan_ids.reshape(1, ROWS)
        )
        first_far = lax.ppermute(w_turned[0], AXES, mirror)
        w_out_far = lax.ppermute(w_out, AXES, mirror)
        x_near = over_y(copies)
        x_near, first_far, w_out_far = lax.optimization_barrier((x_near, first_far, w_out_far))
        x_far = swapped(x_near)

        def gathered_out(layer, ready):
            (outs,) = call(
                relay_kernel, 1, [(4, ROWS, D)], [], w_out[layer], w_out_far[layer], wait_for=(ready,)
            )
            return over_y(outs)

        out_near = gathered_out(0, x_near)
        (second_own,) = call(
            pass_kernel, 1, [(3 * HEAD_DIM, D)], [], w_turned[1], wait_for=(x_near,)
        )
        second_far = lax.ppermute(second_own, AXES, mirror)
        (o_copies,) = call(
            first_kernel,
            8,
            [(4, PATCH, LANES)],
            [
                ((PATCH, D), BF16),
                ((PATCH, LANES), BF16),
                ((PATCH, 2 * LANES), BF16),
                ((LANES, PATCH), BF16),
                ((2, HEAD_DIM + 16, PATCH), BF16),
                ((PATCH, LANES), BF16),
            ],
            x_near, x_far, ln_gain[0:1], w_turned[0], first_far,
        )
        o_copies, out_near = lax.optimization_barrier((o_copies, out_near))
        out_far = swapped(out_near)
        o_near = over_y(o_copies)
        o_near, second_far, out_far = lax.optimization_barrier((o_near, second_far, out_far))
        o_far = swapped(o_near)
        out_first = out_near.reshape(HALF, D), out_far.reshape(HALF, D)
        last_near = gathered_out(1, o_near)
        middle, halos = [], []
        for part, links in enumerate((inner, outer)):
            middle.append(
                call(
                    functools.partial(middle_kernel, part),
                    4,
                    [(HALF, LANES), (EXT, LANES), (ROWS, D)],
                    [((HALF, D), BF16), ((HALF, D), F32), ((HALF, D), BF16), ((LANES, HALF), BF16)],
                    x_near, x_far, o_near, o_far, *out_first, ln_gain[1:2], second_own, second_far,
                )
            )
            halos.append(lax.ppermute(middle[part][1], AXES, links))
        halos[0], *middle[1] = lax.optimization_barrier((halos[0], *middle[1]))
        parts = None
        for part in range(2):
            queries, kv, _ = middle[part]
            (parts,) = call(
                functools.partial(second_kernel, part),
                3,
                [(8 if part else 4, ROWS, LANES)],
                [
                    ((PATCH, 2 * LANES), BF16),
                    ((2, HEAD_DIM + 16, PATCH), BF16),
                    ((HALF, LANES), BF16),
                ],
                queries, kv, halos[part], *([parts] if part else []),
            )
            if part == 0:
                last_near, parts = lax.optimization_barrier((last_near, parts))
                out_second = last_near.reshape(HALF, D), swapped(last_near).reshape(HALF, D)
        parts = lax.all_to_all(parts, ("y", "c"), 0, 0, tiled=True)
        (result,) = call(
            last_kernel, 1.5, [(ROWS, D)], [((ROWS, D), BF16)],
            parts, *out_second, middle[0][2], middle[1][2],
        )
        return result

    curve_axes, head_axes = ("z", "xl"), ("xh", "y", "c")
    every = curve_axes + head_axes
    return jax.shard_map(
        on_device,
        mesh=Mesh(mesh.devices.reshape(shape), AXES),
        in_specs=(P(every, None), P(every, None), P(every), P(), P(None, None, head_axes), P(None, head_axes, None)),
        out_specs=P(every, None),
        check_vma=False,
    )
```

```python
import functools

import jax
import jax.numpy as jnp
import numpy as np
from jax import lax
from jax.experimental import pallas as pl
from jax.experimental.pallas import tpu as pltpu
from jax.sharding import Mesh
from jax.sharding import PartitionSpec as P

HEAD_DIM = 64
D = 1024
ROWS = 128
PATCH = 1024
HALF = 512
LANES = 128
BLOCKS = D // LANES
EXT = D + 16
EPSILON = 1e-05
FAR = -1e30
AXES = ("z", "xl", "xh", "y", "c")
F32 = jnp.float32
BF16 = jnp.bfloat16


def pairs(shape, move):
    result = []
    for i in range(int(np.prod(shape))):
        place = tuple(int(v) for v in np.unravel_index(i, shape))
        result.append((i, int(np.ravel_multi_index(move(*place), shape))))
    return result


def dot(a, b):
    return lax.dot_general(a, b, (((1,), (0,)), ((), ())), preferred_element_type=F32)


def dot_nt(a, b):
    return lax.dot_general(a, b, (((1,), (1,)), ((), ())), preferred_element_type=F32)


def layer_norm(values, gain):
    center = values - jnp.mean(values, axis=-1, keepdims=True)
    spread = jnp.mean(center * center, axis=-1, keepdims=True)
    return (center * lax.rsqrt(spread + EPSILON) * gain).astype(BF16)


def side_by_side(ref, index):
    return jnp.concatenate([ref[index, b * LANES : (b + 1) * LANES, :] for b in range(BLOCKS)], axis=1)


def tag_columns(rows):
    return jnp.transpose(jnp.concatenate(rows, axis=0))


def one_hot(columns, block):
    lane = lax.broadcasted_iota(jnp.int32, (ROWS, LANES), 1).astype(F32)
    return columns[:, block : block + 1] == lane


def attend(queries, hot, keys_ref, values_ref):
    lane = lax.broadcasted_iota(jnp.int32, queries.shape, 1)
    results = []
    for head in range(2):
        own = jnp.where(lane // HEAD_DIM == head, queries, jnp.zeros_like(queries))
        scores = dot_nt(keys_ref[...], jnp.concatenate([own, hot], axis=1))
        top = jnp.max(scores, axis=0, keepdims=True)
        probs = jnp.exp(scores - top).astype(BF16)
        sums = dot(values_ref[head], probs)
        results.append(sums[:HEAD_DIM] / sums[HEAD_DIM : HEAD_DIM + 1])
    return jnp.transpose(jnp.concatenate(results, axis=0)).astype(BF16)


def order_kernel(points, order, tags, out):
    row = lax.broadcasted_iota(jnp.int32, (ROWS, ROWS), 0)
    picks = jnp.transpose((row == order[...]).astype(F32)).astype(BF16)
    ordered = dot(picks, points[...]).astype(BF16)
    tag_rows = jnp.broadcast_to(tags[...].astype(F32), (16, LANES)).astype(BF16)
    for copy in range(4):
        for b in range(BLOCKS):
            out[copy, b * LANES : (b + 1) * LANES, :] = ordered[:, b * LANES : (b + 1) * LANES]
        out[copy, D:, :] = tag_rows


def joined(own, mirrored, kind):
    cut = slice(kind * HEAD_DIM, (kind + 1) * HEAD_DIM)
    return jnp.concatenate([own[cut, :], mirrored[cut, :]], axis=0)


def fetch(sources, targets, sems):
    copies = [pltpu.make_async_copy(a, b, sems.at[i]) for i, (a, b) in enumerate(zip(sources, targets))]
    for copy in copies:
        copy.start()
    return copies


def project(normed, own, mirrored, queries, keys, turned):
    both = jnp.concatenate([joined(own, mirrored, 0), joined(own, mirrored, 1)], axis=0)
    found = dot_nt(normed[...], both).astype(BF16)
    queries[...] = found[:, :LANES] * jnp.asarray(HEAD_DIM**-0.5, BF16)
    keys[...] = found[:, LANES:]
    turned[...] = dot_nt(joined(own, mirrored, 2), normed[...]).astype(BF16)


def put_values(values_ref, span, turned, swap):
    for head in range(2):
        from_head = 1 - head if swap else head
        values_ref[head, :HEAD_DIM, span] = turned[from_head * HEAD_DIM : (from_head + 1) * HEAD_DIM]


def first_kernel(
    near, far, gain, own_at, mirrored_at, out,
    normed, queries, keys, turned, values, hots, own, mirrored, sems,
):
    copies = fetch((own_at, mirrored_at), (own, mirrored), sems)
    rows = []
    for s, ref in enumerate((near, far)):
        for y in range(4):
            block = s * 4 + y
            normed[block * ROWS : (block + 1) * ROWS, :] = layer_norm(
                side_by_side(ref, y).astype(F32), gain[...]
            )
            rows.append(ref[y, D:, :].astype(F32)[:1])
    columns = tag_columns(rows)
    for copy in copies:
        copy.wait()
    project(normed, own, mirrored, queries, keys.at[:, :LANES], turned)
    put_values(values, slice(0, PATCH), turned, False)
    values[:, HEAD_DIM:, :] = jnp.ones((2, 16, PATCH), BF16)
    for block in range(8):
        hot = one_hot(columns, block)
        span = slice(block * ROWS, (block + 1) * ROWS)
        hots[span, :] = jnp.where(hot, 1.0, 0.0).astype(BF16)
        keys[span, LANES:] = jnp.where(hot, 0.0, FAR).astype(BF16)
    for part in range(4):
        span = slice(part * 256, (part + 1) * 256)
        result = attend(queries[span, :], hots[span, :], keys, values)
        for copy in range(4):
            out[copy, span, :] = result


def half_of(part):
    xh = lax.axis_index("xh")
    return xh if part else 1 - xh


def middle_kernel(
    part, near, far, gain, o_near, o_far, w_mine, w_mine_far, w_next, w_next_far, own_at, mirrored_at,
    q_out, kv, st_out, heads, update, normed, turned, w, own, mirrored, o_sems, w_sems,
):
    my_y, xl, half = lax.axis_index("y"), lax.axis_index("xl"), half_of(part)
    sources, targets = [], []
    for s in range(2):
        span = slice(s * 256, (s + 1) * 256)
        at_near = pl.ds(pl.multiple_of(s * HALF + half * 256, 256), 256)
        at_far = pl.ds(pl.multiple_of((1 - s) * HALF + half * 256, 256), 256)
        for g in range(4):
            sources += [o_near.at[g, at_near, :], o_far.at[g, at_far, :]]
            targets += [
                heads.at[span, g * LANES : (g + 1) * LANES],
                heads.at[span, (g + 4) * LANES : (g + 5) * LANES],
            ]
    o_copies = fetch(sources, targets, o_sems)
    w_copies = fetch(
        (w_mine, w_mine_far, w_next, w_next_far, own_at, mirrored_at),
        (w.at[0, :HALF], w.at[0, HALF:], w.at[1, :HALF], w.at[1, HALF:], own, mirrored),
        w_sems,
    )
    for copy in o_copies + w_copies[:2]:
        copy.wait()
    update[:, pl.ds(pl.multiple_of(xl * HALF, HALF), HALF)] = dot(heads[...], w[0])
    for copy in w_copies[2:]:
        copy.wait()
    update[:, pl.ds(pl.multiple_of((1 - xl) * HALF, HALF), HALF)] = dot(heads[...], w[1])
    rows = []
    for s, ref in enumerate((near, far)):
        for yy in range(2):
            y = half * 2 + yy
            span = slice((s * 2 + yy) * ROWS, (s * 2 + yy + 1) * ROWS)
            stream = (side_by_side(ref, y).astype(F32) + update[span, :]).astype(BF16)
            normed[span, :] = layer_norm(stream.astype(F32), gain[...])
            rows.append(ref[y, D:, :].astype(F32)[:1])
            if s == 0:

                @pl.when(y == my_y)
                def _(stream=stream):
                    st_out[...] = stream

    project(normed, own, mirrored, q_out, kv.at[:HALF, :], turned)
    for b in range(4):
        kv[HALF + b * LANES : HALF + (b + 1) * LANES, :] = turned[:, b * LANES : (b + 1) * LANES]
    kv[D:, :] = jnp.concatenate(rows + [jnp.zeros((12, LANES), F32)], axis=0).astype(BF16)


def second_kernel(part, *refs):
    if part:
        queries, mine, other, had, out, keys, values, hots = refs
    else:
        queries, mine, other, ready, out, keys, values, hots = refs
    half, c = half_of(part), lax.axis_index("c")
    keys[:HALF, :LANES] = mine[:HALF, :]
    keys[HALF:, :HEAD_DIM] = other[:HALF, HEAD_DIM:]
    keys[HALF:, HEAD_DIM:LANES] = other[:HALF, :HEAD_DIM]
    for b in range(4):
        cut = slice(HALF + b * LANES, HALF + (b + 1) * LANES)
        put_values(values, slice(b * LANES, (b + 1) * LANES), mine[cut, :], False)
        put_values(values, slice(HALF + b * LANES, HALF + (b + 1) * LANES), other[cut, :], True)
    values[:, HEAD_DIM:, :] = jnp.ones((2, 16, PATCH), BF16)
    columns = tag_columns([mine[D:, :].astype(F32)[:4], other[D:, :].astype(F32)[:4]])
    for block in range(8):
        hot = one_hot(columns, block)
        span = slice(block * ROWS, (block + 1) * ROWS)
        if block < 4:
            hots[span, :] = jnp.where(hot, 1.0, 0.0).astype(BF16)
        keys[span, LANES:] = jnp.where(hot, 0.0, FAR).astype(BF16)
    for s in range(2):
        span = slice(s * 256, (s + 1) * 256)
        result = attend(queries[span, :], hots[span, :], keys, values)
        core = c if s == 0 else 1 - c
        for yy in range(2):
            block = result[yy * ROWS : (yy + 1) * ROWS]
            if part:
                out[(half * 2 + yy) * 2 + core] = block
                out[((1 - half) * 2 + yy) * 2 + core] = had[s * 2 + yy]
            else:
                out[s * 2 + yy] = block


def last_kernel(parts, w, stream_p, stream_q, out, heads):
    xh, y_half = lax.axis_index("xh"), lax.axis_index("y") // 2
    for b in range(4):
        pair = []
        for block in (parts[2 * b], parts[2 * b + 1]):
            turned = jnp.concatenate([block[:, HEAD_DIM:], block[:, :HEAD_DIM]], axis=1)
            pair.append(jnp.where(xh == 0, block, turned))
        for k in range(2):
            cut = slice(k * HEAD_DIM, (k + 1) * HEAD_DIM)
            heads[:, (k * 4 + b) * LANES : (k * 4 + b + 1) * LANES] = jnp.concatenate(
                [pair[0][:, cut], pair[1][:, cut]], axis=1
            )
    update = dot(heads[...], w[...])

    def put(stream):
        out[...] = (stream[...].astype(F32) + update).astype(BF16)

    pl.when(y_half == half_of(0))(lambda: put(stream_p))
    pl.when(y_half == half_of(1))(lambda: put(stream_q))


def relay_kernel(own, far, ready, out):
    cut = pl.ds(pl.multiple_of(lax.axis_index("xl") * HALF, HALF), HALF)
    for copy in range(out.shape[0]):
        out[copy, : own.shape[0]] = own[:, cut]
        out[copy, own.shape[0] :] = far[:, cut]


def pass_kernel(array, ready, out):
    out[...] = array[...]


def call(kernel, micros, outs, scratch, *args, late=(), semaphores=(), megabytes=16):
    vmem, anywhere = pl.BlockSpec(memory_space=pltpu.VMEM), pl.BlockSpec(memory_space=pl.ANY)
    return pl.pallas_call(
        kernel,
        out_shape=[jax.ShapeDtypeStruct(shape, BF16) for shape in outs],
        in_specs=[vmem] * len(args) + [anywhere] * len(late),
        out_specs=[vmem] * len(outs),
        scratch_shapes=[pltpu.VMEM(shape, dtype) for shape, dtype in scratch]
        + [pltpu.SemaphoreType.DMA((count,)) for count in semaphores],
        compiler_params=pltpu.CompilerParams(vmem_limit_bytes=megabytes * 1024 * 1024),
        cost_estimate=pl.CostEstimate(
            flops=int(micros * 1.1e9), bytes_accessed=0, transcendentals=0
        ),
    )(*args, *late)


def solution(mesh):
    curve, heads = mesh.shape["curve"], mesh.shape["head"]
    shape = (curve // 2, 2, 2, heads // 4, 2)
    deep = shape[0]
    head_axes = ("xh", "y", "c")
    other_core = pairs(shape, lambda z, xl, xh, y, c: (z, xl, xh, y, 1 - c))
    mirror = pairs(shape, lambda z, xl, xh, y, c: (z, 1 - xl, 1 - xh, y, c))
    beside = pairs(shape, lambda z, xl, xh, y, c: (z, 1 - xl, xh, y, c))
    inner = pairs(shape, lambda z, xl, xh, y, c: (z, xl, 1 - xh, y, c))

    def across(z, xl, xh, y, c):
        here = z * 2 + xl
        there = (here + (1 if xh else -1)) % (2 * deep)
        return there // 2, there % 2, 1 - xh, y, c

    outer = pairs(shape, across)

    def over_y(copies):
        return lax.all_to_all(copies, "y", 0, 0, tiled=True)

    def swapped(array):
        return lax.ppermute(array, AXES, other_core)

    def on_device(points, order, scan_ids, ln_gain, w_qkv, w_out):
        w_turned = jnp.swapaxes(w_qkv, 1, 2)
        w_last = lax.all_gather(w_out[1], head_axes, axis=0, tiled=True)
        (copies,) = call(
            order_kernel, 1.2, [(4, EXT, LANES)], [], points, order, scan_ids.reshape(1, ROWS)
        )
        first_far = lax.ppermute(w_turned[0], AXES, mirror)
        out_far = lax.ppermute(w_out[0], AXES, mirror)
        x_near = over_y(copies)
        x_near, first_far, out_far = lax.optimization_barrier((x_near, first_far, out_far))
        x_far = swapped(x_near)
        (shares,) = call(
            relay_kernel, 1, [(4, ROWS, HALF)], [], w_out[0], out_far, late=(x_near,), megabytes=4
        )
        w_mine = over_y(shares)
        (second_own,) = call(
            pass_kernel, 1, [(3 * HEAD_DIM, D)], [], w_turned[1], late=(x_near,), megabytes=4
        )
        second_far = lax.ppermute(second_own, AXES, mirror)
        projection = [((3 * HEAD_DIM, D), BF16)] * 2
        (o_copies,) = call(
            first_kernel,
            8,
            [(4, PATCH, LANES)],
            [
                ((PATCH, D), BF16),
                ((PATCH, LANES), BF16),
                ((PATCH, 2 * LANES), BF16),
                ((LANES, PATCH), BF16),
                ((2, HEAD_DIM + 16, PATCH), BF16),
                ((PATCH, LANES), BF16),
                *projection,
            ],
            x_near, x_far, ln_gain[0:1],
            late=(w_turned[0], first_far), semaphores=(2,),
        )
        o_copies, w_mine = lax.optimization_barrier((o_copies, w_mine))
        w_next = lax.ppermute(w_mine, AXES, beside)
        w_mine_far = swapped(w_mine)
        o_near = over_y(o_copies)
        o_near, second_far, w_next, w_mine_far = lax.optimization_barrier(
            (o_near, second_far, w_next, w_mine_far)
        )
        o_far = swapped(o_near)
        w_next_far = swapped(w_next)
        w_first = [w.reshape(HALF, HALF) for w in (w_mine, w_mine_far, w_next, w_next_far)]
        middle, halos = [], []
        for part, links in enumerate((inner, outer)):
            middle.append(
                call(
                    functools.partial(middle_kernel, part),
                    4,
                    [(HALF, LANES), (EXT, LANES), (ROWS, D)],
                    [
                        ((HALF, D), BF16),
                        ((HALF, D), F32),
                        ((HALF, D), BF16),
                        ((LANES, HALF), BF16),
                        ((2, D, HALF), BF16),
                        *projection,
                    ],
                    x_near, x_far, ln_gain[1:2],
                    late=(o_near, o_far, *w_first, second_own, second_far), semaphores=(16, 6),
                )
            )
            halos.append(lax.ppermute(middle[part][1], AXES, links))
        parts = None
        for part in range(2):
            queries, kv, _ = middle[part]
            (parts,) = call(
                functools.partial(second_kernel, part),
                3 if part else 0,
                [(8 if part else 4, ROWS, LANES)],
                [
                    ((PATCH, 2 * LANES), BF16),
                    ((2, HEAD_DIM + 16, PATCH), BF16),
                    ((HALF, LANES), BF16),
                ],
                queries, kv, halos[part], *([parts] if part else []),
                late=() if part else (middle[1][1],), megabytes=8,
            )
        parts = lax.all_to_all(parts, ("y", "c"), 0, 0, tiled=True)
        (result,) = call(
            last_kernel, 1.5, [(ROWS, D)], [((ROWS, D), BF16)],
            parts, w_last, middle[0][2], middle[1][2], megabytes=8,
        )
        return result

    every = ("z", "xl") + head_axes
    return jax.shard_map(
        on_device,
        mesh=Mesh(mesh.devices.reshape(shape), AXES),
        in_specs=(P(every, None), P(every, None), P(every), P(), P(None, None, head_axes), P(None, head_axes, None)),
        out_specs=P(every, None),
        check_vma=False,
    )
```

```python
import functools

import jax
import jax.numpy as jnp
import numpy as np
from jax import lax
from jax.experimental import pallas as pl
from jax.experimental.pallas import tpu as pltpu
from jax.sharding import Mesh
from jax.sharding import PartitionSpec as P

HEAD_DIM = 64
D = 1024
ROWS = 128
PATCH = 1024
HALF = 512
LANES = 128
BLOCKS = D // LANES
EXT = D + 16
EPSILON = 1e-05
FAR = -1e30
AXES = ("z", "xl", "xh", "y", "c")
F32 = jnp.float32
BF16 = jnp.bfloat16


def pairs(shape, move):
    result = []
    for i in range(int(np.prod(shape))):
        place = tuple(int(v) for v in np.unravel_index(i, shape))
        result.append((i, int(np.ravel_multi_index(move(*place), shape))))
    return result


def dot(a, b):
    return lax.dot_general(a, b, (((1,), (0,)), ((), ())), preferred_element_type=F32)


def dot_nt(a, b):
    return lax.dot_general(a, b, (((1,), (1,)), ((), ())), preferred_element_type=F32)


def layer_norm(values, gain):
    center = values - jnp.mean(values, axis=-1, keepdims=True)
    spread = jnp.mean(center * center, axis=-1, keepdims=True)
    return (center * lax.rsqrt(spread + EPSILON) * gain).astype(BF16)


def side_by_side(ref, index):
    return jnp.concatenate([ref[index, b * LANES : (b + 1) * LANES, :] for b in range(BLOCKS)], axis=1)


def tag_columns(rows):
    return jnp.transpose(jnp.concatenate(rows, axis=0))


def one_hot(columns, block):
    lane = lax.broadcasted_iota(jnp.int32, (ROWS, LANES), 1).astype(F32)
    return columns[:, block : block + 1] == lane


def attend(queries, hot, keys_ref, values_ref):
    lane = lax.broadcasted_iota(jnp.int32, queries.shape, 1)
    results = []
    for head in range(2):
        own = jnp.where(lane // HEAD_DIM == head, queries, jnp.zeros_like(queries))
        scores = dot_nt(keys_ref[...], jnp.concatenate([own, hot], axis=1))
        top = jnp.max(scores, axis=0, keepdims=True)
        probs = jnp.exp(scores - top).astype(BF16)
        sums = dot(values_ref[head], probs)
        results.append(sums[:HEAD_DIM] / sums[HEAD_DIM : HEAD_DIM + 1])
    return jnp.transpose(jnp.concatenate(results, axis=0)).astype(BF16)


def fetch(sources, targets, sems):
    copies = [pltpu.make_async_copy(a, b, sems.at[i]) for i, (a, b) in enumerate(zip(sources, targets))]
    for copy in copies:
        copy.start()
    return copies


def order_kernel(points_at, order_at, tags_at, out, points, order, tags, sems):
    copies = fetch((order_at, points_at, tags_at), (order, points, tags), sems)
    for copy in copies:
        copy.wait()
    row = lax.broadcasted_iota(jnp.int32, (ROWS, ROWS), 0)
    picks = jnp.transpose((row == order[...]).astype(F32)).astype(BF16)
    ordered = dot(picks, points[...]).astype(BF16)
    tag_rows = jnp.broadcast_to(tags[...].astype(F32), (16, LANES)).astype(BF16)
    for copy in range(4):
        for b in range(BLOCKS):
            out[copy, b * LANES : (b + 1) * LANES, :] = ordered[:, b * LANES : (b + 1) * LANES]
        out[copy, D:, :] = tag_rows


def joined(own, mirrored, kind):
    cut = slice(kind * HEAD_DIM, (kind + 1) * HEAD_DIM)
    return jnp.concatenate([own[cut, :], mirrored[cut, :]], axis=0)


def project(normed, own, mirrored, queries, keys, turned):
    both = jnp.concatenate([joined(own, mirrored, 0), joined(own, mirrored, 1)], axis=0)
    found = dot_nt(normed[...], both).astype(BF16)
    queries[...] = found[:, :LANES] * jnp.asarray(HEAD_DIM**-0.5, BF16)
    keys[...] = found[:, LANES:]
    turned[...] = dot_nt(joined(own, mirrored, 2), normed[...]).astype(BF16)


def put_values(values_ref, span, turned, swap):
    for head in range(2):
        from_head = 1 - head if swap else head
        values_ref[head, :HEAD_DIM, span] = turned[from_head * HEAD_DIM : (from_head + 1) * HEAD_DIM]


def first_kernel(
    near, far, gain, own_at, mirrored_at, out,
    normed, queries, keys, turned, values, hots, own, mirrored, sems,
):
    copies = fetch((own_at, mirrored_at), (own, mirrored), sems)
    rows = []
    for s, ref in enumerate((near, far)):
        for y in range(4):
            block = s * 4 + y
            normed[block * ROWS : (block + 1) * ROWS, :] = layer_norm(
                side_by_side(ref, y).astype(F32), gain[...]
            )
            rows.append(ref[y, D:, :].astype(F32)[:1])
    columns = tag_columns(rows)
    for copy in copies:
        copy.wait()
    project(normed, own, mirrored, queries, keys.at[:, :LANES], turned)
    put_values(values, slice(0, PATCH), turned, False)
    values[:, HEAD_DIM:, :] = jnp.ones((2, 16, PATCH), BF16)
    for block in range(8):
        hot = one_hot(columns, block)
        span = slice(block * ROWS, (block + 1) * ROWS)
        hots[span, :] = jnp.where(hot, 1.0, 0.0).astype(BF16)
        keys[span, LANES:] = jnp.where(hot, 0.0, FAR).astype(BF16)
    for part in range(4):
        span = slice(part * 256, (part + 1) * 256)
        result = attend(queries[span, :], hots[span, :], keys, values)
        for copy in range(4):
            out[copy, span, :] = result


def half_of(part):
    xh = lax.axis_index("xh")
    return xh if part else 1 - xh


def middle_kernel(
    part, near, far, gain, o_near, o_far, w_own, w_own_far, w_mir, w_mir_far, own_at, mirrored_at,
    ready, q_out, kv, st_out, heads, update, normed, turned, w, own, mirrored, o_sems, w_sems,
):
    my_y, half = lax.axis_index("y"), half_of(part)
    sources, targets = [], []
    for s in range(2):
        span = slice(s * 256, (s + 1) * 256)
        at_near = pl.ds(pl.multiple_of(s * HALF + half * 256, 256), 256)
        at_far = pl.ds(pl.multiple_of((1 - s) * HALF + half * 256, 256), 256)
        for g in range(4):
            sources += [o_near.at[g, at_near, :], o_far.at[g, at_far, :]]
            targets += [
                heads.at[span, g * LANES : (g + 1) * LANES],
                heads.at[span, (g + 4) * LANES : (g + 5) * LANES],
            ]
    o_copies = fetch(sources, targets, o_sems)
    sources, targets = [own_at, mirrored_at], [own, mirrored]
    for i, ref in enumerate((w_own, w_mir, w_own_far, w_mir_far)):
        for g in range(4):
            row = (i // 2 * 4 + g) * LANES + i % 2 * HEAD_DIM
            sources.append(ref.at[g])
            targets.append(w.at[row : row + HEAD_DIM, :])
    w_copies = fetch(sources, targets, w_sems)
    for copy in o_copies + w_copies:
        copy.wait()
    update[...] = dot(heads[...], w[...])
    rows = []
    for s, ref in enumerate((near, far)):
        for yy in range(2):
            y = half * 2 + yy
            span = slice((s * 2 + yy) * ROWS, (s * 2 + yy + 1) * ROWS)
            stream = (side_by_side(ref, y).astype(F32) + update[span, :]).astype(BF16)
            normed[span, :] = layer_norm(stream.astype(F32), gain[...])
            rows.append(ref[y, D:, :].astype(F32)[:1])
            if s == 0:

                @pl.when(y == my_y)
                def _(stream=stream):
                    st_out[...] = stream

    project(normed, own, mirrored, q_out, kv.at[:HALF, :], turned)
    for b in range(4):
        kv[HALF + b * LANES : HALF + (b + 1) * LANES, :] = turned[:, b * LANES : (b + 1) * LANES]
    kv[D:, :] = jnp.concatenate(rows + [jnp.zeros((12, LANES), F32)], axis=0).astype(BF16)


def second_kernel(part, *refs):
    if part:
        queries, mine, other, had, out, keys, values, hots = refs
    else:
        queries, mine, other, ready, out, keys, values, hots = refs
    half, c = half_of(part), lax.axis_index("c")
    keys[:HALF, :LANES] = mine[:HALF, :]
    keys[HALF:, :HEAD_DIM] = other[:HALF, HEAD_DIM:]
    keys[HALF:, HEAD_DIM:LANES] = other[:HALF, :HEAD_DIM]
    for b in range(4):
        cut = slice(HALF + b * LANES, HALF + (b + 1) * LANES)
        put_values(values, slice(b * LANES, (b + 1) * LANES), mine[cut, :], False)
        put_values(values, slice(HALF + b * LANES, HALF + (b + 1) * LANES), other[cut, :], True)
    values[:, HEAD_DIM:, :] = jnp.ones((2, 16, PATCH), BF16)
    columns = tag_columns([mine[D:, :].astype(F32)[:4], other[D:, :].astype(F32)[:4]])
    for block in range(8):
        hot = one_hot(columns, block)
        span = slice(block * ROWS, (block + 1) * ROWS)
        if block < 4:
            hots[span, :] = jnp.where(hot, 1.0, 0.0).astype(BF16)
        keys[span, LANES:] = jnp.where(hot, 0.0, FAR).astype(BF16)
    for s in range(2):
        span = slice(s * 256, (s + 1) * 256)
        result = attend(queries[span, :], hots[span, :], keys, values)
        core = c if s == 0 else 1 - c
        for yy in range(2):
            block = result[yy * ROWS : (yy + 1) * ROWS]
            if part:
                out[(half * 2 + yy) * 2 + core] = block
                out[((1 - half) * 2 + yy) * 2 + core] = had[s * 2 + yy]
            else:
                out[s * 2 + yy] = block


def last_kernel(parts, w, stream_p, stream_q, out, heads):
    y_half = lax.axis_index("y") // 2
    for g in range(8):
        heads[:, g * LANES : (g + 1) * LANES] = parts[g]
    update = dot(heads[...], w[...])

    def put(stream):
        out[...] = (stream[...].astype(F32) + update).astype(BF16)

    pl.when(y_half == half_of(0))(lambda: put(stream_p))
    pl.when(y_half == half_of(1))(lambda: put(stream_q))


def relay_kernel(count, *refs):
    out = refs[-1]
    for copy in range(out.shape[0]):
        for i in range(count):
            out[copy, i * HEAD_DIM : (i + 1) * HEAD_DIM] = refs[i][...]


def call(kernel, micros, outs, scratch, *args, late=(), semaphores=(), megabytes=16):
    vmem, anywhere = pl.BlockSpec(memory_space=pltpu.VMEM), pl.BlockSpec(memory_space=pl.ANY)
    return pl.pallas_call(
        kernel,
        out_shape=[jax.ShapeDtypeStruct(shape, BF16) for shape in outs],
        in_specs=[vmem] * len(args) + [anywhere] * len(late),
        out_specs=[vmem] * len(outs),
        scratch_shapes=[pltpu.VMEM(shape, dtype) for shape, dtype in scratch]
        + [pltpu.SemaphoreType.DMA((count,)) for count in semaphores],
        compiler_params=pltpu.CompilerParams(vmem_limit_bytes=megabytes * 1024 * 1024),
        cost_estimate=pl.CostEstimate(
            flops=int(micros * 1.1e9), bytes_accessed=0, transcendentals=0
        ),
    )(*args, *late)


def solution(mesh):
    curve, heads = mesh.shape["curve"], mesh.shape["head"]
    shape = (curve // 2, 2, 2, heads // 4, 2)
    deep = shape[0]
    head_axes = ("xh", "y", "c")
    other_core = pairs(shape, lambda z, xl, xh, y, c: (z, xl, xh, y, 1 - c))
    mirror = pairs(shape, lambda z, xl, xh, y, c: (z, 1 - xl, 1 - xh, y, c))
    beside = pairs(shape, lambda z, xl, xh, y, c: (z, 1 - xl, xh, y, c))
    inner = pairs(shape, lambda z, xl, xh, y, c: (z, xl, 1 - xh, y, c))

    def across(z, xl, xh, y, c):
        here = z * 2 + xl
        there = (here + (1 if xh else -1)) % (2 * deep)
        return there // 2, there % 2, 1 - xh, y, c

    outer = pairs(shape, across)

    def over_y(copies):
        return lax.all_to_all(copies, "y", 0, 0, tiled=True)

    def swapped(array):
        return lax.ppermute(array, AXES, other_core)

    def on_device(points, order, scan_ids, ln_gain, w_qkv, w_out):
        w_turned = jnp.swapaxes(w_qkv, 1, 2)
        (copies,) = call(
            order_kernel, 1.2, [(4, EXT, LANES)],
            [((ROWS, D), BF16), ((1, ROWS), jnp.int32), ((1, ROWS), jnp.int32)],
            late=(points, order, scan_ids.reshape(1, ROWS)), semaphores=(3,), megabytes=56,
        )
        first_far = lax.ppermute(w_turned[0], AXES, mirror)
        second_far = lax.ppermute(w_turned[1], AXES, mirror)
        x_near = over_y(copies)
        x_near, first_far = lax.optimization_barrier((x_near, first_far))
        x_far = swapped(x_near)
        (shares,) = call(
            functools.partial(relay_kernel, 1), 1, [(4, HEAD_DIM, D)], [], w_out[0],
            late=(x_near,), megabytes=4,
        )
        w_own = over_y(shares)
        projection = [((3 * HEAD_DIM, D), BF16)] * 2
        (o_copies,) = call(
            first_kernel,
            8,
            [(4, PATCH, LANES)],
            [
                ((PATCH, D), BF16),
                ((PATCH, LANES), BF16),
                ((PATCH, 2 * LANES), BF16),
                ((LANES, PATCH), BF16),
                ((2, HEAD_DIM + 16, PATCH), BF16),
                ((PATCH, LANES), BF16),
                *projection,
            ],
            x_near, x_far, ln_gain[0:1],
            late=(w_turned[0], first_far), semaphores=(2,), megabytes=56,
        )
        o_copies, w_own, second_far = lax.optimization_barrier((o_copies, w_own, second_far))
        w_mir = lax.ppermute(w_own, AXES, mirror)
        w_own_far = swapped(w_own)
        last_far = lax.ppermute(w_out[1], AXES, mirror)
        o_near = over_y(o_copies)
        o_near, w_mir, w_own_far, last_far = lax.optimization_barrier(
            (o_near, w_mir, w_own_far, last_far)
        )
        o_far = swapped(o_near)
        w_mir_far = swapped(w_mir)
        (shares,) = call(
            functools.partial(relay_kernel, 2), 1, [(8, ROWS, D)], [], w_out[1], last_far,
            late=(o_near,), megabytes=4,
        )
        w_last = lax.all_to_all(shares, ("y", "c"), 0, 0, tiled=True).reshape(D, D)
        middle, halos = [], []
        for part, links in enumerate((inner, outer)):
            middle.append(
                call(
                    functools.partial(middle_kernel, part),
                    4,
                    [(HALF, LANES), (EXT, LANES), (ROWS, D)],
                    [
                        ((HALF, D), BF16),
                        ((HALF, D), F32),
                        ((HALF, D), BF16),
                        ((LANES, HALF), BF16),
                        ((D, D), BF16),
                        *projection,
                    ],
                    x_near, x_far, ln_gain[1:2],
                    late=(o_near, o_far, w_own, w_own_far, w_mir, w_mir_far, w_turned[1], second_far, shares),
                    semaphores=(16, 18), megabytes=56,
                )
            )
            halos.append(lax.ppermute(middle[part][1], AXES, links))
        parts = None
        for part in range(2):
            queries, kv, _ = middle[part]
            (parts,) = call(
                functools.partial(second_kernel, part),
                3 if part else 0,
                [(8 if part else 4, ROWS, LANES)],
                [
                    ((PATCH, 2 * LANES), BF16),
                    ((2, HEAD_DIM + 16, PATCH), BF16),
                    ((HALF, LANES), BF16),
                ],
                queries, kv, halos[part], *([parts] if part else []),
                late=() if part else (middle[1][1],), megabytes=8,
            )
        parts, w_last = lax.optimization_barrier((parts, w_last))
        parts = lax.all_to_all(parts, ("y", "c"), 0, 0, tiled=True)
        (result,) = call(
            last_kernel, 1.5, [(ROWS, D)], [((ROWS, D), BF16)],
            parts, w_last, middle[0][2], middle[1][2], megabytes=8,
        )
        return result

    every = ("z", "xl") + head_axes
    return jax.shard_map(
        on_device,
        mesh=Mesh(mesh.devices.reshape(shape), AXES),
        in_specs=(P(every, None), P(every, None), P(every), P(), P(None, None, head_axes), P(None, head_axes, None)),
        out_specs=P(every, None),
        check_vma=False,
    )
```

```python
import functools

import jax
import jax.numpy as jnp
import numpy as np
from jax import lax
from jax.experimental import pallas as pl
from jax.experimental.pallas import tpu as pltpu
from jax.sharding import Mesh
from jax.sharding import PartitionSpec as P

HEAD_DIM = 64
D = 1024
ROWS = 128
PATCH = 1024
HALF = 512
LANES = 128
BLOCKS = D // LANES
EXT = D + 16
FULL = EXT + BLOCKS * HEAD_DIM
EPSILON = 1e-05
FAR = -1e30
AXES = ("z", "xl", "xh", "y", "c")
F32 = jnp.float32
BF16 = jnp.bfloat16


def pairs(shape, move):
    result = []
    for i in range(int(np.prod(shape))):
        place = tuple(int(v) for v in np.unravel_index(i, shape))
        result.append((i, int(np.ravel_multi_index(move(*place), shape))))
    return result


def dot(a, b):
    return lax.dot_general(a, b, (((1,), (0,)), ((), ())), preferred_element_type=F32)


def dot_nt(a, b):
    return lax.dot_general(a, b, (((1,), (1,)), ((), ())), preferred_element_type=F32)


def layer_norm(values, gain):
    center = values - jnp.mean(values, axis=-1, keepdims=True)
    spread = jnp.mean(center * center, axis=-1, keepdims=True)
    return (center * lax.rsqrt(spread + EPSILON) * gain).astype(BF16)


def side_by_side(ref, index):
    return jnp.concatenate([ref[index, b * LANES : (b + 1) * LANES, :] for b in range(BLOCKS)], axis=1)


def tag_columns(rows):
    return jnp.transpose(jnp.concatenate(rows, axis=0))


def one_hot(columns, block):
    lane = lax.broadcasted_iota(jnp.int32, (ROWS, LANES), 1).astype(F32)
    return columns[:, block : block + 1] == lane


def attend(queries, hot, keys_ref, values_ref):
    lane = lax.broadcasted_iota(jnp.int32, queries.shape, 1)
    results = []
    for head in range(2):
        own = jnp.where(lane // HEAD_DIM == head, queries, jnp.zeros_like(queries))
        scores = dot_nt(keys_ref[...], jnp.concatenate([own, hot], axis=1))
        top = jnp.max(scores, axis=0, keepdims=True)
        probs = jnp.exp(scores - top).astype(BF16)
        sums = dot(values_ref[head], probs)
        results.append(sums[:HEAD_DIM] / sums[HEAD_DIM : HEAD_DIM + 1])
    return jnp.transpose(jnp.concatenate(results, axis=0)).astype(BF16)


def fetch(sources, targets, sems):
    copies = [pltpu.make_async_copy(a, b, sems.at[i]) for i, (a, b) in enumerate(zip(sources, targets))]
    for copy in copies:
        copy.start()
    return copies


def order_kernel(points_at, order_at, tags_at, w_at, out, points, order, tags, w, sems):
    copies = fetch((order_at, points_at, tags_at, w_at.at[0]), (order, points, tags, w), sems)
    for copy in copies:
        copy.wait()
    row = lax.broadcasted_iota(jnp.int32, (ROWS, ROWS), 0)
    picks = jnp.transpose((row == order[...]).astype(F32)).astype(BF16)
    ordered = dot(picks, points[...]).astype(BF16)
    tag_rows = jnp.broadcast_to(tags[...].astype(F32), (16, LANES)).astype(BF16)
    for copy in range(4):
        for b in range(BLOCKS):
            out[copy, b * LANES : (b + 1) * LANES, :] = ordered[:, b * LANES : (b + 1) * LANES]
            out[copy, EXT + b * HEAD_DIM : EXT + (b + 1) * HEAD_DIM, :] = w[:, b * LANES : (b + 1) * LANES]
        out[copy, D:EXT, :] = tag_rows


def joined(own, mirrored, kind):
    cut = slice(kind * HEAD_DIM, (kind + 1) * HEAD_DIM)
    return jnp.concatenate([own[cut, :], mirrored[cut, :]], axis=0)


def project(normed, own, mirrored, queries, keys, turned):
    both = jnp.concatenate([joined(own, mirrored, 0), joined(own, mirrored, 1)], axis=0)
    found = dot_nt(normed[...], both).astype(BF16)
    queries[...] = found[:, :LANES] * jnp.asarray(HEAD_DIM**-0.5, BF16)
    keys[...] = found[:, LANES:]
    turned[...] = dot_nt(joined(own, mirrored, 2), normed[...]).astype(BF16)


def put_values(values_ref, span, turned, swap):
    for head in range(2):
        from_head = 1 - head if swap else head
        values_ref[head, :HEAD_DIM, span] = turned[from_head * HEAD_DIM : (from_head + 1) * HEAD_DIM]


def first_kernel(
    gain, near, far, own_at, mirrored_at, out,
    points, normed, queries, keys, turned, values, hots, own, mirrored, sems, w_sems,
):
    sources = [ref.at[y, :EXT, :] for ref in (near, far) for y in range(4)]
    blocks = fetch(sources, [points.at[b] for b in range(8)], sems)
    copies = fetch((own_at.at[0], mirrored_at.at[0]), (own, mirrored), w_sems)
    rows = []
    for block in range(8):
        blocks[block].wait()
        normed[block * ROWS : (block + 1) * ROWS, :] = layer_norm(
            side_by_side(points, block).astype(F32), gain[...]
        )
        rows.append(points[block, D:, :].astype(F32)[:1])
    columns = tag_columns(rows)
    for copy in copies:
        copy.wait()
    project(normed, own, mirrored, queries, keys.at[:, :LANES], turned)
    put_values(values, slice(0, PATCH), turned, False)
    values[:, HEAD_DIM:, :] = jnp.ones((2, 16, PATCH), BF16)
    for block in range(8):
        hot = one_hot(columns, block)
        span = slice(block * ROWS, (block + 1) * ROWS)
        hots[span, :] = jnp.where(hot, 1.0, 0.0).astype(BF16)
        keys[span, LANES:] = jnp.where(hot, 0.0, FAR).astype(BF16)
    for part in range(4):
        span = slice(part * 256, (part + 1) * 256)
        result = attend(queries[span, :], hots[span, :], keys, values)
        for copy in range(4):
            out[copy, span, :] = result


def half_of(part):
    xh = lax.axis_index("xh")
    return xh if part else 1 - xh


def middle_kernel(
    part, gain, o_near, o_far, w_own, w_own_far, w_mir, w_mir_far, near, far, own_at, mirrored_at, ready,
    q_out, kv, st_out,
    heads, update, normed, turned, w, points, own, mirrored, o_sems, w_sems, sems,
):
    my_y, half = lax.axis_index("y"), half_of(part)
    sources, targets = [], []
    for s in range(2):
        span = slice(s * 256, (s + 1) * 256)
        at_near = pl.ds(pl.multiple_of(s * HALF + half * 256, 256), 256)
        at_far = pl.ds(pl.multiple_of((1 - s) * HALF + half * 256, 256), 256)
        for g in range(4):
            sources += [o_near.at[g, at_near, :], o_far.at[g, at_far, :]]
            targets += [
                heads.at[span, g * LANES : (g + 1) * LANES],
                heads.at[span, (g + 4) * LANES : (g + 5) * LANES],
            ]
    copies = fetch(sources, targets, o_sems)
    sources, targets = [], []
    for i, ref in enumerate((w_own, w_mir, w_own_far, w_mir_far)):
        for g in range(4):
            row = (i // 2 * 4 + g) * LANES + i % 2 * HEAD_DIM
            sources.append(ref.at[g])
            targets.append(w.at[:, row : row + HEAD_DIM, :])
    copies += fetch(sources, targets, w_sems)
    late = fetch(
        (
            near.at[pl.ds(half * 2, 2), :EXT, :], far.at[pl.ds(half * 2, 2), :EXT, :],
            own_at.at[1], mirrored_at.at[1],
        ),
        (points.at[:2], points.at[2:], own, mirrored),
        sems,
    )
    for copy in copies:
        copy.wait()
    for j in range(4):
        both = jnp.concatenate([w[2 * j], w[2 * j + 1]], axis=1)
        update[:, j * 256 : (j + 1) * 256] = dot(heads[...], both)
    for copy in late:
        copy.wait()
    rows = []
    for block in range(4):
        span = slice(block * ROWS, (block + 1) * ROWS)
        stream = (side_by_side(points, block).astype(F32) + update[span, :]).astype(BF16)
        normed[span, :] = layer_norm(stream.astype(F32), gain[...])
        rows.append(points[block, D:, :].astype(F32)[:1])
        if block < 2:

            @pl.when(half * 2 + block == my_y)
            def _(stream=stream):
                st_out[...] = stream

    project(normed, own, mirrored, q_out, kv.at[:HALF, :], turned)
    for b in range(4):
        kv[HALF + b * LANES : HALF + (b + 1) * LANES, :] = turned[:, b * LANES : (b + 1) * LANES]
    kv[D:, :] = jnp.concatenate(rows + [jnp.zeros((12, LANES), F32)], axis=0).astype(BF16)


def second_kernel(part, *refs):
    if part:
        queries, mine, other, had, out, keys, values, hots = refs
    else:
        queries, mine, other, ready, out, keys, values, hots = refs
    half, c = half_of(part), lax.axis_index("c")
    keys[:HALF, :LANES] = mine[:HALF, :]
    keys[HALF:, :HEAD_DIM] = other[:HALF, HEAD_DIM:]
    keys[HALF:, HEAD_DIM:LANES] = other[:HALF, :HEAD_DIM]
    for b in range(4):
        cut = slice(HALF + b * LANES, HALF + (b + 1) * LANES)
        put_values(values, slice(b * LANES, (b + 1) * LANES), mine[cut, :], False)
        put_values(values, slice(HALF + b * LANES, HALF + (b + 1) * LANES), other[cut, :], True)
    values[:, HEAD_DIM:, :] = jnp.ones((2, 16, PATCH), BF16)
    columns = tag_columns([mine[D:, :].astype(F32)[:4], other[D:, :].astype(F32)[:4]])
    for block in range(8):
        hot = one_hot(columns, block)
        span = slice(block * ROWS, (block + 1) * ROWS)
        if block < 4:
            hots[span, :] = jnp.where(hot, 1.0, 0.0).astype(BF16)
        keys[span, LANES:] = jnp.where(hot, 0.0, FAR).astype(BF16)
    for s in range(2):
        span = slice(s * 256, (s + 1) * 256)
        result = attend(queries[span, :], hots[span, :], keys, values)
        core = c if s == 0 else 1 - c
        for yy in range(2):
            block = result[yy * ROWS : (yy + 1) * ROWS]
            if part:
                out[(half * 2 + yy) * 2 + core] = block
                out[((1 - half) * 2 + yy) * 2 + core] = had[s * 2 + yy]
            else:
                out[s * 2 + yy] = block


def last_kernel(parts, w, stream_p, stream_q, out, heads):
    y_half = lax.axis_index("y") // 2
    for g in range(8):
        heads[:, g * LANES : (g + 1) * LANES] = parts[g]
    update = dot(heads[...], w[...])

    def put(stream):
        out[...] = (stream[...].astype(F32) + update).astype(BF16)

    pl.when(y_half == half_of(0))(lambda: put(stream_p))
    pl.when(y_half == half_of(1))(lambda: put(stream_q))


def relay_kernel(own, mirrored, ready, out):
    for copy in range(out.shape[0]):
        out[copy, :HEAD_DIM] = own[...]
        out[copy, HEAD_DIM:] = mirrored[...]


def call(kernel, micros, outs, scratch, *args, late=(), semaphores=(), megabytes=16):
    vmem, anywhere = pl.BlockSpec(memory_space=pltpu.VMEM), pl.BlockSpec(memory_space=pl.ANY)
    return pl.pallas_call(
        kernel,
        out_shape=[jax.ShapeDtypeStruct(shape, BF16) for shape in outs],
        in_specs=[vmem] * len(args) + [anywhere] * len(late),
        out_specs=[vmem] * len(outs),
        scratch_shapes=[pltpu.VMEM(shape, dtype) for shape, dtype in scratch]
        + [pltpu.SemaphoreType.DMA((count,)) for count in semaphores],
        compiler_params=pltpu.CompilerParams(vmem_limit_bytes=megabytes * 1024 * 1024),
        cost_estimate=pl.CostEstimate(
            flops=int(micros * 1.1e9), bytes_accessed=0, transcendentals=0
        ),
    )(*args, *late)


def solution(mesh):
    curve, heads = mesh.shape["curve"], mesh.shape["head"]
    shape = (curve // 2, 2, 2, heads // 4, 2)
    deep = shape[0]
    head_axes = ("xh", "y", "c")
    other_core = pairs(shape, lambda z, xl, xh, y, c: (z, xl, xh, y, 1 - c))
    mirror = pairs(shape, lambda z, xl, xh, y, c: (z, 1 - xl, 1 - xh, y, c))
    beside = pairs(shape, lambda z, xl, xh, y, c: (z, 1 - xl, xh, y, c))
    inner = pairs(shape, lambda z, xl, xh, y, c: (z, xl, 1 - xh, y, c))

    def across(z, xl, xh, y, c):
        here = z * 2 + xl
        there = (here + (1 if xh else -1)) % (2 * deep)
        return there // 2, there % 2, 1 - xh, y, c

    outer = pairs(shape, across)

    def over_y(copies):
        return lax.all_to_all(copies, "y", 0, 0, tiled=True)

    def swapped(array):
        return lax.ppermute(array, AXES, other_core)

    def on_device(points, order, scan_ids, ln_gain, w_qkv, w_out):
        w_turned = jnp.swapaxes(w_qkv, 1, 2)
        (copies,) = call(
            order_kernel, 1.2, [(4, FULL, LANES)],
            [
                ((ROWS, D), BF16), ((1, ROWS), jnp.int32), ((1, ROWS), jnp.int32),
                ((HEAD_DIM, D), BF16),
            ],
            late=(points, order, scan_ids.reshape(1, ROWS), w_out), semaphores=(4,), megabytes=56,
        )
        w_far = lax.ppermute(w_turned, AXES, mirror)
        near = over_y(copies)
        near, w_far = lax.optimization_barrier((near, w_far))
        far = swapped(near)

        def out_weights(array):
            return array[:, EXT:].reshape(4, BLOCKS, HEAD_DIM, LANES)

        w_own = out_weights(near)
        w_mir = lax.ppermute(w_own, AXES, mirror)
        projection = [((3 * HEAD_DIM, D), BF16)] * 2
        (o_copies,) = call(
            first_kernel,
            8,
            [(4, PATCH, LANES)],
            [
                ((8, EXT, LANES), BF16),
                ((PATCH, D), BF16),
                ((PATCH, LANES), BF16),
                ((PATCH, 2 * LANES), BF16),
                ((LANES, PATCH), BF16),
                ((2, HEAD_DIM + 16, PATCH), BF16),
                ((PATCH, LANES), BF16),
                *projection,
            ],
            ln_gain[0:1],
            late=(near, far, w_turned, w_far), semaphores=(8, 2), megabytes=56,
        )
        o_copies, w_mir = lax.optimization_barrier((o_copies, w_mir))
        last_far = lax.ppermute(w_out[1], AXES, mirror)
        w_mir_far = swapped(w_mir)
        w_own_far = out_weights(far)
        o_near = over_y(o_copies)
        o_near, w_mir_far, w_own_far, last_far = lax.optimization_barrier(
            (o_near, w_mir_far, w_own_far, last_far)
        )
        o_far = swapped(o_near)
        (shares,) = call(
            relay_kernel, 1, [(8, ROWS, D)], [], w_out[1], last_far, late=(o_near,), megabytes=4
        )
        w_last = lax.all_to_all(shares, ("y", "c"), 0, 0, tiled=True).reshape(D, D)
        middle, halos = [], []
        for part, links in enumerate((inner, outer)):
            middle.append(
                call(
                    functools.partial(middle_kernel, part),
                    4,
                    [(HALF, LANES), (EXT, LANES), (ROWS, D)],
                    [
                        ((HALF, D), BF16),
                        ((HALF, D), F32),
                        ((HALF, D), BF16),
                        ((LANES, HALF), BF16),
                        ((BLOCKS, D, LANES), BF16),
                        ((4, EXT, LANES), BF16),
                        *projection,
                    ],
                    ln_gain[1:2],
                    late=(
                        o_near, o_far, w_own, w_own_far, w_mir, w_mir_far, near, far,
                        w_turned, w_far, shares,
                    ),
                    semaphores=(16, 16, 4), megabytes=56,
                )
            )
            halos.append(lax.ppermute(middle[part][1], AXES, links))
        parts = None
        for part in range(2):
            queries, kv, _ = middle[part]
            (parts,) = call(
                functools.partial(second_kernel, part),
                3 if part else 0,
                [(8 if part else 4, ROWS, LANES)],
                [
                    ((PATCH, 2 * LANES), BF16),
                    ((2, HEAD_DIM + 16, PATCH), BF16),
                    ((HALF, LANES), BF16),
                ],
                queries, kv, halos[part], *([parts] if part else []),
                late=() if part else (middle[1][1],), megabytes=8,
            )
        parts, w_last = lax.optimization_barrier((parts, w_last))
        parts = lax.all_to_all(parts, ("y", "c"), 0, 0, tiled=True)
        (result,) = call(
            last_kernel, 1.5, [(ROWS, D)], [((ROWS, D), BF16)],
            parts, w_last, middle[0][2], middle[1][2], megabytes=8,
        )
        return result

    every = ("z", "xl") + head_axes
    return jax.shard_map(
        on_device,
        mesh=Mesh(mesh.devices.reshape(shape), AXES),
        in_specs=(P(every, None), P(every, None), P(every), P(), P(None, None, head_axes), P(None, head_axes, None)),
        out_specs=P(every, None),
        check_vma=False,
    )
```

```python
import functools

import jax
import jax.numpy as jnp
import numpy as np
from jax import lax
from jax.experimental import pallas as pl
from jax.experimental.pallas import tpu as pltpu
from jax.sharding import Mesh
from jax.sharding import PartitionSpec as P

HEAD_DIM = 64
D = 1024
ROWS = 128
PATCH = 1024
HALF = 512
LANES = 128
BLOCKS = D // LANES
EXT = D + 16
FULL = EXT + BLOCKS * HEAD_DIM
EPSILON = 1e-05
FAR = -1e30
AXES = ("z", "xl", "xh", "y", "c")
F32 = jnp.float32
BF16 = jnp.bfloat16


def pairs(shape, move):
    result = []
    for i in range(int(np.prod(shape))):
        place = tuple(int(v) for v in np.unravel_index(i, shape))
        result.append((i, int(np.ravel_multi_index(move(*place), shape))))
    return result


def dot(a, b):
    return lax.dot_general(a, b, (((1,), (0,)), ((), ())), preferred_element_type=F32)


def dot_nt(a, b):
    return lax.dot_general(a, b, (((1,), (1,)), ((), ())), preferred_element_type=F32)


def layer_norm(values, gain):
    center = values - jnp.mean(values, axis=-1, keepdims=True)
    spread = jnp.mean(center * center, axis=-1, keepdims=True)
    return (center * lax.rsqrt(spread + EPSILON) * gain).astype(BF16)


def side_by_side(ref, index):
    return jnp.concatenate([ref[index, b * LANES : (b + 1) * LANES, :] for b in range(BLOCKS)], axis=1)


def tag_columns(rows):
    return jnp.transpose(jnp.concatenate(rows, axis=0))


def one_hot(columns, block):
    lane = lax.broadcasted_iota(jnp.int32, (ROWS, LANES), 1).astype(F32)
    return columns[:, block : block + 1] == lane


def attend(queries, hot, keys_ref, values_ref):
    lane = lax.broadcasted_iota(jnp.int32, queries.shape, 1)
    results = []
    for head in range(2):
        own = jnp.where(lane // HEAD_DIM == head, queries, jnp.zeros_like(queries))
        scores = dot_nt(keys_ref[...], jnp.concatenate([own, hot], axis=1))
        top = jnp.max(scores, axis=0, keepdims=True)
        probs = jnp.exp(scores - top).astype(BF16)
        sums = dot(values_ref[head], probs)
        results.append(sums[:HEAD_DIM] / sums[HEAD_DIM : HEAD_DIM + 1])
    return jnp.transpose(jnp.concatenate(results, axis=0)).astype(BF16)


def fetch(sources, targets, sems):
    copies = [pltpu.make_async_copy(a, b, sems.at[i]) for i, (a, b) in enumerate(zip(sources, targets))]
    for copy in copies:
        copy.start()
    return copies


def order_kernel(points_at, order_at, tags_at, w_at, out, points, order, tags, w, sems):
    copies = fetch((order_at, points_at, tags_at, w_at.at[0]), (order, points, tags, w), sems)
    for copy in copies:
        copy.wait()
    row = lax.broadcasted_iota(jnp.int32, (ROWS, ROWS), 0)
    picks = jnp.transpose((row == order[...]).astype(F32)).astype(BF16)
    ordered = dot(picks, points[...]).astype(BF16)
    tag_rows = jnp.broadcast_to(tags[...].astype(F32), (16, LANES)).astype(BF16)
    for copy in range(4):
        for b in range(BLOCKS):
            out[copy, b * LANES : (b + 1) * LANES, :] = ordered[:, b * LANES : (b + 1) * LANES]
            out[copy, EXT + b * HEAD_DIM : EXT + (b + 1) * HEAD_DIM, :] = w[:, b * LANES : (b + 1) * LANES]
        out[copy, D:EXT, :] = tag_rows


def joined(own, mirrored, kind):
    cut = slice(kind * HEAD_DIM, (kind + 1) * HEAD_DIM)
    return jnp.concatenate([own[cut, :], mirrored[cut, :]], axis=0)


def project(normed, own, mirrored, queries, keys, turned):
    both = jnp.concatenate([joined(own, mirrored, 0), joined(own, mirrored, 1)], axis=0)
    found = dot_nt(normed[...], both).astype(BF16)
    queries[...] = found[:, :LANES] * jnp.asarray(HEAD_DIM**-0.5, BF16)
    keys[...] = found[:, LANES:]
    turned[...] = dot_nt(joined(own, mirrored, 2), normed[...]).astype(BF16)


def put_values(values_ref, span, turned, swap):
    for head in range(2):
        from_head = 1 - head if swap else head
        values_ref[head, :HEAD_DIM, span] = turned[from_head * HEAD_DIM : (from_head + 1) * HEAD_DIM]


def first_kernel(
    gain, near, far, own_at, mirrored_at, out,
    points, normed, queries, keys, turned, values, hots, own, mirrored, sems, w_sems,
):
    sources = [ref.at[y, :EXT, :] for ref in (near, far) for y in range(4)]
    blocks = fetch(sources, [points.at[b] for b in range(8)], sems)
    copies = fetch((own_at.at[0], mirrored_at), (own, mirrored), w_sems)
    rows = []
    for block in range(8):
        blocks[block].wait()
        normed[block * ROWS : (block + 1) * ROWS, :] = layer_norm(
            side_by_side(points, block).astype(F32), gain[0:1, :]
        )
        rows.append(points[block, D:, :].astype(F32)[:1])
    columns = tag_columns(rows)
    for copy in copies:
        copy.wait()
    project(normed, own, mirrored, queries, keys.at[:, :LANES], turned)
    put_values(values, slice(0, PATCH), turned, False)
    values[:, HEAD_DIM:, :] = jnp.ones((2, 16, PATCH), BF16)
    for block in range(8):
        hot = one_hot(columns, block)
        span = slice(block * ROWS, (block + 1) * ROWS)
        hots[span, :] = jnp.where(hot, 1.0, 0.0).astype(BF16)
        keys[span, LANES:] = jnp.where(hot, 0.0, FAR).astype(BF16)
    for part in range(4):
        span = slice(part * 256, (part + 1) * 256)
        result = attend(queries[span, :], hots[span, :], keys, values)
        for copy in range(4):
            out[copy, span, :] = result


def half_of(part):
    xh = lax.axis_index("xh")
    return xh if part else 1 - xh


def middle_kernel(
    gain, o_near, o_far, near, far, w_mir, w_mir_far, own_at, mirrored_at, ready,
    q_out, kv_p, kv_q, st_out,
    heads, update, normed, queries, keys, turned, w, points, own, mirrored,
    o_sems, w_sems, sems,
):
    my_y = lax.axis_index("y")
    sources, targets = [], []
    for i, ref in enumerate((near, w_mir, far, w_mir_far)):
        for g in range(4):
            row = (i // 2 * 4 + g) * LANES + i % 2 * HEAD_DIM
            if i % 2:
                sources.append(ref.at[g])
            else:
                sources.append(ref.at[g, EXT:FULL, :].reshape(BLOCKS, HEAD_DIM, LANES))
            targets.append(w.at[:, row : row + HEAD_DIM, :])
    w_copies = fetch(sources, targets, w_sems)

    def heads_of(s):
        span, other = slice(s * HALF, (s + 1) * HALF), slice((1 - s) * HALF, (2 - s) * HALF)
        sources = [o_near.at[:, span, :], o_far.at[:, other, :]]
        targets = [heads.at[:4, span, :], heads.at[4:, span, :]]
        return fetch(sources, targets, o_sems.at[s])

    o_copies = [heads_of(0)]
    late = fetch((near.at[:, :EXT, :],), (points.at[0],), sems.at[0:1])
    o_copies.append(heads_of(1))
    late += fetch(
        (far.at[:, :EXT, :], own_at.at[1], mirrored_at.at[: 3 * HEAD_DIM]),
        (points.at[1], own, mirrored),
        sems.at[1:4],
    )
    for copy in w_copies:
        copy.wait()
    rows = []
    for s in range(2):
        for copy in o_copies[s]:
            copy.wait()
        span = slice(s * HALF, (s + 1) * HALF)
        left = jnp.concatenate([heads[g, span, :] for g in range(BLOCKS)], axis=1)
        for j in range(4):
            both = jnp.concatenate([w[2 * j], w[2 * j + 1]], axis=1)
            update[:, j * 256 : (j + 1) * 256] = dot(left, both)
        late[s].wait()
        for y in range(4):
            there = slice(y * ROWS, (y + 1) * ROWS)
            x = jnp.concatenate(
                [points[s, y, b * LANES : (b + 1) * LANES, :] for b in range(BLOCKS)], axis=1
            )
            stream = (x.astype(F32) + update[there, :]).astype(BF16)
            normed[s * HALF + y * ROWS : s * HALF + (y + 1) * ROWS, :] = layer_norm(
                stream.astype(F32), gain[1:2, :]
            )
            rows.append(points[s, y, D:, :].astype(F32)[:1])
            if s == 0:

                @pl.when(y == my_y)
                def _(stream=stream):
                    st_out[...] = stream

    for copy in late[2:]:
        copy.wait()
    project(normed, own, mirrored, queries, keys, turned)
    for part, kv in enumerate((kv_p, kv_q)):
        half = half_of(part)
        for s in range(2):
            at = pl.multiple_of(s * HALF + half * 256, 256)
            q_out[part, s * 256 : (s + 1) * 256, :] = queries[pl.ds(at, 256), :]
            kv[s * 256 : (s + 1) * 256, :] = keys[pl.ds(at, 256), :]
            for b in range(2):
                cut = slice(HALF + (s * 2 + b) * LANES, HALF + (s * 2 + b + 1) * LANES)
                kv[cut, :] = turned[:, pl.ds(pl.multiple_of(at + b * LANES, LANES), LANES)]
        tags = [jnp.where(half == 0, rows[s * 4 + b], rows[s * 4 + 2 + b]) for s in range(2) for b in range(2)]
        kv[D:, :] = jnp.concatenate(tags + [jnp.zeros((12, LANES), F32)], axis=0).astype(BF16)


def second_kernel(part, *refs):
    if part:
        queries, mine, other, had, out, keys, values, hots = refs
    else:
        queries, mine, other, out, keys, values, hots = refs
    half, c = half_of(part), lax.axis_index("c")
    keys[:HALF, :LANES] = mine[:HALF, :]
    keys[HALF:, :HEAD_DIM] = other[:HALF, HEAD_DIM:]
    keys[HALF:, HEAD_DIM:LANES] = other[:HALF, :HEAD_DIM]
    for b in range(4):
        cut = slice(HALF + b * LANES, HALF + (b + 1) * LANES)
        put_values(values, slice(b * LANES, (b + 1) * LANES), mine[cut, :], False)
        put_values(values, slice(HALF + b * LANES, HALF + (b + 1) * LANES), other[cut, :], True)
    values[:, HEAD_DIM:, :] = jnp.ones((2, 16, PATCH), BF16)
    columns = tag_columns([mine[D:, :].astype(F32)[:4], other[D:, :].astype(F32)[:4]])
    for block in range(8):
        hot = one_hot(columns, block)
        span = slice(block * ROWS, (block + 1) * ROWS)
        if block < 4:
            hots[span, :] = jnp.where(hot, 1.0, 0.0).astype(BF16)
        keys[span, LANES:] = jnp.where(hot, 0.0, FAR).astype(BF16)
    for s in range(2):
        span = slice(s * 256, (s + 1) * 256)
        result = attend(queries[part, span, :], hots[span, :], keys, values)
        core = c if s == 0 else 1 - c
        for yy in range(2):
            block = result[yy * ROWS : (yy + 1) * ROWS]
            if part:
                out[(half * 2 + yy) * 2 + core] = block
                out[((1 - half) * 2 + yy) * 2 + core] = had[s * 2 + yy]
            else:
                out[s * 2 + yy] = block


def last_kernel(parts, w, stream, out, heads):
    for g in range(8):
        heads[:, g * LANES : (g + 1) * LANES] = parts[g]
    update = dot(heads[...], w[...])

    out[...] = (stream[...].astype(F32) + update).astype(BF16)


def relay_kernel(own, rest, out):
    for copy in range(out.shape[0]):
        out[copy, :HEAD_DIM] = own[...]
        out[copy, HEAD_DIM:] = rest[3 * HEAD_DIM :]


def call(kernel, micros, outs, scratch, *args, late=(), semaphores=(), megabytes=16):
    vmem, anywhere = pl.BlockSpec(memory_space=pltpu.VMEM), pl.BlockSpec(memory_space=pl.ANY)
    return pl.pallas_call(
        kernel,
        out_shape=[jax.ShapeDtypeStruct(shape, BF16) for shape in outs],
        in_specs=[vmem] * len(args) + [anywhere] * len(late),
        out_specs=[vmem] * len(outs),
        scratch_shapes=[pltpu.VMEM(shape, dtype) for shape, dtype in scratch]
        + [
            pltpu.SemaphoreType.DMA(count if isinstance(count, tuple) else (count,))
            for count in semaphores
        ],
        compiler_params=pltpu.CompilerParams(vmem_limit_bytes=megabytes * 1024 * 1024),
        cost_estimate=pl.CostEstimate(
            flops=int(micros * 1.1e9), bytes_accessed=0, transcendentals=0
        ),
    )(*args, *late)


def solution(mesh):
    curve, heads = mesh.shape["curve"], mesh.shape["head"]
    shape = (curve // 2, 2, 2, heads // 4, 2)
    deep = shape[0]
    head_axes = ("xh", "y", "c")
    other_core = pairs(shape, lambda z, xl, xh, y, c: (z, xl, xh, y, 1 - c))
    mirror = pairs(shape, lambda z, xl, xh, y, c: (z, 1 - xl, 1 - xh, y, c))
    beside = pairs(shape, lambda z, xl, xh, y, c: (z, 1 - xl, xh, y, c))
    inner = pairs(shape, lambda z, xl, xh, y, c: (z, xl, 1 - xh, y, c))

    def across(z, xl, xh, y, c):
        here = z * 2 + xl
        there = (here + (1 if xh else -1)) % (2 * deep)
        return there // 2, there % 2, 1 - xh, y, c

    outer = pairs(shape, across)

    def over_y(copies):
        return lax.all_to_all(copies, "y", 0, 0, tiled=True)

    def swapped(array):
        return lax.ppermute(array, AXES, other_core)

    def on_device(points, order, scan_ids, ln_gain, w_qkv, w_out):
        w_turned = jnp.swapaxes(w_qkv, 1, 2)
        (copies,) = call(
            order_kernel, 1.2, [(4, FULL, LANES)],
            [
                ((ROWS, D), BF16), ((1, ROWS), jnp.int32), ((1, ROWS), jnp.int32),
                ((HEAD_DIM, D), BF16),
            ],
            late=(points, order, scan_ids.reshape(1, ROWS), w_out), semaphores=(4,), megabytes=56,
        )
        first_far = lax.ppermute(w_turned[0], AXES, mirror)
        near = over_y(copies)
        near, first_far = lax.optimization_barrier((near, first_far))
        far = swapped(near)

        def out_weights(array):
            return array[:, EXT:].reshape(4, BLOCKS, HEAD_DIM, LANES)

        w_own = out_weights(near)
        w_mir = lax.ppermute(w_own, AXES, mirror)
        projection = [((3 * HEAD_DIM, D), BF16)] * 2
        (o_copies,) = call(
            first_kernel,
            8,
            [(4, PATCH, LANES)],
            [
                ((8, EXT, LANES), BF16),
                ((PATCH, D), BF16),
                ((PATCH, LANES), BF16),
                ((PATCH, 2 * LANES), BF16),
                ((LANES, PATCH), BF16),
                ((2, HEAD_DIM + 16, PATCH), BF16),
                ((PATCH, LANES), BF16),
                *projection,
            ],
            ln_gain,
            late=(near, far, w_turned, first_far), semaphores=(8, 2), megabytes=56,
        )
        o_copies, w_mir = lax.optimization_barrier((o_copies, w_mir))
        rest = jnp.concatenate([w_turned[1], w_out[1]], axis=0)
        o_copies, rest = lax.optimization_barrier((o_copies, rest))
        rest_far = lax.ppermute(rest, AXES, mirror)
        w_mir_far = swapped(w_mir)
        o_near = over_y(o_copies)
        (shares,) = call(relay_kernel, 1, [(8, ROWS, D)], [], w_out[1], rest_far, megabytes=4)
        o_near, w_mir_far, rest_far, shares = lax.optimization_barrier(
            (o_near, w_mir_far, rest_far, shares)
        )
        o_far = swapped(o_near)
        w_last = lax.all_to_all(shares, ("y", "c"), 0, 0, tiled=True).reshape(D, D)
        queries, *kvs, stream = call(
            middle_kernel,
            8,
            [(2, HALF, LANES), (EXT, LANES), (EXT, LANES), (ROWS, D)],
            [
                ((BLOCKS, PATCH, LANES), BF16),
                ((HALF, D), F32),
                ((PATCH, D), BF16),
                ((PATCH, LANES), BF16),
                ((PATCH, LANES), BF16),
                ((LANES, PATCH), BF16),
                ((BLOCKS, D, LANES), BF16),
                ((2, 4, EXT, LANES), BF16),
                *projection,
            ],
            ln_gain,
            late=(o_near, o_far, near, far, w_mir, w_mir_far, w_turned, rest_far, shares),
            semaphores=((2, 2), 16, 4), megabytes=56,
        )
        halos = [lax.ppermute(kv, AXES, links) for kv, links in zip(kvs, (inner, outer))]
        parts = None
        for part in range(2):
            kv = kvs[part]
            (parts,) = call(
                functools.partial(second_kernel, part),
                3 if part else 0,
                [(8 if part else 4, ROWS, LANES)],
                [
                    ((PATCH, 2 * LANES), BF16),
                    ((2, HEAD_DIM + 16, PATCH), BF16),
                    ((HALF, LANES), BF16),
                ],
                queries, kv, halos[part], *([parts] if part else []),
                megabytes=8,
            )
        parts, w_last = lax.optimization_barrier((parts, w_last))
        parts = lax.all_to_all(parts, ("y", "c"), 0, 0, tiled=True)
        (result,) = call(
            last_kernel, 1.5, [(ROWS, D)], [((ROWS, D), BF16)],
            parts, w_last, stream, megabytes=8,
        )
        return result

    every = ("z", "xl") + head_axes
    return jax.shard_map(
        on_device,
        mesh=Mesh(mesh.devices.reshape(shape), AXES),
        in_specs=(P(every, None), P(every, None), P(every), P(), P(None, None, head_axes), P(None, head_axes, None)),
        out_specs=P(every, None),
        check_vma=False,
    )
```

```python
import functools

import jax
import jax.numpy as jnp
import numpy as np
from jax import lax
from jax.experimental import pallas as pl
from jax.experimental.pallas import tpu as pltpu
from jax.sharding import Mesh
from jax.sharding import PartitionSpec as P

HEAD_DIM = 64
D = 1024
ROWS = 128
PATCH = 1024
HALF = 512
LANES = 128
BLOCKS = D // LANES
EXT = D + 16
FULL = EXT + BLOCKS * HEAD_DIM
EPSILON = 1e-05
FAR = -1e30
AXES = ("z", "xl", "xh", "y", "c")
F32 = jnp.float32
BF16 = jnp.bfloat16


def pairs(shape, move):
    result = []
    for i in range(int(np.prod(shape))):
        place = tuple(int(v) for v in np.unravel_index(i, shape))
        result.append((i, int(np.ravel_multi_index(move(*place), shape))))
    return result


def dot(a, b):
    return lax.dot_general(a, b, (((1,), (0,)), ((), ())), preferred_element_type=F32)


def dot_nt(a, b):
    return lax.dot_general(a, b, (((1,), (1,)), ((), ())), preferred_element_type=F32)


def layer_norm(values, gain):
    center = values - jnp.mean(values, axis=-1, keepdims=True)
    spread = jnp.mean(center * center, axis=-1, keepdims=True)
    return (center * lax.rsqrt(spread + EPSILON) * gain).astype(BF16)


def side_by_side(ref, index):
    return jnp.concatenate([ref[index, b * LANES : (b + 1) * LANES, :] for b in range(BLOCKS)], axis=1)


def tag_columns(rows):
    return jnp.transpose(jnp.concatenate(rows, axis=0))


def one_hot(columns, block):
    lane = lax.broadcasted_iota(jnp.int32, (ROWS, LANES), 1).astype(F32)
    return columns[:, block : block + 1] == lane


def attend(queries, hot, keys_ref, values_ref):
    lane = lax.broadcasted_iota(jnp.int32, queries.shape, 1)
    pieces = [slice(k * 256, (k + 1) * 256) for k in range(4)]
    scores = []
    for head in range(2):
        own = jnp.where(lane // HEAD_DIM == head, queries, jnp.zeros_like(queries))
        both = jnp.concatenate([own, hot], axis=1)
        scores.append([dot_nt(keys_ref[piece, :], both) for piece in pieces])
    results = []
    for head in range(2):
        tops = [jnp.max(part, axis=0, keepdims=True) for part in scores[head]]
        top = functools.reduce(jnp.maximum, tops)
        sums = sum(
            dot(values_ref[head, :, piece], jnp.exp(part - top).astype(BF16))
            for part, piece in zip(scores[head], pieces)
        )
        results.append(sums[:HEAD_DIM] / sums[HEAD_DIM : HEAD_DIM + 1])
    return jnp.transpose(jnp.concatenate(results, axis=0)).astype(BF16)


def fetch(sources, targets, sems):
    copies = [pltpu.make_async_copy(a, b, sems.at[i]) for i, (a, b) in enumerate(zip(sources, targets))]
    for copy in copies:
        copy.start()
    return copies


def order_kernel(points_at, order_at, tags_at, w_at, out, points, order, tags, w, sems):
    copies = fetch((order_at, points_at, tags_at, w_at.at[0]), (order, points, tags, w), sems)
    for copy in copies:
        copy.wait()
    row = lax.broadcasted_iota(jnp.int32, (ROWS, ROWS), 0)
    picks = jnp.transpose((row == order[...]).astype(F32)).astype(BF16)
    ordered = dot(picks, points[...]).astype(BF16)
    tag_rows = jnp.broadcast_to(tags[...].astype(F32), (16, LANES)).astype(BF16)
    for copy in range(4):
        for b in range(BLOCKS):
            out[copy, b * LANES : (b + 1) * LANES, :] = ordered[:, b * LANES : (b + 1) * LANES]
            out[copy, EXT + b * HEAD_DIM : EXT + (b + 1) * HEAD_DIM, :] = w[:, b * LANES : (b + 1) * LANES]
        out[copy, D:EXT, :] = tag_rows


def joined(own, mirrored, kind):
    cut = slice(kind * HEAD_DIM, (kind + 1) * HEAD_DIM)
    return jnp.concatenate([own[cut, :], mirrored[cut, :]], axis=0)


def project(normed, own, mirrored, queries, keys, turned):
    every = jnp.concatenate([joined(own, mirrored, kind) for kind in range(3)], axis=0)
    found = dot_nt(normed, every)
    queries[...] = found[:, :LANES].astype(BF16) * jnp.asarray(HEAD_DIM**-0.5, BF16)
    keys[...] = found[:, LANES : 2 * LANES].astype(BF16)
    turned[...] = jnp.transpose(found[:, 2 * LANES :]).astype(BF16)


def put_values(values_ref, span, turned, swap):
    for head in range(2):
        from_head = 1 - head if swap else head
        values_ref[head, :HEAD_DIM, span] = turned[from_head * HEAD_DIM : (from_head + 1) * HEAD_DIM]


def first_kernel(
    gain, near, far, own, mirrored, out, normed, queries, keys, turned, values, hots
):
    rows = []
    for block in range(8):
        ref, y = (near, far)[block // 4], block % 4
        normed[block * ROWS : (block + 1) * ROWS, :] = layer_norm(
            side_by_side(ref, y).astype(F32), gain[0:1, :]
        )
        rows.append(ref[y, D:EXT, :].astype(F32)[:1])
    columns = tag_columns(rows)
    project(normed[...], own.at[0], mirrored, queries, keys.at[:, :LANES], turned)
    put_values(values, slice(0, PATCH), turned, False)
    values[:, HEAD_DIM:, :] = jnp.ones((2, 16, PATCH), BF16)
    for block in range(8):
        hot = one_hot(columns, block)
        span = slice(block * ROWS, (block + 1) * ROWS)
        hots[span, :] = jnp.where(hot, 1.0, 0.0).astype(BF16)
        keys[span, LANES:] = jnp.where(hot, 0.0, FAR).astype(BF16)
    for part in range(4):
        span = slice(part * 256, (part + 1) * 256)
        result = attend(queries[span, :], hots[span, :], keys, values)
        for copy in range(4):
            out[copy, span, :] = result


def half_of(part):
    xh = lax.axis_index("xh")
    return xh if part else 1 - xh


def middle_kernel(
    gain, o_near, o_far, near, far, w_mir, w_mir_far, own_at, mirrored_at, ready,
    q_out, kv_p, kv_q, st_out,
    heads, update, normed, queries, keys, turned, w, points, own, mirrored,
    o_sems, w_sems, sems,
):
    my_y = lax.axis_index("y")
    sources, targets = [], []
    for i, ref in enumerate((near, w_mir, far, w_mir_far)):
        for g in range(4):
            row = (i // 2 * 4 + g) * LANES + i % 2 * HEAD_DIM
            if i % 2:
                sources.append(ref.at[g])
            else:
                sources.append(ref.at[g, EXT:FULL, :].reshape(BLOCKS, HEAD_DIM, LANES))
            targets.append(w.at[:, row : row + HEAD_DIM, :])
    w_copies = fetch(sources, targets, w_sems)

    late = fetch((own_at.at[1], mirrored_at), (own, mirrored), sems.at[2:4])
    top, end = slice(0, HALF), slice(HALF, PATCH)
    o_copies = fetch(
        (o_near, o_far.at[:, end, :], o_far.at[:, top, :]),
        (heads.at[:4], heads.at[4:, top, :], heads.at[4:, end, :]),
        o_sems,
    )
    x_copies = fetch((near.at[:, :EXT, :], far.at[:, :EXT, :]), (points.at[0], points.at[1]), sems)
    for copy in w_copies + o_copies:
        copy.wait()
    left = jnp.concatenate([heads[g] for g in range(BLOCKS)], axis=1)
    for j in range(2):
        both = jnp.concatenate([w[4 * j + i] for i in range(4)], axis=1)
        update[:, j * 512 : (j + 1) * 512] = dot(left, both)
    rows = []
    for s in range(2):
        x_copies[s].wait()
        for y in range(4):
            there = slice(s * HALF + y * ROWS, s * HALF + (y + 1) * ROWS)
            x = jnp.concatenate(
                [points[s, y, b * LANES : (b + 1) * LANES, :] for b in range(BLOCKS)], axis=1
            )
            stream = (x.astype(F32) + update[there, :]).astype(BF16)
            normed[there, :] = layer_norm(stream.astype(F32), gain[1:2, :])
            rows.append(points[s, y, D:, :].astype(F32)[:1])
            if s == 0:

                @pl.when(y == my_y)
                def _(stream=stream):
                    st_out[...] = stream

    for copy in late:
        copy.wait()
    project(normed[...], own, mirrored, queries, keys, turned)
    for part, kv in enumerate((kv_p, kv_q)):
        half = half_of(part)
        for s in range(2):
            at = pl.multiple_of(s * HALF + half * 256, 256)
            q_out[part, s * 256 : (s + 1) * 256, :] = queries[pl.ds(at, 256), :]
            kv[s * 256 : (s + 1) * 256, :] = keys[pl.ds(at, 256), :]
            for b in range(2):
                cut = slice(HALF + (s * 2 + b) * LANES, HALF + (s * 2 + b + 1) * LANES)
                kv[cut, :] = turned[:, pl.ds(pl.multiple_of(at + b * LANES, LANES), LANES)]
        tags = [jnp.where(half == 0, rows[s * 4 + b], rows[s * 4 + 2 + b]) for s in range(2) for b in range(2)]
        kv[D:, :] = jnp.concatenate(tags + [jnp.zeros((12, LANES), F32)], axis=0).astype(BF16)


def second_kernel(part, *refs):
    if part:
        queries, mine, other, had, out, keys, values, hots = refs
    else:
        queries, mine, other, out, keys, values, hots = refs
    half, c = half_of(part), lax.axis_index("c")
    keys[:HALF, :LANES] = mine[:HALF, :]
    keys[HALF:, :HEAD_DIM] = other[:HALF, HEAD_DIM:]
    keys[HALF:, HEAD_DIM:LANES] = other[:HALF, :HEAD_DIM]
    for b in range(4):
        cut = slice(HALF + b * LANES, HALF + (b + 1) * LANES)
        put_values(values, slice(b * LANES, (b + 1) * LANES), mine[cut, :], False)
        put_values(values, slice(HALF + b * LANES, HALF + (b + 1) * LANES), other[cut, :], True)
    values[:, HEAD_DIM:, :] = jnp.ones((2, 16, PATCH), BF16)
    columns = tag_columns([mine[D:, :].astype(F32)[:4], other[D:, :].astype(F32)[:4]])
    for block in range(8):
        hot = one_hot(columns, block)
        span = slice(block * ROWS, (block + 1) * ROWS)
        if block < 4:
            hots[span, :] = jnp.where(hot, 1.0, 0.0).astype(BF16)
        keys[span, LANES:] = jnp.where(hot, 0.0, FAR).astype(BF16)
    for s in range(2):
        span = slice(s * 256, (s + 1) * 256)
        result = attend(queries[part, span, :], hots[span, :], keys, values)
        core = c if s == 0 else 1 - c
        for yy in range(2):
            block = result[yy * ROWS : (yy + 1) * ROWS]
            if part:
                out[(half * 2 + yy) * 2 + core] = block
                out[((1 - half) * 2 + yy) * 2 + core] = had[s * 2 + yy]
            else:
                out[s * 2 + yy] = block


def last_kernel(parts, w, stream, out, heads):
    for g in range(8):
        heads[:, g * LANES : (g + 1) * LANES] = parts[g]
    update = dot(heads[...], w[...])

    out[...] = (stream[...].astype(F32) + update).astype(BF16)


def relay_kernel(own, rest, ready, out):
    for copy in range(out.shape[0]):
        out[copy, :HEAD_DIM] = own[...]
        out[copy, HEAD_DIM:] = rest[3 * HEAD_DIM :]


def call(kernel, micros, outs, scratch, *args, late=(), semaphores=(), megabytes=16):
    vmem, anywhere = pl.BlockSpec(memory_space=pltpu.VMEM), pl.BlockSpec(memory_space=pl.ANY)
    return pl.pallas_call(
        kernel,
        out_shape=[jax.ShapeDtypeStruct(shape, BF16) for shape in outs],
        in_specs=[vmem] * len(args) + [anywhere] * len(late),
        out_specs=[vmem] * len(outs),
        scratch_shapes=[pltpu.VMEM(shape, dtype) for shape, dtype in scratch]
        + [
            pltpu.SemaphoreType.DMA(count if isinstance(count, tuple) else (count,))
            for count in semaphores
        ],
        compiler_params=pltpu.CompilerParams(vmem_limit_bytes=megabytes * 1024 * 1024),
        cost_estimate=pl.CostEstimate(
            flops=int(micros * 1.1e9), bytes_accessed=0, transcendentals=0
        ),
    )(*args, *late)


def solution(mesh):
    curve, heads = mesh.shape["curve"], mesh.shape["head"]
    shape = (curve // 2, 2, 2, heads // 4, 2)
    deep = shape[0]
    head_axes = ("xh", "y", "c")
    other_core = pairs(shape, lambda z, xl, xh, y, c: (z, xl, xh, y, 1 - c))
    mirror = pairs(shape, lambda z, xl, xh, y, c: (z, 1 - xl, 1 - xh, y, c))
    beside = pairs(shape, lambda z, xl, xh, y, c: (z, 1 - xl, xh, y, c))
    inner = pairs(shape, lambda z, xl, xh, y, c: (z, xl, 1 - xh, y, c))

    def across(z, xl, xh, y, c):
        here = z * 2 + xl
        there = (here + (1 if xh else -1)) % (2 * deep)
        return there // 2, there % 2, 1 - xh, y, c

    outer = pairs(shape, across)

    def over_y(copies):
        return lax.all_to_all(copies, "y", 0, 0, tiled=True)

    def swapped(array):
        return lax.ppermute(array, AXES, other_core)

    def on_device(points, order, scan_ids, ln_gain, w_qkv, w_out):
        w_turned = jnp.swapaxes(w_qkv, 1, 2)
        (copies,) = call(
            order_kernel, 1.2, [(4, FULL, LANES)],
            [
                ((ROWS, D), BF16), ((1, ROWS), jnp.int32), ((1, ROWS), jnp.int32),
                ((HEAD_DIM, D), BF16),
            ],
            late=(points, order, scan_ids.reshape(1, ROWS), w_out), semaphores=(4,), megabytes=56,
        )
        first = jnp.concatenate([w_turned[0], w_out[1]], axis=0)
        first_far = lax.ppermute(first, AXES, mirror)
        near = over_y(copies)
        near, first_far = lax.optimization_barrier((near, first_far))
        far = swapped(near)

        def out_weights(array):
            return array[:, EXT:].reshape(4, BLOCKS, HEAD_DIM, LANES)

        w_own = out_weights(near)
        w_mir = lax.ppermute(w_own, AXES, mirror)
        projection = [((3 * HEAD_DIM, D), BF16)] * 2
        (o_copies,) = call(
            first_kernel,
            8,
            [(4, PATCH, LANES)],
            [
                ((PATCH, D), BF16),
                ((PATCH, LANES), BF16),
                ((PATCH, 2 * LANES), BF16),
                ((LANES, PATCH), BF16),
                ((2, HEAD_DIM + 16, PATCH), BF16),
                ((PATCH, LANES), BF16),
            ],
            ln_gain, near, far, w_turned, first_far, megabytes=16,
        )
        o_copies, w_mir = lax.optimization_barrier((o_copies, w_mir))
        o_copies, rest = lax.optimization_barrier((o_copies, w_turned[1]))
        rest_far = lax.ppermute(rest, AXES, mirror)
        w_mir_far = swapped(w_mir)
        o_near = over_y(o_copies)
        (shares,) = call(
            relay_kernel, 1, [(8, ROWS, D)], [], w_out[1], first_far, late=(w_mir_far,), megabytes=4
        )
        o_near, w_mir_far, rest_far, shares = lax.optimization_barrier(
            (o_near, w_mir_far, rest_far, shares)
        )
        o_far = swapped(o_near)
        w_last = lax.all_to_all(shares, ("y", "c"), 0, 0, tiled=True).reshape(D, D)
        queries, *kvs, stream = call(
            middle_kernel,
            8,
            [(2, HALF, LANES), (EXT, LANES), (EXT, LANES), (ROWS, D)],
            [
                ((BLOCKS, PATCH, LANES), BF16),
                ((PATCH, D), F32),
                ((PATCH, D), BF16),
                ((PATCH, LANES), BF16),
                ((PATCH, LANES), BF16),
                ((LANES, PATCH), BF16),
                ((BLOCKS, D, LANES), BF16),
                ((2, 4, EXT, LANES), BF16),
                *projection,
            ],
            ln_gain,
            late=(o_near, o_far, near, far, w_mir, w_mir_far, w_turned, rest_far, shares),
            semaphores=(3, 16, 4), megabytes=56,
        )
        halos = [lax.ppermute(kv, AXES, links) for kv, links in zip(kvs, (inner, outer))]
        parts = None
        for part in range(2):
            kv = kvs[part]
            (parts,) = call(
                functools.partial(second_kernel, part),
                3 if part else 0,
                [(8 if part else 4, ROWS, LANES)],
                [
                    ((PATCH, 2 * LANES), BF16),
                    ((2, HEAD_DIM + 16, PATCH), BF16),
                    ((HALF, LANES), BF16),
                ],
                queries, kv, halos[part], *([parts] if part else []),
                megabytes=8,
            )
        parts, w_last = lax.optimization_barrier((parts, w_last))
        parts = lax.all_to_all(parts, ("y", "c"), 0, 0, tiled=True)
        (result,) = call(
            last_kernel, 1.5, [(ROWS, D)], [((ROWS, D), BF16)],
            parts, w_last, stream, megabytes=8,
        )
        return result

    every = ("z", "xl") + head_axes
    return jax.shard_map(
        on_device,
        mesh=Mesh(mesh.devices.reshape(shape), AXES),
        in_specs=(P(every, None), P(every, None), P(every), P(), P(None, None, head_axes), P(None, head_axes, None)),
        out_specs=P(every, None),
        check_vma=False,
    )
```

```python
import functools

import jax
import jax.numpy as jnp
import numpy as np
from jax import lax
from jax.experimental import pallas as pl
from jax.experimental.pallas import tpu as pltpu
from jax.sharding import Mesh
from jax.sharding import PartitionSpec as P

HEAD_DIM = 64
D = 1024
ROWS = 128
PATCH = 1024
HALF = 512
LANES = 128
BLOCKS = D // LANES
EXT = D + 16
FULL = EXT + BLOCKS * HEAD_DIM
EPSILON = 1e-05
FAR = -1e30
AXES = ("z", "xl", "xh", "y", "c")
F32 = jnp.float32
BF16 = jnp.bfloat16


def pairs(shape, move):
    result = []
    for i in range(int(np.prod(shape))):
        place = tuple(int(v) for v in np.unravel_index(i, shape))
        result.append((i, int(np.ravel_multi_index(move(*place), shape))))
    return result


def dot(a, b):
    return lax.dot_general(a, b, (((1,), (0,)), ((), ())), preferred_element_type=F32)


def dot_nt(a, b):
    return lax.dot_general(a, b, (((1,), (1,)), ((), ())), preferred_element_type=F32)


def layer_norm(values, gain):
    center = values - jnp.mean(values, axis=-1, keepdims=True)
    spread = jnp.mean(center * center, axis=-1, keepdims=True)
    return (center * lax.rsqrt(spread + EPSILON) * gain).astype(BF16)


def side_by_side(ref, index):
    return jnp.concatenate([ref[index, b * LANES : (b + 1) * LANES, :] for b in range(BLOCKS)], axis=1)


def tag_columns(rows):
    return jnp.transpose(jnp.concatenate(rows, axis=0))


def one_hot(columns, block):
    lane = lax.broadcasted_iota(jnp.int32, (ROWS, LANES), 1).astype(F32)
    return columns[:, block : block + 1] == lane


def attend(queries, hot, keys_ref, values_ref):
    lane = lax.broadcasted_iota(jnp.int32, queries.shape, 1)
    pieces = [slice(k * 256, (k + 1) * 256) for k in range(4)]
    scores = []
    for head in range(2):
        own = jnp.where(lane // HEAD_DIM == head, queries, jnp.zeros_like(queries))
        both = jnp.concatenate([own, hot], axis=1)
        scores.append([dot_nt(keys_ref[piece, :], both) for piece in pieces])
    results = []
    for head in range(2):
        tops = [jnp.max(part, axis=0, keepdims=True) for part in scores[head]]
        top = functools.reduce(jnp.maximum, tops)
        sums = sum(
            dot(values_ref[head, :, piece], jnp.exp(part - top).astype(BF16))
            for part, piece in zip(scores[head], pieces)
        )
        results.append(sums[:HEAD_DIM] / sums[HEAD_DIM : HEAD_DIM + 1])
    return jnp.transpose(jnp.concatenate(results, axis=0)).astype(BF16)


def fetch(sources, targets, sems):
    copies = [pltpu.make_async_copy(a, b, sems.at[i]) for i, (a, b) in enumerate(zip(sources, targets))]
    for copy in copies:
        copy.start()
    return copies


def order_kernel(points_at, order_at, tags_at, w_at, out, points, order, tags, w, sems):
    copies = fetch((order_at, points_at, tags_at, w_at.at[0]), (order, points, tags, w), sems)
    for copy in copies:
        copy.wait()
    row = lax.broadcasted_iota(jnp.int32, (ROWS, ROWS), 0)
    picks = jnp.transpose((row == order[...]).astype(F32)).astype(BF16)
    ordered = dot(picks, points[...]).astype(BF16)
    tag_rows = jnp.broadcast_to(tags[...].astype(F32), (16, LANES)).astype(BF16)
    for copy in range(4):
        for b in range(BLOCKS):
            out[copy, b * LANES : (b + 1) * LANES, :] = ordered[:, b * LANES : (b + 1) * LANES]
            out[copy, EXT + b * HEAD_DIM : EXT + (b + 1) * HEAD_DIM, :] = w[:, b * LANES : (b + 1) * LANES]
        out[copy, D:EXT, :] = tag_rows


def joined(own, mirrored, kind):
    cut = slice(kind * HEAD_DIM, (kind + 1) * HEAD_DIM)
    return jnp.concatenate([own[cut, :], mirrored[cut, :]], axis=0)


def project(normed, own, mirrored, queries, keys, turned):
    every = jnp.concatenate([joined(own, mirrored, kind) for kind in range(3)], axis=0)
    found = dot_nt(normed, every)
    queries[...] = found[:, :LANES].astype(BF16) * jnp.asarray(HEAD_DIM**-0.5, BF16)
    keys[...] = found[:, LANES : 2 * LANES].astype(BF16)
    turned[...] = jnp.transpose(found[:, 2 * LANES :]).astype(BF16)


def put_values(values_ref, span, turned, swap):
    for head in range(2):
        from_head = 1 - head if swap else head
        values_ref[head, :HEAD_DIM, span] = turned[from_head * HEAD_DIM : (from_head + 1) * HEAD_DIM]


def first_kernel(
    gain, near, far, own, mirrored, out, normed, queries, keys, turned, values, hots
):
    rows = []
    for block in range(8):
        ref, y = (near, far)[block // 4], block % 4
        normed[block * ROWS : (block + 1) * ROWS, :] = layer_norm(
            side_by_side(ref, y).astype(F32), gain[0:1, :]
        )
        rows.append(ref[y, D:EXT, :].astype(F32)[:1])
    columns = tag_columns(rows)
    project(normed[...], own.at[0], mirrored, queries, keys.at[:, :LANES], turned)
    put_values(values, slice(0, PATCH), turned, False)
    values[:, HEAD_DIM:, :] = jnp.ones((2, 16, PATCH), BF16)
    for block in range(8):
        hot = one_hot(columns, block)
        span = slice(block * ROWS, (block + 1) * ROWS)
        hots[span, :] = jnp.where(hot, 1.0, 0.0).astype(BF16)
        keys[span, LANES:] = jnp.where(hot, 0.0, FAR).astype(BF16)
    for part in range(4):
        span = slice(part * 256, (part + 1) * 256)
        result = attend(queries[span, :], hots[span, :], keys, values)
        for copy in range(4):
            out[copy, span, :] = result


def half_of(part):
    xh = lax.axis_index("xh")
    return xh if part else 1 - xh


def middle_kernel(
    gain, o_near, o_far, near, far, w_mir, w_mir_far, own_at, mirrored_at, ready,
    q_out, kv_p, kv_q, st_out,
    heads, update, normed, queries, keys, turned, w, points, own, mirrored,
    o_sems, w_sems, sems,
):
    my_y = lax.axis_index("y")
    sources, targets = [], []
    for i, ref in enumerate((near, w_mir, far, w_mir_far)):
        for g in range(4):
            row = (i // 2 * 4 + g) * LANES + i % 2 * HEAD_DIM
            if i % 2:
                sources.append(ref.at[g])
            else:
                sources.append(ref.at[g, EXT:FULL, :].reshape(BLOCKS, HEAD_DIM, LANES))
            targets.append(w.at[:, row : row + HEAD_DIM, :])
    w_copies = fetch(sources, targets, w_sems)

    late = fetch((own_at.at[1], mirrored_at), (own, mirrored), sems.at[2:4])
    top, end = slice(0, HALF), slice(HALF, PATCH)
    o_copies = fetch(
        (o_near, o_far.at[:, end, :], o_far.at[:, top, :]),
        (heads.at[:4], heads.at[4:, top, :], heads.at[4:, end, :]),
        o_sems,
    )
    x_copies = fetch((near.at[:, :EXT, :], far.at[:, :EXT, :]), (points.at[0], points.at[1]), sems)
    for copy in w_copies + o_copies:
        copy.wait()
    left = jnp.concatenate([heads[g] for g in range(BLOCKS)], axis=1)
    for j in range(2):
        both = jnp.concatenate([w[4 * j + i] for i in range(4)], axis=1)
        update[:, j * 512 : (j + 1) * 512] = dot(left, both)
    rows = []
    for s in range(2):
        x_copies[s].wait()
        for y in range(4):
            there = slice(s * HALF + y * ROWS, s * HALF + (y + 1) * ROWS)
            x = jnp.concatenate(
                [points[s, y, b * LANES : (b + 1) * LANES, :] for b in range(BLOCKS)], axis=1
            )
            stream = (x.astype(F32) + update[there, :]).astype(BF16)
            normed[there, :] = layer_norm(stream.astype(F32), gain[1:2, :])
            rows.append(points[s, y, D:, :].astype(F32)[:1])
            if s == 0:

                @pl.when(y == my_y)
                def _(stream=stream):
                    st_out[...] = stream

    for copy in late:
        copy.wait()
    project(normed[...], own, mirrored, queries, keys, turned)
    for part, kv in enumerate((kv_p, kv_q)):
        half = half_of(part)
        for s in range(2):
            at = pl.multiple_of(s * HALF + half * 256, 256)
            q_out[part, s * 256 : (s + 1) * 256, :] = queries[pl.ds(at, 256), :]
            kv[s * 256 : (s + 1) * 256, :] = keys[pl.ds(at, 256), :]
            for b in range(2):
                cut = slice(HALF + (s * 2 + b) * LANES, HALF + (s * 2 + b + 1) * LANES)
                kv[cut, :] = turned[:, pl.ds(pl.multiple_of(at + b * LANES, LANES), LANES)]
        tags = [jnp.where(half == 0, rows[s * 4 + b], rows[s * 4 + 2 + b]) for s in range(2) for b in range(2)]
        kv[D:, :] = jnp.concatenate(tags + [jnp.zeros((12, LANES), F32)], axis=0).astype(BF16)


def second_kernel(part, *refs):
    if part:
        queries, mine, other, had, out, keys, values, hots = refs
    else:
        queries, mine, other, out, keys, values, hots = refs
    half, c = half_of(part), lax.axis_index("c")
    keys[:HALF, :LANES] = mine[:HALF, :]
    keys[HALF:, :HEAD_DIM] = other[:HALF, HEAD_DIM:]
    keys[HALF:, HEAD_DIM:LANES] = other[:HALF, :HEAD_DIM]
    for b in range(4):
        cut = slice(HALF + b * LANES, HALF + (b + 1) * LANES)
        put_values(values, slice(b * LANES, (b + 1) * LANES), mine[cut, :], False)
        put_values(values, slice(HALF + b * LANES, HALF + (b + 1) * LANES), other[cut, :], True)
    values[:, HEAD_DIM:, :] = jnp.ones((2, 16, PATCH), BF16)
    columns = tag_columns([mine[D:, :].astype(F32)[:4], other[D:, :].astype(F32)[:4]])
    for block in range(8):
        hot = one_hot(columns, block)
        span = slice(block * ROWS, (block + 1) * ROWS)
        if block < 4:
            hots[span, :] = jnp.where(hot, 1.0, 0.0).astype(BF16)
        keys[span, LANES:] = jnp.where(hot, 0.0, FAR).astype(BF16)
    for s in range(2):
        span = slice(s * 256, (s + 1) * 256)
        result = attend(queries[part, span, :], hots[span, :], keys, values)
        core = c if s == 0 else 1 - c
        for yy in range(2):
            block = result[yy * ROWS : (yy + 1) * ROWS]
            if part:
                out[(half * 2 + yy) * 2 + core] = block
                out[((1 - half) * 2 + yy) * 2 + core] = had[s * 2 + yy]
            else:
                out[s * 2 + yy] = block


def last_kernel(parts, w, stream, out, heads):
    for g in range(8):
        heads[:, g * LANES : (g + 1) * LANES] = parts[g]
    update = dot(heads[...], w[...])

    out[...] = (stream[...].astype(F32) + update).astype(BF16)


def relay_kernel(own, rest, ready, out):
    for copy in range(out.shape[0]):
        out[copy, :HEAD_DIM] = own[...]
        out[copy, HEAD_DIM:] = rest[3 * HEAD_DIM :]


def call(kernel, micros, outs, scratch, *args, late=(), semaphores=(), megabytes=16):
    vmem, anywhere = pl.BlockSpec(memory_space=pltpu.VMEM), pl.BlockSpec(memory_space=pl.ANY)
    return pl.pallas_call(
        kernel,
        out_shape=[jax.ShapeDtypeStruct(shape, BF16) for shape in outs],
        in_specs=[vmem] * len(args) + [anywhere] * len(late),
        out_specs=[vmem] * len(outs),
        scratch_shapes=[pltpu.VMEM(shape, dtype) for shape, dtype in scratch]
        + [
            pltpu.SemaphoreType.DMA(count if isinstance(count, tuple) else (count,))
            for count in semaphores
        ],
        compiler_params=pltpu.CompilerParams(vmem_limit_bytes=megabytes * 1024 * 1024),
        cost_estimate=pl.CostEstimate(
            flops=int(micros * 1.1e9), bytes_accessed=0, transcendentals=0
        ),
    )(*args, *late)


def solution(mesh):
    curve, heads = mesh.shape["curve"], mesh.shape["head"]
    shape = (curve // 2, 2, 2, heads // 4, 2)
    deep = shape[0]
    head_axes = ("xh", "y", "c")
    other_core = pairs(shape, lambda z, xl, xh, y, c: (z, xl, xh, y, 1 - c))
    mirror = pairs(shape, lambda z, xl, xh, y, c: (z, 1 - xl, 1 - xh, y, c))
    beside = pairs(shape, lambda z, xl, xh, y, c: (z, 1 - xl, xh, y, c))
    inner = pairs(shape, lambda z, xl, xh, y, c: (z, xl, 1 - xh, y, c))

    def across(z, xl, xh, y, c):
        here = z * 2 + xl
        there = (here + (1 if xh else -1)) % (2 * deep)
        return there // 2, there % 2, 1 - xh, y, c

    outer = pairs(shape, across)

    def over_y(copies):
        return lax.all_to_all(copies, "y", 0, 0, tiled=True)

    def swapped(array):
        return lax.ppermute(array, AXES, other_core)

    def on_device(points, order, scan_ids, ln_gain, w_qkv, w_out):
        w_turned = jnp.swapaxes(w_qkv, 1, 2)
        (copies,) = call(
            order_kernel, 1.2, [(4, FULL, LANES)],
            [
                ((ROWS, D), BF16), ((1, ROWS), jnp.int32), ((1, ROWS), jnp.int32),
                ((HEAD_DIM, D), BF16),
            ],
            late=(points, order, scan_ids.reshape(1, ROWS), w_out), semaphores=(4,), megabytes=56,
        )
        first = jnp.concatenate([w_turned[0], w_out[1]], axis=0)
        first_far = lax.ppermute(first, AXES, mirror)
        near = over_y(copies)
        near, first_far, rest = lax.optimization_barrier((near, first_far, w_turned[1]))
        rest_far = lax.ppermute(rest, AXES, mirror)
        far = swapped(near)

        def out_weights(array):
            return array[:, EXT:].reshape(4, BLOCKS, HEAD_DIM, LANES)

        w_own = out_weights(near)
        projection = [((3 * HEAD_DIM, D), BF16)] * 2
        (o_copies,) = call(
            first_kernel,
            8,
            [(4, PATCH, LANES)],
            [
                ((PATCH, D), BF16),
                ((PATCH, LANES), BF16),
                ((PATCH, 2 * LANES), BF16),
                ((LANES, PATCH), BF16),
                ((2, HEAD_DIM + 16, PATCH), BF16),
                ((PATCH, LANES), BF16),
            ],
            ln_gain, near, far, w_turned, first_far, megabytes=16,
        )
        o_copies, rest_far, w_own = lax.optimization_barrier((o_copies, rest_far, w_own))
        w_mir = lax.ppermute(w_own, AXES, mirror)
        w_mir_far = swapped(w_mir)
        o_near = over_y(o_copies)
        (shares,) = call(
            relay_kernel, 1, [(8, ROWS, D)], [], w_out[1], first_far, late=(rest_far,), megabytes=4
        )
        o_near, w_mir_far, rest_far, shares = lax.optimization_barrier(
            (o_near, w_mir_far, rest_far, shares)
        )
        o_far = swapped(o_near)
        w_last = lax.all_to_all(shares, ("y", "c"), 0, 0, tiled=True).reshape(D, D)
        queries, *kvs, stream = call(
            middle_kernel,
            8,
            [(2, HALF, LANES), (EXT, LANES), (EXT, LANES), (ROWS, D)],
            [
                ((BLOCKS, PATCH, LANES), BF16),
                ((PATCH, D), F32),
                ((PATCH, D), BF16),
                ((PATCH, LANES), BF16),
                ((PATCH, LANES), BF16),
                ((LANES, PATCH), BF16),
                ((BLOCKS, D, LANES), BF16),
                ((2, 4, EXT, LANES), BF16),
                *projection,
            ],
            ln_gain,
            late=(o_near, o_far, near, far, w_mir, w_mir_far, w_turned, rest_far, shares),
            semaphores=(3, 16, 4), megabytes=56,
        )
        halos = [lax.ppermute(kv, AXES, links) for kv, links in zip(kvs, (inner, outer))]
        parts = None
        for part in range(2):
            kv = kvs[part]
            (parts,) = call(
                functools.partial(second_kernel, part),
                3 if part else 0,
                [(8 if part else 4, ROWS, LANES)],
                [
                    ((PATCH, 2 * LANES), BF16),
                    ((2, HEAD_DIM + 16, PATCH), BF16),
                    ((HALF, LANES), BF16),
                ],
                queries, kv, halos[part], *([parts] if part else []),
                megabytes=8,
            )
        parts, w_last = lax.optimization_barrier((parts, w_last))
        parts = lax.all_to_all(parts, ("y", "c"), 0, 0, tiled=True)
        (result,) = call(
            last_kernel, 1.5, [(ROWS, D)], [((ROWS, D), BF16)],
            parts, w_last, stream, megabytes=8,
        )
        return result

    every = ("z", "xl") + head_axes
    return jax.shard_map(
        on_device,
        mesh=Mesh(mesh.devices.reshape(shape), AXES),
        in_specs=(P(every, None), P(every, None), P(every), P(), P(None, None, head_axes), P(None, head_axes, None)),
        out_specs=P(every, None),
        check_vma=False,
    )
```

```python
import functools

import jax
import jax.numpy as jnp
import numpy as np
from jax import lax
from jax.experimental import pallas as pl
from jax.experimental.pallas import tpu as pltpu
from jax.sharding import Mesh
from jax.sharding import PartitionSpec as P

HEAD_DIM = 64
D = 1024
ROWS = 128
PATCH = 1024
HALF = 512
LANES = 128
BLOCKS = D // LANES
EXT = D + 16
QKV_PART = 3 * HEAD_DIM // 2
OUT_PART = HEAD_DIM // 2
FULL = EXT + BLOCKS * HEAD_DIM
EPSILON = 1e-05
FAR = -1e30
AXES = ("z", "xl", "xh", "y", "c")
F32 = jnp.float32
BF16 = jnp.bfloat16


def pairs(shape, move):
    result = []
    for i in range(int(np.prod(shape))):
        place = tuple(int(v) for v in np.unravel_index(i, shape))
        result.append((i, int(np.ravel_multi_index(move(*place), shape))))
    return result


def dot(a, b):
    return lax.dot_general(a, b, (((1,), (0,)), ((), ())), preferred_element_type=F32)


def dot_nt(a, b):
    return lax.dot_general(a, b, (((1,), (1,)), ((), ())), preferred_element_type=F32)


def layer_norm(values, gain):
    center = values - jnp.mean(values, axis=-1, keepdims=True)
    spread = jnp.mean(center * center, axis=-1, keepdims=True)
    return (center * lax.rsqrt(spread + EPSILON) * gain).astype(BF16)


def side_by_side(ref, index):
    return jnp.concatenate([ref[index, b * LANES : (b + 1) * LANES, :] for b in range(BLOCKS)], axis=1)


def tag_columns(rows):
    return jnp.transpose(jnp.concatenate(rows, axis=0))


def one_hot(columns, block):
    lane = lax.broadcasted_iota(jnp.int32, (ROWS, LANES), 1).astype(F32)
    return columns[:, block : block + 1] == lane


def attend(queries, hot, keys_ref, values_ref):
    lane = lax.broadcasted_iota(jnp.int32, queries.shape, 1)
    pieces = [slice(k * 256, (k + 1) * 256) for k in range(4)]
    scores = []
    for head in range(2):
        own = jnp.where(lane // HEAD_DIM == head, queries, jnp.zeros_like(queries))
        both = jnp.concatenate([own, hot], axis=1)
        scores.append([dot_nt(keys_ref[piece, :], both) for piece in pieces])
    results = []
    for head in range(2):
        tops = [jnp.max(part, axis=0, keepdims=True) for part in scores[head]]
        top = functools.reduce(jnp.maximum, tops)
        sums = sum(
            dot(values_ref[head, :, piece], jnp.exp(part - top).astype(BF16))
            for part, piece in zip(scores[head], pieces)
        )
        results.append(sums[:HEAD_DIM] / sums[HEAD_DIM : HEAD_DIM + 1])
    return jnp.transpose(jnp.concatenate(results, axis=0)).astype(BF16)


def fetch(sources, targets, sems):
    copies = [pltpu.make_async_copy(a, b, sems.at[i]) for i, (a, b) in enumerate(zip(sources, targets))]
    for copy in copies:
        copy.start()
    return copies


def order_kernel(points_at, order_at, tags_at, w_at, out, points, order, tags, w, sems):
    copies = fetch((order_at, points_at, tags_at, w_at.at[0]), (order, points, tags, w), sems)
    for copy in copies:
        copy.wait()
    row = lax.broadcasted_iota(jnp.int32, (ROWS, ROWS), 0)
    picks = jnp.transpose((row == order[...]).astype(F32)).astype(BF16)
    ordered = dot(picks, points[...]).astype(BF16)
    tag_rows = jnp.broadcast_to(tags[...].astype(F32), (16, LANES)).astype(BF16)
    for copy in range(4):
        for b in range(BLOCKS):
            out[copy, b * LANES : (b + 1) * LANES, :] = ordered[:, b * LANES : (b + 1) * LANES]
            out[copy, EXT + b * HEAD_DIM : EXT + (b + 1) * HEAD_DIM, :] = w[:, b * LANES : (b + 1) * LANES]
        out[copy, D:EXT, :] = tag_rows


def joined(own, mirrored, kind):
    cut = slice(kind * HEAD_DIM, (kind + 1) * HEAD_DIM)
    return jnp.concatenate([own[cut, :], mirrored[cut, :]], axis=0)


def project(normed, own, mirrored, queries, keys, turned):
    every = jnp.concatenate([joined(own, mirrored, kind) for kind in range(3)], axis=0)
    found = dot_nt(normed, every)
    queries[...] = found[:, :LANES].astype(BF16) * jnp.asarray(HEAD_DIM**-0.5, BF16)
    keys[...] = found[:, LANES : 2 * LANES].astype(BF16)
    turned[...] = jnp.transpose(found[:, 2 * LANES :]).astype(BF16)


def put_values(values_ref, span, turned, swap):
    for head in range(2):
        from_head = 1 - head if swap else head
        values_ref[head, :HEAD_DIM, span] = turned[from_head * HEAD_DIM : (from_head + 1) * HEAD_DIM]


def first_kernel(
    gain, near, far, own, mirrored, out, w_own, normed, queries, keys, turned, values, hots
):
    rows = []
    for block in range(8):
        ref, y = (near, far)[block // 4], block % 4
        normed[block * ROWS : (block + 1) * ROWS, :] = layer_norm(
            side_by_side(ref, y).astype(F32), gain[0:1, :]
        )
        rows.append(ref[y, D:EXT, :].astype(F32)[:1])
    for y in range(4):
        for b in range(BLOCKS):
            w_own[y, b] = near[y, EXT + b * HEAD_DIM : EXT + (b + 1) * HEAD_DIM, :]
    columns = tag_columns(rows)
    project(normed[...], own.at[0], mirrored, queries, keys.at[:, :LANES], turned)
    put_values(values, slice(0, PATCH), turned, False)
    values[:, HEAD_DIM:, :] = jnp.ones((2, 16, PATCH), BF16)
    for block in range(8):
        hot = one_hot(columns, block)
        span = slice(block * ROWS, (block + 1) * ROWS)
        hots[span, :] = jnp.where(hot, 1.0, 0.0).astype(BF16)
        keys[span, LANES:] = jnp.where(hot, 0.0, FAR).astype(BF16)
    for part in range(4):
        span = slice(part * 256, (part + 1) * 256)
        result = attend(queries[span, :], hots[span, :], keys, values)
        for copy in range(4):
            out[copy, span, :] = result


def half_of(part):
    xh = lax.axis_index("xh")
    return xh if part else 1 - xh


def middle_kernel(
    gain, o_near, o_far, near, far, w_mir, w_mir_far, own_at, mine_at, other_at, ready,
    q_out, kv_p, kv_q, st_out,
    heads, update, normed, queries, keys, turned, w, points, own, mirrored,
    o_sems, w_sems, sems,
):
    my_y = lax.axis_index("y")
    sources, targets = [], []
    for i, ref in enumerate((near, w_mir, far, w_mir_far)):
        for g in range(4):
            row = (i // 2 * 4 + g) * LANES + i % 2 * HEAD_DIM
            if i % 2:
                sources.append(ref.at[g])
            else:
                sources.append(ref.at[g, EXT:FULL, :].reshape(BLOCKS, HEAD_DIM, LANES))
            targets.append(w.at[:, row : row + HEAD_DIM, :])
    w_copies = fetch(sources, targets, w_sems)

    xl = lax.axis_index("xl")
    at_mine, at_other = [
        pl.ds(pl.multiple_of(k * QKV_PART, QKV_PART), QKV_PART) for k in (xl, 1 - xl)
    ]
    late = fetch(
        (own_at.at[1], mine_at.at[:QKV_PART], other_at.at[:QKV_PART]),
        (own, mirrored.at[at_mine, :], mirrored.at[at_other, :]),
        sems.at[2:5],
    )
    top, end = slice(0, HALF), slice(HALF, PATCH)
    o_copies = fetch(
        (o_near, o_far.at[:, end, :], o_far.at[:, top, :]),
        (heads.at[:4], heads.at[4:, top, :], heads.at[4:, end, :]),
        o_sems,
    )
    x_copies = fetch((near.at[:, :EXT, :], far.at[:, :EXT, :]), (points.at[0], points.at[1]), sems)
    for copy in w_copies + o_copies:
        copy.wait()
    left = jnp.concatenate([heads[g] for g in range(BLOCKS)], axis=1)
    for j in range(2):
        both = jnp.concatenate([w[4 * j + i] for i in range(4)], axis=1)
        update[:, j * 512 : (j + 1) * 512] = dot(left, both)
    rows = []
    for s in range(2):
        x_copies[s].wait()
        for y in range(4):
            there = slice(s * HALF + y * ROWS, s * HALF + (y + 1) * ROWS)
            x = jnp.concatenate(
                [points[s, y, b * LANES : (b + 1) * LANES, :] for b in range(BLOCKS)], axis=1
            )
            stream = (x.astype(F32) + update[there, :]).astype(BF16)
            normed[there, :] = layer_norm(stream.astype(F32), gain[1:2, :])
            rows.append(points[s, y, D:, :].astype(F32)[:1])
            if s == 0:

                @pl.when(y == my_y)
                def _(stream=stream):
                    st_out[...] = stream

    for copy in late:
        copy.wait()
    project(normed[...], own, mirrored, queries, keys, turned)
    for part, kv in enumerate((kv_p, kv_q)):
        half = half_of(part)
        for s in range(2):
            at = pl.multiple_of(s * HALF + half * 256, 256)
            q_out[part, s * 256 : (s + 1) * 256, :] = queries[pl.ds(at, 256), :]
            kv[s * 256 : (s + 1) * 256, :] = keys[pl.ds(at, 256), :]
            for b in range(2):
                cut = slice(HALF + (s * 2 + b) * LANES, HALF + (s * 2 + b + 1) * LANES)
                kv[cut, :] = turned[:, pl.ds(pl.multiple_of(at + b * LANES, LANES), LANES)]
        tags = [jnp.where(half == 0, rows[s * 4 + b], rows[s * 4 + 2 + b]) for s in range(2) for b in range(2)]
        kv[D:, :] = jnp.concatenate(tags + [jnp.zeros((12, LANES), F32)], axis=0).astype(BF16)


def second_kernel(part, *refs):
    if part:
        queries, mine, other, had, out, keys, values, hots = refs
    else:
        queries, mine, other, out, keys, values, hots = refs
    half, c = half_of(part), lax.axis_index("c")
    keys[:HALF, :LANES] = mine[:HALF, :]
    keys[HALF:, :HEAD_DIM] = other[:HALF, HEAD_DIM:]
    keys[HALF:, HEAD_DIM:LANES] = other[:HALF, :HEAD_DIM]
    for b in range(4):
        cut = slice(HALF + b * LANES, HALF + (b + 1) * LANES)
        put_values(values, slice(b * LANES, (b + 1) * LANES), mine[cut, :], False)
        put_values(values, slice(HALF + b * LANES, HALF + (b + 1) * LANES), other[cut, :], True)
    values[:, HEAD_DIM:, :] = jnp.ones((2, 16, PATCH), BF16)
    columns = tag_columns([mine[D:, :].astype(F32)[:4], other[D:, :].astype(F32)[:4]])
    for block in range(8):
        hot = one_hot(columns, block)
        span = slice(block * ROWS, (block + 1) * ROWS)
        if block < 4:
            hots[span, :] = jnp.where(hot, 1.0, 0.0).astype(BF16)
        keys[span, LANES:] = jnp.where(hot, 0.0, FAR).astype(BF16)
    for s in range(2):
        span = slice(s * 256, (s + 1) * 256)
        result = attend(queries[part, span, :], hots[span, :], keys, values)
        core = c if s == 0 else 1 - c
        for yy in range(2):
            block = result[yy * ROWS : (yy + 1) * ROWS]
            if part:
                out[(half * 2 + yy) * 2 + core] = block
                out[((1 - half) * 2 + yy) * 2 + core] = had[s * 2 + yy]
            else:
                out[s * 2 + yy] = block


def last_kernel(parts, w, stream, out, heads):
    for g in range(8):
        heads[:, g * LANES : (g + 1) * LANES] = parts[g]
    update = dot(heads[...], w[...])

    out[...] = (stream[...].astype(F32) + update).astype(BF16)


def relay_kernel(own, mine, other, out):
    xl = lax.axis_index("xl")
    at_mine, at_other = [
        pl.ds(pl.multiple_of(HEAD_DIM + k * OUT_PART, OUT_PART), OUT_PART) for k in (xl, 1 - xl)
    ]
    for copy in range(out.shape[0]):
        out[copy, :HEAD_DIM] = own[...]
        out[copy, at_mine, :] = mine[QKV_PART:]
        out[copy, at_other, :] = other[QKV_PART:]


def call(kernel, micros, outs, scratch, *args, late=(), semaphores=(), megabytes=16):
    vmem, anywhere = pl.BlockSpec(memory_space=pltpu.VMEM), pl.BlockSpec(memory_space=pl.ANY)
    return pl.pallas_call(
        kernel,
        out_shape=[jax.ShapeDtypeStruct(shape, BF16) for shape in outs],
        in_specs=[vmem] * len(args) + [anywhere] * len(late),
        out_specs=[vmem] * len(outs),
        scratch_shapes=[pltpu.VMEM(shape, dtype) for shape, dtype in scratch]
        + [
            pltpu.SemaphoreType.DMA(count if isinstance(count, tuple) else (count,))
            for count in semaphores
        ],
        compiler_params=pltpu.CompilerParams(vmem_limit_bytes=megabytes * 1024 * 1024),
        cost_estimate=pl.CostEstimate(
            flops=int(micros * 1.1e9), bytes_accessed=0, transcendentals=0
        ),
    )(*args, *late)


def solution(mesh):
    curve, heads = mesh.shape["curve"], mesh.shape["head"]
    shape = (curve // 2, 2, 2, heads // 4, 2)
    deep = shape[0]
    head_axes = ("xh", "y", "c")
    other_core = pairs(shape, lambda z, xl, xh, y, c: (z, xl, xh, y, 1 - c))
    mirror = pairs(shape, lambda z, xl, xh, y, c: (z, 1 - xl, 1 - xh, y, c))
    beside = pairs(shape, lambda z, xl, xh, y, c: (z, 1 - xl, xh, y, c))
    inner = pairs(shape, lambda z, xl, xh, y, c: (z, xl, 1 - xh, y, c))

    def across(z, xl, xh, y, c):
        here = z * 2 + xl
        there = (here + (1 if xh else -1)) % (2 * deep)
        return there // 2, there % 2, 1 - xh, y, c

    outer = pairs(shape, across)

    def over_y(copies):
        return lax.all_to_all(copies, "y", 0, 0, tiled=True)

    def swapped(array):
        return lax.ppermute(array, AXES, other_core)

    def on_device(points, order, scan_ids, ln_gain, w_qkv, w_out):
        w_turned = jnp.swapaxes(w_qkv, 1, 2)
        (copies,) = call(
            order_kernel, 1.2, [(4, FULL, LANES)],
            [
                ((ROWS, D), BF16), ((1, ROWS), jnp.int32), ((1, ROWS), jnp.int32),
                ((HEAD_DIM, D), BF16),
            ],
            late=(points, order, scan_ids.reshape(1, ROWS), w_out), semaphores=(4,), megabytes=56,
        )
        share = 1 - lax.axis_index("xl")
        first = jnp.concatenate(
            [
                w_turned[0],
                lax.dynamic_slice_in_dim(w_turned[1], share * QKV_PART, QKV_PART, 0),
                lax.dynamic_slice_in_dim(w_out[1], share * OUT_PART, OUT_PART, 0),
            ],
            axis=0,
        )
        first_far = lax.ppermute(first, AXES, mirror)
        near = over_y(copies)
        near, first_far = lax.optimization_barrier((near, first_far))
        far = swapped(near)

        projection = [((3 * HEAD_DIM, D), BF16)] * 2
        o_copies, w_own = call(
            first_kernel,
            8,
            [(4, PATCH, LANES), (4, BLOCKS, HEAD_DIM, LANES)],
            [
                ((PATCH, D), BF16),
                ((PATCH, LANES), BF16),
                ((PATCH, 2 * LANES), BF16),
                ((LANES, PATCH), BF16),
                ((2, HEAD_DIM + 16, PATCH), BF16),
                ((PATCH, LANES), BF16),
            ],
            ln_gain, near, far, w_turned, first_far, megabytes=16,
        )
        share_far = first_far[3 * HEAD_DIM :]
        o_copies, w_own, share_far = lax.optimization_barrier((o_copies, w_own, share_far))
        rest_far = lax.ppermute(share_far, AXES, beside)
        w_mir = lax.ppermute(w_own, AXES, mirror)
        w_mir, rest_far = lax.optimization_barrier((w_mir, rest_far))
        w_mir_far = swapped(w_mir)
        o_near = over_y(o_copies)
        (shares,) = call(
            relay_kernel, 1, [(8, ROWS, D)], [], w_out[1], share_far, rest_far, megabytes=4
        )
        o_near, w_mir_far, rest_far, shares = lax.optimization_barrier(
            (o_near, w_mir_far, rest_far, shares)
        )
        o_far = swapped(o_near)
        w_last = lax.all_to_all(shares, ("y", "c"), 0, 0, tiled=True).reshape(D, D)
        queries, *kvs, stream = call(
            middle_kernel,
            8,
            [(2, HALF, LANES), (EXT, LANES), (EXT, LANES), (ROWS, D)],
            [
                ((BLOCKS, PATCH, LANES), BF16),
                ((PATCH, D), F32),
                ((PATCH, D), BF16),
                ((PATCH, LANES), BF16),
                ((PATCH, LANES), BF16),
                ((LANES, PATCH), BF16),
                ((BLOCKS, D, LANES), BF16),
                ((2, 4, EXT, LANES), BF16),
                *projection,
            ],
            ln_gain,
            late=(o_near, o_far, near, far, w_mir, w_mir_far, w_turned, share_far, rest_far, shares),
            semaphores=(3, 16, 5), megabytes=56,
        )
        halos = [lax.ppermute(kv, AXES, links) for kv, links in zip(kvs, (inner, outer))]
        parts = None
        for part in range(2):
            kv = kvs[part]
            (parts,) = call(
                functools.partial(second_kernel, part),
                3 if part else 0,
                [(8 if part else 4, ROWS, LANES)],
                [
                    ((PATCH, 2 * LANES), BF16),
                    ((2, HEAD_DIM + 16, PATCH), BF16),
                    ((HALF, LANES), BF16),
                ],
                queries, kv, halos[part], *([parts] if part else []),
                megabytes=8,
            )
        parts, w_last = lax.optimization_barrier((parts, w_last))
        parts = lax.all_to_all(parts, ("y", "c"), 0, 0, tiled=True)
        (result,) = call(
            last_kernel, 1.5, [(ROWS, D)], [((ROWS, D), BF16)],
            parts, w_last, stream, megabytes=8,
        )
        return result

    every = ("z", "xl") + head_axes
    return jax.shard_map(
        on_device,
        mesh=Mesh(mesh.devices.reshape(shape), AXES),
        in_specs=(P(every, None), P(every, None), P(every), P(), P(None, None, head_axes), P(None, head_axes, None)),
        out_specs=P(every, None),
        check_vma=False,
    )
```

```python
import functools

import jax
import jax.numpy as jnp
import numpy as np
from jax import lax
from jax.experimental import pallas as pl
from jax.experimental.pallas import tpu as pltpu
from jax.sharding import Mesh
from jax.sharding import PartitionSpec as P

HEAD_DIM = 64
D = 1024
ROWS = 128
PATCH = 1024
HALF = 512
LANES = 128
BLOCKS = D // LANES
EXT = D + 16
QKV_PART = 3 * HEAD_DIM // 2
OUT_PART = HEAD_DIM // 2
FULL = EXT + BLOCKS * HEAD_DIM
EPSILON = 1e-05
FAR = -1e30
AXES = ("z", "xl", "xh", "y", "c")
F32 = jnp.float32
BF16 = jnp.bfloat16


def pairs(shape, move):
    result = []
    for i in range(int(np.prod(shape))):
        place = tuple(int(v) for v in np.unravel_index(i, shape))
        result.append((i, int(np.ravel_multi_index(move(*place), shape))))
    return result


def dot(a, b):
    return lax.dot_general(a, b, (((1,), (0,)), ((), ())), preferred_element_type=F32)


def dot_nt(a, b):
    return lax.dot_general(a, b, (((1,), (1,)), ((), ())), preferred_element_type=F32)


def layer_norm(values, gain):
    center = values - jnp.mean(values, axis=-1, keepdims=True)
    spread = jnp.mean(center * center, axis=-1, keepdims=True)
    return (center * lax.rsqrt(spread + EPSILON) * gain).astype(BF16)


def side_by_side(ref, index):
    return jnp.concatenate([ref[index, b * LANES : (b + 1) * LANES, :] for b in range(BLOCKS)], axis=1)


def tag_columns(rows):
    return jnp.transpose(jnp.concatenate(rows, axis=0))


def one_hot(columns, block):
    lane = lax.broadcasted_iota(jnp.int32, (ROWS, LANES), 1).astype(F32)
    return columns[:, block : block + 1] == lane


def attend(queries, hot, keys_ref, values_ref):
    lane = lax.broadcasted_iota(jnp.int32, queries.shape, 1)
    pieces = [slice(k * 256, (k + 1) * 256) for k in range(4)]
    scores = []
    for head in range(2):
        own = jnp.where(lane // HEAD_DIM == head, queries, jnp.zeros_like(queries))
        both = jnp.concatenate([own, hot], axis=1)
        scores.append([dot_nt(keys_ref[piece, :], both) for piece in pieces])
    results = []
    for head in range(2):
        tops = [jnp.max(part, axis=0, keepdims=True) for part in scores[head]]
        top = functools.reduce(jnp.maximum, tops)
        sums = sum(
            dot(values_ref[head, :, piece], jnp.exp(part - top).astype(BF16))
            for part, piece in zip(scores[head], pieces)
        )
        results.append(sums[:HEAD_DIM] / sums[HEAD_DIM : HEAD_DIM + 1])
    return jnp.transpose(jnp.concatenate(results, axis=0)).astype(BF16)


def fetch(sources, targets, sems):
    copies = [pltpu.make_async_copy(a, b, sems.at[i]) for i, (a, b) in enumerate(zip(sources, targets))]
    for copy in copies:
        copy.start()
    return copies


def order_kernel(points_at, order_at, tags_at, w_at, out, points, order, tags, w, sems):
    copies = fetch((order_at, points_at, tags_at, w_at.at[0]), (order, points, tags, w), sems)
    for copy in copies:
        copy.wait()
    row = lax.broadcasted_iota(jnp.int32, (ROWS, ROWS), 0)
    picks = jnp.transpose((row == order[...]).astype(F32)).astype(BF16)
    ordered = dot(picks, points[...]).astype(BF16)
    tag_rows = jnp.broadcast_to(tags[...].astype(F32), (16, LANES)).astype(BF16)
    for copy in range(4):
        for b in range(BLOCKS):
            out[copy, b * LANES : (b + 1) * LANES, :] = ordered[:, b * LANES : (b + 1) * LANES]
            out[copy, EXT + b * HEAD_DIM : EXT + (b + 1) * HEAD_DIM, :] = w[:, b * LANES : (b + 1) * LANES]
        out[copy, D:EXT, :] = tag_rows


def joined(own, mirrored, kind):
    cut = slice(kind * HEAD_DIM, (kind + 1) * HEAD_DIM)
    return jnp.concatenate([own[cut, :], mirrored[cut, :]], axis=0)


def project(normed, own, mirrored, queries, keys, turned):
    every = jnp.concatenate([joined(own, mirrored, kind) for kind in range(3)], axis=0)
    found = dot_nt(normed, every)
    queries[...] = found[:, :LANES].astype(BF16) * jnp.asarray(HEAD_DIM**-0.5, BF16)
    keys[...] = found[:, LANES : 2 * LANES].astype(BF16)
    turned[...] = jnp.transpose(found[:, 2 * LANES :]).astype(BF16)


def put_values(values_ref, span, turned, swap):
    for head in range(2):
        from_head = 1 - head if swap else head
        values_ref[head, :HEAD_DIM, span] = turned[from_head * HEAD_DIM : (from_head + 1) * HEAD_DIM]


def first_kernel(
    gain, near, far, own, mirrored, out, normed, queries, keys, turned, values, hots
):
    rows = []
    for block in range(8):
        ref, y = (near, far)[block // 4], block % 4
        normed[block * ROWS : (block + 1) * ROWS, :] = layer_norm(
            side_by_side(ref, y).astype(F32), gain[0:1, :]
        )
        rows.append(ref[y, D:EXT, :].astype(F32)[:1])
    columns = tag_columns(rows)
    project(normed[...], own.at[0], mirrored, queries, keys.at[:, :LANES], turned)
    put_values(values, slice(0, PATCH), turned, False)
    values[:, HEAD_DIM:, :] = jnp.ones((2, 16, PATCH), BF16)
    for block in range(8):
        hot = one_hot(columns, block)
        span = slice(block * ROWS, (block + 1) * ROWS)
        hots[span, :] = jnp.where(hot, 1.0, 0.0).astype(BF16)
        keys[span, LANES:] = jnp.where(hot, 0.0, FAR).astype(BF16)
    for part in range(4):
        span = slice(part * 256, (part + 1) * 256)
        result = attend(queries[span, :], hots[span, :], keys, values)
        for copy in range(4):
            out[copy, span, :] = result


def half_of(part):
    xh = lax.axis_index("xh")
    return xh if part else 1 - xh


def middle_kernel(
    gain, o_near, o_far, near, far, w_mir, w_mir_far, own_at, mine_at, other_at, ready,
    q_out, kv_p, kv_q, st_out,
    heads, update, normed, queries, keys, turned, w, points, own, mirrored,
    o_sems, w_sems, sems,
):
    my_y = lax.axis_index("y")
    sources, targets = [], []
    for i, ref in enumerate((near, w_mir, far, w_mir_far)):
        for g in range(4):
            row = (i // 2 * 4 + g) * LANES + i % 2 * HEAD_DIM
            if i % 2:
                sources.append(ref.at[g])
            else:
                sources.append(ref.at[g, EXT:FULL, :].reshape(BLOCKS, HEAD_DIM, LANES))
            targets.append(w.at[:, row : row + HEAD_DIM, :])
    w_copies = fetch(sources, targets, w_sems)

    xl = lax.axis_index("xl")
    at_mine, at_other = [
        pl.ds(pl.multiple_of(k * QKV_PART, QKV_PART), QKV_PART) for k in (xl, 1 - xl)
    ]
    late = fetch(
        (own_at.at[1], mine_at.at[:QKV_PART], other_at.at[:QKV_PART]),
        (own, mirrored.at[at_mine, :], mirrored.at[at_other, :]),
        sems.at[2:5],
    )
    top, end = slice(0, HALF), slice(HALF, PATCH)
    o_copies = fetch(
        (o_near, o_far.at[:, end, :], o_far.at[:, top, :]),
        (heads.at[:4], heads.at[4:, top, :], heads.at[4:, end, :]),
        o_sems,
    )
    x_copies = fetch((near.at[:, :EXT, :], far.at[:, :EXT, :]), (points.at[0], points.at[1]), sems)
    for copy in w_copies + o_copies:
        copy.wait()
    left = jnp.concatenate([heads[g] for g in range(BLOCKS)], axis=1)
    for j in range(2):
        both = jnp.concatenate([w[4 * j + i] for i in range(4)], axis=1)
        update[:, j * 512 : (j + 1) * 512] = dot(left, both)
    rows = []
    for s in range(2):
        x_copies[s].wait()
        for y in range(4):
            there = slice(s * HALF + y * ROWS, s * HALF + (y + 1) * ROWS)
            x = jnp.concatenate(
                [points[s, y, b * LANES : (b + 1) * LANES, :] for b in range(BLOCKS)], axis=1
            )
            stream = (x.astype(F32) + update[there, :]).astype(BF16)
            normed[there, :] = layer_norm(stream.astype(F32), gain[1:2, :])
            rows.append(points[s, y, D:, :].astype(F32)[:1])
            if s == 0:

                @pl.when(y == my_y)
                def _(stream=stream):
                    st_out[...] = stream

    for copy in late:
        copy.wait()
    project(normed[...], own, mirrored, queries, keys, turned)
    for part, kv in enumerate((kv_p, kv_q)):
        half = half_of(part)
        for s in range(2):
            at = pl.multiple_of(s * HALF + half * 256, 256)
            q_out[part, s * 256 : (s + 1) * 256, :] = queries[pl.ds(at, 256), :]
            kv[s * 256 : (s + 1) * 256, :] = keys[pl.ds(at, 256), :]
            for b in range(2):
                cut = slice(HALF + (s * 2 + b) * LANES, HALF + (s * 2 + b + 1) * LANES)
                kv[cut, :] = turned[:, pl.ds(pl.multiple_of(at + b * LANES, LANES), LANES)]
        tags = [jnp.where(half == 0, rows[s * 4 + b], rows[s * 4 + 2 + b]) for s in range(2) for b in range(2)]
        kv[D:, :] = jnp.concatenate(tags + [jnp.zeros((12, LANES), F32)], axis=0).astype(BF16)


def second_kernel(part, *refs):
    if part:
        queries, mine, other, had, out, keys, values, hots = refs
    else:
        queries, mine, other, out, keys, values, hots = refs
    half, c = half_of(part), lax.axis_index("c")
    keys[:HALF, :LANES] = mine[:HALF, :]
    keys[HALF:, :HEAD_DIM] = other[:HALF, HEAD_DIM:]
    keys[HALF:, HEAD_DIM:LANES] = other[:HALF, :HEAD_DIM]
    for b in range(4):
        cut = slice(HALF + b * LANES, HALF + (b + 1) * LANES)
        put_values(values, slice(b * LANES, (b + 1) * LANES), mine[cut, :], False)
        put_values(values, slice(HALF + b * LANES, HALF + (b + 1) * LANES), other[cut, :], True)
    values[:, HEAD_DIM:, :] = jnp.ones((2, 16, PATCH), BF16)
    columns = tag_columns([mine[D:, :].astype(F32)[:4], other[D:, :].astype(F32)[:4]])
    for block in range(8):
        hot = one_hot(columns, block)
        span = slice(block * ROWS, (block + 1) * ROWS)
        if block < 4:
            hots[span, :] = jnp.where(hot, 1.0, 0.0).astype(BF16)
        keys[span, LANES:] = jnp.where(hot, 0.0, FAR).astype(BF16)
    for s in range(2):
        span = slice(s * 256, (s + 1) * 256)
        result = attend(queries[part, span, :], hots[span, :], keys, values)
        core = c if s == 0 else 1 - c
        for yy in range(2):
            block = result[yy * ROWS : (yy + 1) * ROWS]
            if part:
                out[(half * 2 + yy) * 2 + core] = block
                out[((1 - half) * 2 + yy) * 2 + core] = had[s * 2 + yy]
            else:
                out[s * 2 + yy] = block


def last_kernel(parts, w, stream, out, heads):
    for g in range(8):
        heads[:, g * LANES : (g + 1) * LANES] = parts[g]
    update = dot(heads[...], w[...])

    out[...] = (stream[...].astype(F32) + update).astype(BF16)


def relay_kernel(own, mine, other, out):
    xl = lax.axis_index("xl")
    at_mine, at_other = [
        pl.ds(pl.multiple_of(HEAD_DIM + k * OUT_PART, OUT_PART), OUT_PART) for k in (xl, 1 - xl)
    ]
    for copy in range(out.shape[0]):
        out[copy, :HEAD_DIM] = own[...]
        out[copy, at_mine, :] = mine[QKV_PART:]
        out[copy, at_other, :] = other[QKV_PART:]


def call(kernel, micros, outs, scratch, *args, late=(), semaphores=(), megabytes=16):
    vmem, anywhere = pl.BlockSpec(memory_space=pltpu.VMEM), pl.BlockSpec(memory_space=pl.ANY)
    return pl.pallas_call(
        kernel,
        out_shape=[jax.ShapeDtypeStruct(shape, BF16) for shape in outs],
        in_specs=[vmem] * len(args) + [anywhere] * len(late),
        out_specs=[vmem] * len(outs),
        scratch_shapes=[pltpu.VMEM(shape, dtype) for shape, dtype in scratch]
        + [
            pltpu.SemaphoreType.DMA(count if isinstance(count, tuple) else (count,))
            for count in semaphores
        ],
        compiler_params=pltpu.CompilerParams(vmem_limit_bytes=megabytes * 1024 * 1024),
        cost_estimate=pl.CostEstimate(
            flops=int(micros * 1.1e9), bytes_accessed=0, transcendentals=0
        ),
    )(*args, *late)


def solution(mesh):
    curve, heads = mesh.shape["curve"], mesh.shape["head"]
    shape = (curve // 2, 2, 2, heads // 4, 2)
    deep = shape[0]
    head_axes = ("xh", "y", "c")
    other_core = pairs(shape, lambda z, xl, xh, y, c: (z, xl, xh, y, 1 - c))
    mirror = pairs(shape, lambda z, xl, xh, y, c: (z, 1 - xl, 1 - xh, y, c))
    beside = pairs(shape, lambda z, xl, xh, y, c: (z, 1 - xl, xh, y, c))
    inner = pairs(shape, lambda z, xl, xh, y, c: (z, xl, 1 - xh, y, c))

    def across(z, xl, xh, y, c):
        here = z * 2 + xl
        there = (here + (1 if xh else -1)) % (2 * deep)
        return there // 2, there % 2, 1 - xh, y, c

    outer = pairs(shape, across)

    def over_y(copies):
        return lax.all_to_all(copies, "y", 0, 0, tiled=True)

    def swapped(array):
        return lax.ppermute(array, AXES, other_core)

    def on_device(points, order, scan_ids, ln_gain, w_qkv, w_out):
        w_turned = jnp.swapaxes(w_qkv, 1, 2)
        (copies,) = call(
            order_kernel, 1.2, [(4, FULL, LANES)],
            [
                ((ROWS, D), BF16), ((1, ROWS), jnp.int32), ((1, ROWS), jnp.int32),
                ((HEAD_DIM, D), BF16),
            ],
            late=(points, order, scan_ids.reshape(1, ROWS), w_out), semaphores=(4,), megabytes=56,
        )
        share = 1 - lax.axis_index("xl")
        first = jnp.concatenate(
            [
                w_turned[0],
                lax.dynamic_slice_in_dim(w_turned[1], share * QKV_PART, QKV_PART, 0),
                lax.dynamic_slice_in_dim(w_out[1], share * OUT_PART, OUT_PART, 0),
            ],
            axis=0,
        )
        first_far = lax.ppermute(first, AXES, mirror)
        near = over_y(copies)
        near, first_far = lax.optimization_barrier((near, first_far))
        far = swapped(near)

        projection = [((3 * HEAD_DIM, D), BF16)] * 2
        (o_copies,) = call(
            first_kernel,
            8,
            [(4, PATCH, LANES)],
            [
                ((PATCH, D), BF16),
                ((PATCH, LANES), BF16),
                ((PATCH, 2 * LANES), BF16),
                ((LANES, PATCH), BF16),
                ((2, HEAD_DIM + 16, PATCH), BF16),
                ((PATCH, LANES), BF16),
            ],
            ln_gain, near, far, w_turned, first_far, megabytes=16,
        )
        w_own = near[:, EXT:].reshape(4, BLOCKS, HEAD_DIM, LANES)
        share_far = first_far[3 * HEAD_DIM :]
        o_copies, w_own, share_far = lax.optimization_barrier((o_copies, w_own, share_far))
        rest_far = lax.ppermute(share_far, AXES, beside)
        w_mir = lax.ppermute(w_own, AXES, mirror)
        (shares,) = call(
            relay_kernel, 1, [(8, ROWS, D)], [], w_out[1], share_far, rest_far, megabytes=4
        )
        o_near, w_mir, rest_far, shares = lax.optimization_barrier(
            (over_y(o_copies), w_mir, rest_far, shares)
        )
        o_far = swapped(o_near)
        w_mir_far = swapped(w_mir)
        w_last = lax.all_to_all(shares, ("y", "c"), 0, 0, tiled=True).reshape(D, D)
        queries, *kvs, stream = call(
            middle_kernel,
            8,
            [(2, HALF, LANES), (EXT, LANES), (EXT, LANES), (ROWS, D)],
            [
                ((BLOCKS, PATCH, LANES), BF16),
                ((PATCH, D), F32),
                ((PATCH, D), BF16),
                ((PATCH, LANES), BF16),
                ((PATCH, LANES), BF16),
                ((LANES, PATCH), BF16),
                ((BLOCKS, D, LANES), BF16),
                ((2, 4, EXT, LANES), BF16),
                *projection,
            ],
            ln_gain,
            late=(o_near, o_far, near, far, w_mir, w_mir_far, w_turned, share_far, rest_far, shares),
            semaphores=(3, 16, 5), megabytes=52,
        )
        halos = [lax.ppermute(kv, AXES, links) for kv, links in zip(kvs, (inner, outer))]
        parts = None
        for part in range(2):
            kv = kvs[part]
            (parts,) = call(
                functools.partial(second_kernel, part),
                3 if part else 0,
                [(8 if part else 4, ROWS, LANES)],
                [
                    ((PATCH, 2 * LANES), BF16),
                    ((2, HEAD_DIM + 16, PATCH), BF16),
                    ((HALF, LANES), BF16),
                ],
                queries, kv, halos[part], *([parts] if part else []),
                megabytes=8,
            )
        parts, w_last = lax.optimization_barrier((parts, w_last))
        parts = lax.all_to_all(parts, ("y", "c"), 0, 0, tiled=True)
        (result,) = call(
            last_kernel, 1.5, [(ROWS, D)], [((ROWS, D), BF16)],
            parts, w_last, stream, megabytes=8,
        )
        return result

    every = ("z", "xl") + head_axes
    return jax.shard_map(
        on_device,
        mesh=Mesh(mesh.devices.reshape(shape), AXES),
        in_specs=(P(every, None), P(every, None), P(every), P(), P(None, None, head_axes), P(None, head_axes, None)),
        out_specs=P(every, None),
        check_vma=False,
    )
```

```python
import functools

import jax
import jax.numpy as jnp
import numpy as np
from jax import lax
from jax.experimental import pallas as pl
from jax.experimental.pallas import tpu as pltpu
from jax.sharding import Mesh
from jax.sharding import PartitionSpec as P

HEAD_DIM = 64
D = 1024
ROWS = 128
PATCH = 1024
HALF = 512
LANES = 128
BLOCKS = D // LANES
EXT = D + 16
QKV_PART = 3 * HEAD_DIM // 2
OUT_PART = HEAD_DIM // 2
FULL = EXT + BLOCKS * HEAD_DIM
EPSILON = 1e-05
FAR = -1e30
AXES = ("z", "xl", "xh", "y", "c")
F32 = jnp.float32
BF16 = jnp.bfloat16


def pairs(shape, move):
    result = []
    for i in range(int(np.prod(shape))):
        place = tuple(int(v) for v in np.unravel_index(i, shape))
        result.append((i, int(np.ravel_multi_index(move(*place), shape))))
    return result


def dot(a, b):
    return lax.dot_general(a, b, (((1,), (0,)), ((), ())), preferred_element_type=F32)


def dot_nt(a, b):
    return lax.dot_general(a, b, (((1,), (1,)), ((), ())), preferred_element_type=F32)


def layer_norm(values, gain):
    center = values - jnp.mean(values, axis=-1, keepdims=True)
    spread = jnp.mean(center * center, axis=-1, keepdims=True)
    return (center * lax.rsqrt(spread + EPSILON) * gain).astype(BF16)


def side_by_side(ref, index):
    return jnp.concatenate([ref[index, b * LANES : (b + 1) * LANES, :] for b in range(BLOCKS)], axis=1)


def tag_columns(rows):
    return jnp.transpose(jnp.concatenate(rows, axis=0))


def one_hot(columns, block):
    lane = lax.broadcasted_iota(jnp.int32, (ROWS, LANES), 1).astype(F32)
    return columns[:, block : block + 1] == lane


def attend(queries, hot, keys_ref, values_ref):
    lane = lax.broadcasted_iota(jnp.int32, queries.shape, 1)
    pieces = [slice(k * 256, (k + 1) * 256) for k in range(4)]
    scores = []
    for head in range(2):
        own = jnp.where(lane // HEAD_DIM == head, queries, jnp.zeros_like(queries))
        both = jnp.concatenate([own, hot], axis=1)
        scores.append([dot_nt(keys_ref[piece, :], both) for piece in pieces])
    results = []
    for head in range(2):
        tops = [jnp.max(part, axis=0, keepdims=True) for part in scores[head]]
        top = functools.reduce(jnp.maximum, tops)
        sums = sum(
            dot(values_ref[head, :, piece], jnp.exp(part - top).astype(BF16))
            for part, piece in zip(scores[head], pieces)
        )
        results.append(sums[:HEAD_DIM] / sums[HEAD_DIM : HEAD_DIM + 1])
    return jnp.transpose(jnp.concatenate(results, axis=0)).astype(BF16)


def fetch(sources, targets, sems):
    copies = [pltpu.make_async_copy(a, b, sems.at[i]) for i, (a, b) in enumerate(zip(sources, targets))]
    for copy in copies:
        copy.start()
    return copies


def order_kernel(points_at, order_at, tags_at, w_at, out, points, order, tags, w, sems):
    copies = fetch((order_at, points_at, tags_at, w_at.at[0]), (order, points, tags, w), sems)
    for copy in copies:
        copy.wait()
    row = lax.broadcasted_iota(jnp.int32, (ROWS, ROWS), 0)
    picks = jnp.transpose((row == order[...]).astype(F32)).astype(BF16)
    ordered = dot(picks, points[...]).astype(BF16)
    tag_rows = jnp.broadcast_to(tags[...].astype(F32), (16, LANES)).astype(BF16)
    for copy in range(4):
        for b in range(BLOCKS):
            out[copy, b * LANES : (b + 1) * LANES, :] = ordered[:, b * LANES : (b + 1) * LANES]
            out[copy, EXT + b * HEAD_DIM : EXT + (b + 1) * HEAD_DIM, :] = w[:, b * LANES : (b + 1) * LANES]
        out[copy, D:EXT, :] = tag_rows


def joined(own, mirrored, kind):
    cut = slice(kind * HEAD_DIM, (kind + 1) * HEAD_DIM)
    return jnp.concatenate([own[cut, :], mirrored[cut, :]], axis=0)


def project(normed, own, mirrored, queries, keys, turned):
    every = jnp.concatenate([joined(own, mirrored, kind) for kind in range(3)], axis=0)
    found = dot_nt(normed, every)
    queries[...] = found[:, :LANES].astype(BF16) * jnp.asarray(HEAD_DIM**-0.5, BF16)
    keys[...] = found[:, LANES : 2 * LANES].astype(BF16)
    turned[...] = jnp.transpose(found[:, 2 * LANES :]).astype(BF16)


def put_values(values_ref, span, turned, swap):
    for head in range(2):
        from_head = 1 - head if swap else head
        values_ref[head, :HEAD_DIM, span] = turned[from_head * HEAD_DIM : (from_head + 1) * HEAD_DIM]


def first_kernel(
    gain, near, far, own, mirrored_at, out,
    normed, queries, keys, turned, values, hots, mirrored, sems,
):
    (copy,) = fetch((mirrored_at.at[: 3 * HEAD_DIM],), (mirrored,), sems)
    rows = []
    for block in range(8):
        ref, y = (near, far)[block // 4], block % 4
        normed[block * ROWS : (block + 1) * ROWS, :] = layer_norm(
            side_by_side(ref, y).astype(F32), gain[0:1, :]
        )
        rows.append(ref[y, D:EXT, :].astype(F32)[:1])
    columns = tag_columns(rows)
    copy.wait()
    project(normed[...], own.at[0], mirrored, queries, keys.at[:, :LANES], turned)
    put_values(values, slice(0, PATCH), turned, False)
    values[:, HEAD_DIM:, :] = jnp.ones((2, 16, PATCH), BF16)
    for block in range(8):
        hot = one_hot(columns, block)
        span = slice(block * ROWS, (block + 1) * ROWS)
        hots[span, :] = jnp.where(hot, 1.0, 0.0).astype(BF16)
        keys[span, LANES:] = jnp.where(hot, 0.0, FAR).astype(BF16)
    for part in range(4):
        span = slice(part * 256, (part + 1) * 256)
        result = attend(queries[span, :], hots[span, :], keys, values)
        for copy in range(4):
            out[copy, span, :] = result


def half_of(part):
    xh = lax.axis_index("xh")
    return xh if part else 1 - xh


def middle_kernel(
    gain, o_near, o_far, near, far, w_mir, w_mir_far, own_at, mine_at, other_at, ready,
    q_out, kv_p, kv_q, st_out,
    heads, update, normed, queries, keys, turned, w, points, own, mirrored,
    o_sems, w_sems, sems,
):
    my_y = lax.axis_index("y")
    sources, targets = [], []
    for i, ref in enumerate((near, w_mir, far, w_mir_far)):
        for g in range(4):
            row = (i // 2 * 4 + g) * LANES + i % 2 * HEAD_DIM
            if i % 2:
                sources.append(ref.at[g])
            else:
                sources.append(ref.at[g, EXT:FULL, :].reshape(BLOCKS, HEAD_DIM, LANES))
            targets.append(w.at[:, row : row + HEAD_DIM, :])
    w_copies = fetch(sources, targets, w_sems)

    xl = lax.axis_index("xl")
    at_mine, at_other = [
        pl.ds(pl.multiple_of(k * QKV_PART, QKV_PART), QKV_PART) for k in (xl, 1 - xl)
    ]
    top, end = slice(0, HALF), slice(HALF, PATCH)
    o_copies = fetch(
        (o_near, o_far.at[:, end, :], o_far.at[:, top, :]),
        (heads.at[:4], heads.at[4:, top, :], heads.at[4:, end, :]),
        o_sems,
    )
    x_copies = fetch((near.at[:, :EXT, :], far.at[:, :EXT, :]), (points.at[0], points.at[1]), sems)
    late = fetch(
        (own_at.at[1], mine_at.at[:QKV_PART], other_at.at[:QKV_PART]),
        (own, mirrored.at[at_mine, :], mirrored.at[at_other, :]),
        sems.at[2:5],
    )
    for copy in w_copies + o_copies:
        copy.wait()
    left = jnp.concatenate([heads[g] for g in range(BLOCKS)], axis=1)
    for j in range(2):
        both = jnp.concatenate([w[4 * j + i] for i in range(4)], axis=1)
        update[:, j * 512 : (j + 1) * 512] = dot(left, both)
    rows = []
    for s in range(2):
        x_copies[s].wait()
        for y in range(4):
            there = slice(s * HALF + y * ROWS, s * HALF + (y + 1) * ROWS)
            x = jnp.concatenate(
                [points[s, y, b * LANES : (b + 1) * LANES, :] for b in range(BLOCKS)], axis=1
            )
            stream = (x.astype(F32) + update[there, :]).astype(BF16)
            normed[there, :] = layer_norm(stream.astype(F32), gain[1:2, :])
            rows.append(points[s, y, D:, :].astype(F32)[:1])
            if s == 0:

                @pl.when(y == my_y)
                def _(stream=stream):
                    st_out[...] = stream

    for copy in late:
        copy.wait()
    project(normed[...], own, mirrored, queries, keys, turned)
    for part, kv in enumerate((kv_p, kv_q)):
        half = half_of(part)
        for s in range(2):
            at = pl.multiple_of(s * HALF + half * 256, 256)
            q_out[part, s * 256 : (s + 1) * 256, :] = queries[pl.ds(at, 256), :]
            kv[s * 256 : (s + 1) * 256, :] = keys[pl.ds(at, 256), :]
            for b in range(2):
                cut = slice(HALF + (s * 2 + b) * LANES, HALF + (s * 2 + b + 1) * LANES)
                kv[cut, :] = turned[:, pl.ds(pl.multiple_of(at + b * LANES, LANES), LANES)]
        tags = [jnp.where(half == 0, rows[s * 4 + b], rows[s * 4 + 2 + b]) for s in range(2) for b in range(2)]
        kv[D:, :] = jnp.concatenate(tags + [jnp.zeros((12, LANES), F32)], axis=0).astype(BF16)


def second_kernel(part, *refs):
    if part:
        queries, mine, other, had, out, keys, values, hots = refs
    else:
        queries, mine, other, out, keys, values, hots = refs
    half, c = half_of(part), lax.axis_index("c")
    keys[:HALF, :LANES] = mine[:HALF, :]
    keys[HALF:, :HEAD_DIM] = other[:HALF, HEAD_DIM:]
    keys[HALF:, HEAD_DIM:LANES] = other[:HALF, :HEAD_DIM]
    for b in range(4):
        cut = slice(HALF + b * LANES, HALF + (b + 1) * LANES)
        put_values(values, slice(b * LANES, (b + 1) * LANES), mine[cut, :], False)
        put_values(values, slice(HALF + b * LANES, HALF + (b + 1) * LANES), other[cut, :], True)
    values[:, HEAD_DIM:, :] = jnp.ones((2, 16, PATCH), BF16)
    columns = tag_columns([mine[D:, :].astype(F32)[:4], other[D:, :].astype(F32)[:4]])
    for block in range(8):
        hot = one_hot(columns, block)
        span = slice(block * ROWS, (block + 1) * ROWS)
        if block < 4:
            hots[span, :] = jnp.where(hot, 1.0, 0.0).astype(BF16)
        keys[span, LANES:] = jnp.where(hot, 0.0, FAR).astype(BF16)
    for s in range(2):
        span = slice(s * 256, (s + 1) * 256)
        result = attend(queries[part, span, :], hots[span, :], keys, values)
        core = c if s == 0 else 1 - c
        for yy in range(2):
            block = result[yy * ROWS : (yy + 1) * ROWS]
            if part:
                out[(half * 2 + yy) * 2 + core] = block
                out[((1 - half) * 2 + yy) * 2 + core] = had[s * 2 + yy]
            else:
                out[s * 2 + yy] = block


def last_kernel(parts, w, stream, out, heads):
    for g in range(8):
        heads[:, g * LANES : (g + 1) * LANES] = parts[g]
    update = dot(heads[...], w[...])

    out[...] = (stream[...].astype(F32) + update).astype(BF16)


def relay_kernel(own, mine, other, out):
    xl = lax.axis_index("xl")
    at_mine, at_other = [
        pl.ds(pl.multiple_of(HEAD_DIM + k * OUT_PART, OUT_PART), OUT_PART) for k in (xl, 1 - xl)
    ]
    for copy in range(out.shape[0]):
        out[copy, :HEAD_DIM] = own[...]
        out[copy, at_mine, :] = mine[QKV_PART:]
        out[copy, at_other, :] = other[QKV_PART:]


def call(kernel, micros, outs, scratch, *args, late=(), semaphores=(), megabytes=16):
    vmem, anywhere = pl.BlockSpec(memory_space=pltpu.VMEM), pl.BlockSpec(memory_space=pl.ANY)
    return pl.pallas_call(
        kernel,
        out_shape=[jax.ShapeDtypeStruct(shape, BF16) for shape in outs],
        in_specs=[vmem] * len(args) + [anywhere] * len(late),
        out_specs=[vmem] * len(outs),
        scratch_shapes=[pltpu.VMEM(shape, dtype) for shape, dtype in scratch]
        + [
            pltpu.SemaphoreType.DMA(count if isinstance(count, tuple) else (count,))
            for count in semaphores
        ],
        compiler_params=pltpu.CompilerParams(vmem_limit_bytes=megabytes * 1024 * 1024),
        cost_estimate=pl.CostEstimate(
            flops=int(micros * 1.1e9), bytes_accessed=0, transcendentals=0
        ),
    )(*args, *late)


def solution(mesh):
    curve, heads = mesh.shape["curve"], mesh.shape["head"]
    shape = (curve // 2, 2, 2, heads // 4, 2)
    deep = shape[0]
    head_axes = ("xh", "y", "c")
    other_core = pairs(shape, lambda z, xl, xh, y, c: (z, xl, xh, y, 1 - c))
    mirror = pairs(shape, lambda z, xl, xh, y, c: (z, 1 - xl, 1 - xh, y, c))
    beside = pairs(shape, lambda z, xl, xh, y, c: (z, 1 - xl, xh, y, c))
    inner = pairs(shape, lambda z, xl, xh, y, c: (z, xl, 1 - xh, y, c))

    def across(z, xl, xh, y, c):
        here = z * 2 + xl
        there = (here + (1 if xh else -1)) % (2 * deep)
        return there // 2, there % 2, 1 - xh, y, c

    outer = pairs(shape, across)

    def over_y(copies):
        return lax.all_to_all(copies, "y", 0, 0, tiled=True)

    def swapped(array):
        return lax.ppermute(array, AXES, other_core)

    def on_device(points, order, scan_ids, ln_gain, w_qkv, w_out):
        w_turned = jnp.swapaxes(w_qkv, 1, 2)
        (copies,) = call(
            order_kernel, 1.2, [(4, FULL, LANES)],
            [
                ((ROWS, D), BF16), ((1, ROWS), jnp.int32), ((1, ROWS), jnp.int32),
                ((HEAD_DIM, D), BF16),
            ],
            late=(points, order, scan_ids.reshape(1, ROWS), w_out), semaphores=(4,), megabytes=56,
        )
        share = 1 - lax.axis_index("xl")
        first = jnp.concatenate(
            [
                w_turned[0],
                lax.dynamic_slice_in_dim(w_turned[1], share * QKV_PART, QKV_PART, 0),
                lax.dynamic_slice_in_dim(w_out[1], share * OUT_PART, OUT_PART, 0),
            ],
            axis=0,
        )
        first_far = lax.ppermute(first, AXES, mirror)
        near = over_y(copies)
        near, first_far = lax.optimization_barrier((near, first_far))
        far = swapped(near)

        projection = [((3 * HEAD_DIM, D), BF16)] * 2
        (o_copies,) = call(
            first_kernel,
            8,
            [(4, PATCH, LANES)],
            [
                ((PATCH, D), BF16),
                ((PATCH, LANES), BF16),
                ((PATCH, 2 * LANES), BF16),
                ((LANES, PATCH), BF16),
                ((2, HEAD_DIM + 16, PATCH), BF16),
                ((PATCH, LANES), BF16),
                ((3 * HEAD_DIM, D), BF16),
            ],
            ln_gain, near, far, w_turned, late=(first_far,), semaphores=(1,), megabytes=16,
        )
        w_own = near[:, EXT:].reshape(4, BLOCKS, HEAD_DIM, LANES)
        share_far = first_far[3 * HEAD_DIM :]
        o_copies, w_own, share_far = lax.optimization_barrier((o_copies, w_own, share_far))
        rest_far = lax.ppermute(share_far, AXES, beside)
        w_mir = lax.ppermute(w_own, AXES, mirror)
        (shares,) = call(
            relay_kernel, 1, [(8, ROWS, D)], [], w_out[1], share_far, rest_far, megabytes=4
        )
        o_near, w_mir, rest_far, shares = lax.optimization_barrier(
            (over_y(o_copies), w_mir, rest_far, shares)
        )
        o_far = swapped(o_near)
        w_mir_far = swapped(w_mir)
        w_last = lax.all_to_all(shares, ("y", "c"), 0, 0, tiled=True).reshape(D, D)
        queries, *kvs, stream = call(
            middle_kernel,
            8,
            [(2, HALF, LANES), (EXT, LANES), (EXT, LANES), (ROWS, D)],
            [
                ((BLOCKS, PATCH, LANES), BF16),
                ((PATCH, D), F32),
                ((PATCH, D), BF16),
                ((PATCH, LANES), BF16),
                ((PATCH, LANES), BF16),
                ((LANES, PATCH), BF16),
                ((BLOCKS, D, LANES), BF16),
                ((2, 4, EXT, LANES), BF16),
                *projection,
            ],
            ln_gain,
            late=(o_near, o_far, near, far, w_mir, w_mir_far, w_turned, share_far, rest_far, shares),
            semaphores=(3, 16, 5), megabytes=52,
        )
        halos = [lax.ppermute(kv, AXES, links) for kv, links in zip(kvs, (inner, outer))]
        parts = None
        for part in range(2):
            kv = kvs[part]
            (parts,) = call(
                functools.partial(second_kernel, part),
                3 if part else 0,
                [(8 if part else 4, ROWS, LANES)],
                [
                    ((PATCH, 2 * LANES), BF16),
                    ((2, HEAD_DIM + 16, PATCH), BF16),
                    ((HALF, LANES), BF16),
                ],
                queries, kv, halos[part], *([parts] if part else []),
                megabytes=8,
            )
        parts, w_last = lax.optimization_barrier((parts, w_last))
        parts = lax.all_to_all(parts, ("y", "c"), 0, 0, tiled=True)
        (result,) = call(
            last_kernel, 1.5, [(ROWS, D)], [((ROWS, D), BF16)],
            parts, w_last, stream, megabytes=8,
        )
        return result

    every = ("z", "xl") + head_axes
    return jax.shard_map(
        on_device,
        mesh=Mesh(mesh.devices.reshape(shape), AXES),
        in_specs=(P(every, None), P(every, None), P(every), P(), P(None, None, head_axes), P(None, head_axes, None)),
        out_specs=P(every, None),
        check_vma=False,
    )
```

```python
import functools

import jax
import jax.numpy as jnp
import numpy as np
from jax import lax
from jax.experimental import pallas as pl
from jax.experimental.pallas import tpu as pltpu
from jax.sharding import Mesh
from jax.sharding import PartitionSpec as P

HEAD_DIM = 64
D = 1024
ROWS = 128
PATCH = 1024
HALF = 512
LANES = 128
BLOCKS = D // LANES
EXT = D + 16
QKV_PART = 3 * HEAD_DIM // 2
OUT_PART = HEAD_DIM // 2
FULL = EXT + BLOCKS * HEAD_DIM
EPSILON = 1e-05
FAR = -1e30
AXES = ("z", "xl", "xh", "y", "c")
F32 = jnp.float32
BF16 = jnp.bfloat16


def pairs(shape, move):
    result = []
    for i in range(int(np.prod(shape))):
        place = tuple(int(v) for v in np.unravel_index(i, shape))
        result.append((i, int(np.ravel_multi_index(move(*place), shape))))
    return result


def dot(a, b):
    return lax.dot_general(a, b, (((1,), (0,)), ((), ())), preferred_element_type=F32)


def dot_nt(a, b):
    return lax.dot_general(a, b, (((1,), (1,)), ((), ())), preferred_element_type=F32)


def layer_norm(values, gain):
    center = values - jnp.mean(values, axis=-1, keepdims=True)
    spread = jnp.mean(center * center, axis=-1, keepdims=True)
    return (center * lax.rsqrt(spread + EPSILON) * gain).astype(BF16)


def side_by_side(ref, index):
    return jnp.concatenate([ref[index, b * LANES : (b + 1) * LANES, :] for b in range(BLOCKS)], axis=1)


def tag_columns(rows):
    return jnp.transpose(jnp.concatenate(rows, axis=0))


def one_hot(columns, block):
    lane = lax.broadcasted_iota(jnp.int32, (ROWS, LANES), 1).astype(F32)
    return columns[:, block : block + 1] == lane


def attend(queries, hot, keys_ref, values_ref):
    lane = lax.broadcasted_iota(jnp.int32, queries.shape, 1)
    pieces = [slice(k * 256, (k + 1) * 256) for k in range(4)]
    scores = []
    for head in range(2):
        own = jnp.where(lane // HEAD_DIM == head, queries, jnp.zeros_like(queries))
        both = jnp.concatenate([own, hot], axis=1)
        scores.append([dot_nt(keys_ref[piece, :], both) for piece in pieces])
    results = []
    for head in range(2):
        tops = [jnp.max(part, axis=0, keepdims=True) for part in scores[head]]
        top = functools.reduce(jnp.maximum, tops)
        sums = sum(
            dot(values_ref[head, :, piece], jnp.exp(part - top).astype(BF16))
            for part, piece in zip(scores[head], pieces)
        )
        results.append(sums[:HEAD_DIM] / sums[HEAD_DIM : HEAD_DIM + 1])
    return jnp.transpose(jnp.concatenate(results, axis=0)).astype(BF16)


def fetch(sources, targets, sems):
    copies = [pltpu.make_async_copy(a, b, sems.at[i]) for i, (a, b) in enumerate(zip(sources, targets))]
    for copy in copies:
        copy.start()
    return copies


def order_kernel(points_at, order_at, tags_at, w_at, out, points, order, tags, w, sems):
    copies = fetch((order_at, points_at, tags_at, w_at.at[0]), (order, points, tags, w), sems)
    for copy in copies:
        copy.wait()
    row = lax.broadcasted_iota(jnp.int32, (ROWS, ROWS), 0)
    picks = jnp.transpose((row == order[...]).astype(F32)).astype(BF16)
    ordered = dot(picks, points[...]).astype(BF16)
    tag_rows = jnp.broadcast_to(tags[...].astype(F32), (16, LANES)).astype(BF16)
    for copy in range(4):
        for b in range(BLOCKS):
            out[copy, b * LANES : (b + 1) * LANES, :] = ordered[:, b * LANES : (b + 1) * LANES]
            out[copy, EXT + b * HEAD_DIM : EXT + (b + 1) * HEAD_DIM, :] = w[:, b * LANES : (b + 1) * LANES]
        out[copy, D:EXT, :] = tag_rows


def joined(own, mirrored, kind):
    cut = slice(kind * HEAD_DIM, (kind + 1) * HEAD_DIM)
    return jnp.concatenate([own[cut, :], mirrored[cut, :]], axis=0)


def project(normed, own, mirrored, queries, keys, turned):
    every = jnp.concatenate([joined(own, mirrored, kind) for kind in range(3)], axis=0)
    found = dot_nt(normed, every)
    queries[...] = found[:, :LANES].astype(BF16) * jnp.asarray(HEAD_DIM**-0.5, BF16)
    keys[...] = found[:, LANES : 2 * LANES].astype(BF16)
    turned[...] = jnp.transpose(found[:, 2 * LANES :]).astype(BF16)


def put_values(values_ref, span, turned, swap):
    for head in range(2):
        from_head = 1 - head if swap else head
        values_ref[head, :HEAD_DIM, span] = turned[from_head * HEAD_DIM : (from_head + 1) * HEAD_DIM]


def first_kernel(
    gain, near, far, own, mirrored_at, out,
    normed, queries, keys, turned, values, hots, mirrored, sems,
):
    (copy,) = fetch((mirrored_at.at[: 3 * HEAD_DIM],), (mirrored,), sems)
    rows = []
    for block in range(8):
        ref, y = (near, far)[block // 4], block % 4
        normed[block * ROWS : (block + 1) * ROWS, :] = layer_norm(
            side_by_side(ref, y).astype(F32), gain[0:1, :]
        )
        rows.append(ref[y, D:EXT, :].astype(F32)[:1])
    columns = tag_columns(rows)
    copy.wait()
    project(normed[...], own.at[0], mirrored, queries, keys.at[:, :LANES], turned)
    put_values(values, slice(0, PATCH), turned, False)
    values[:, HEAD_DIM:, :] = jnp.ones((2, 16, PATCH), BF16)
    for block in range(8):
        hot = one_hot(columns, block)
        span = slice(block * ROWS, (block + 1) * ROWS)
        hots[span, :] = jnp.where(hot, 1.0, 0.0).astype(BF16)
        keys[span, LANES:] = jnp.where(hot, 0.0, FAR).astype(BF16)
    for part in range(4):
        span = slice(part * 256, (part + 1) * 256)
        result = attend(queries[span, :], hots[span, :], keys, values)
        for copy in range(4):
            out[copy, span, :] = result


def half_of(part):
    xh = lax.axis_index("xh")
    return xh if part else 1 - xh


def middle_kernel(
    gain, o_near, o_far, near, far, w_mir, w_mir_far, own_at, mine_at, other_at, ready,
    q_out, kv_p, kv_q, st_out,
    heads, update, normed, queries, keys, turned, w, points, own, mirrored,
    o_sems, w_sems, sems,
):
    my_y = lax.axis_index("y")
    sources, targets = [], []
    for i, ref in enumerate((near, w_mir, far, w_mir_far)):
        for g in range(4):
            row = (i // 2 * 4 + g) * LANES + i % 2 * HEAD_DIM
            if i % 2:
                sources.append(ref.at[g])
            else:
                sources.append(ref.at[g, EXT:FULL, :].reshape(BLOCKS, HEAD_DIM, LANES))
            targets.append(w.at[:, row : row + HEAD_DIM, :])
    w_copies = fetch(sources, targets, w_sems)

    xl = lax.axis_index("xl")
    at_mine, at_other = [
        pl.ds(pl.multiple_of(k * QKV_PART, QKV_PART), QKV_PART) for k in (xl, 1 - xl)
    ]
    top, end = slice(0, HALF), slice(HALF, PATCH)
    o_copies = fetch(
        (o_near, o_far.at[:, end, :], o_far.at[:, top, :]),
        (heads.at[:4], heads.at[4:, top, :], heads.at[4:, end, :]),
        o_sems,
    )
    x_copies = fetch((near.at[:, :EXT, :], far.at[:, :EXT, :]), (points.at[0], points.at[1]), sems)
    late = fetch(
        (own_at.at[1], mine_at.at[:QKV_PART], other_at.at[:QKV_PART]),
        (own, mirrored.at[at_mine, :], mirrored.at[at_other, :]),
        sems.at[2:5],
    )
    for copy in w_copies + o_copies:
        copy.wait()
    left = jnp.concatenate([heads[g] for g in range(BLOCKS)], axis=1)
    for j in range(2):
        both = jnp.concatenate([w[4 * j + i] for i in range(4)], axis=1)
        update[:, j * 512 : (j + 1) * 512] = dot(left, both)
    rows = []
    for s in range(2):
        x_copies[s].wait()
        for y in range(4):
            there = slice(s * HALF + y * ROWS, s * HALF + (y + 1) * ROWS)
            x = jnp.concatenate(
                [points[s, y, b * LANES : (b + 1) * LANES, :] for b in range(BLOCKS)], axis=1
            )
            stream = (x.astype(F32) + update[there, :]).astype(BF16)
            normed[there, :] = layer_norm(stream.astype(F32), gain[1:2, :])
            rows.append(points[s, y, D:, :].astype(F32)[:1])
            if s == 0:

                @pl.when(y == my_y)
                def _(stream=stream):
                    st_out[...] = stream

    for copy in late:
        copy.wait()
    project(normed[...], own, mirrored, queries, keys, turned)
    for part, kv in enumerate((kv_p, kv_q)):
        half = half_of(part)
        for s in range(2):
            at = pl.multiple_of(s * HALF + half * 256, 256)
            q_out[part, s * 256 : (s + 1) * 256, :] = queries[pl.ds(at, 256), :]
            kv[s * 256 : (s + 1) * 256, :] = keys[pl.ds(at, 256), :]
            for b in range(2):
                cut = slice(HALF + (s * 2 + b) * LANES, HALF + (s * 2 + b + 1) * LANES)
                kv[cut, :] = turned[:, pl.ds(pl.multiple_of(at + b * LANES, LANES), LANES)]
        tags = [jnp.where(half == 0, rows[s * 4 + b], rows[s * 4 + 2 + b]) for s in range(2) for b in range(2)]
        kv[D:, :] = jnp.concatenate(tags + [jnp.zeros((12, LANES), F32)], axis=0).astype(BF16)


def second_kernel(part, *refs):
    if part:
        queries, mine, other, had, out, keys, values, hots = refs
    else:
        queries, mine, other, out, keys, values, hots = refs
    half, c = half_of(part), lax.axis_index("c")
    keys[:HALF, :LANES] = mine[:HALF, :]
    keys[HALF:, :HEAD_DIM] = other[:HALF, HEAD_DIM:]
    keys[HALF:, HEAD_DIM:LANES] = other[:HALF, :HEAD_DIM]
    for b in range(4):
        cut = slice(HALF + b * LANES, HALF + (b + 1) * LANES)
        put_values(values, slice(b * LANES, (b + 1) * LANES), mine[cut, :], False)
        put_values(values, slice(HALF + b * LANES, HALF + (b + 1) * LANES), other[cut, :], True)
    values[:, HEAD_DIM:, :] = jnp.ones((2, 16, PATCH), BF16)
    columns = tag_columns([mine[D:, :].astype(F32)[:4], other[D:, :].astype(F32)[:4]])
    for block in range(8):
        hot = one_hot(columns, block)
        span = slice(block * ROWS, (block + 1) * ROWS)
        if block < 4:
            hots[span, :] = jnp.where(hot, 1.0, 0.0).astype(BF16)
        keys[span, LANES:] = jnp.where(hot, 0.0, FAR).astype(BF16)
    for s in range(2):
        span = slice(s * 256, (s + 1) * 256)
        result = attend(queries[part, span, :], hots[span, :], keys, values)
        core = c if s == 0 else 1 - c
        for yy in range(2):
            block = result[yy * ROWS : (yy + 1) * ROWS]
            if part:
                out[(half * 2 + yy) * 2 + core] = block
                out[((1 - half) * 2 + yy) * 2 + core] = had[s * 2 + yy]
            else:
                out[s * 2 + yy] = block


def last_kernel(parts, w, stream, out, heads):
    for g in range(8):
        heads[:, g * LANES : (g + 1) * LANES] = parts[g]
    update = dot(heads[...], w[...])

    out[...] = (stream[...].astype(F32) + update).astype(BF16)


def relay_kernel(own, mine, other, out):
    xl = lax.axis_index("xl")
    at_mine, at_other = [
        pl.ds(pl.multiple_of(HEAD_DIM + k * OUT_PART, OUT_PART), OUT_PART) for k in (xl, 1 - xl)
    ]
    for copy in range(out.shape[0]):
        out[copy, :HEAD_DIM] = own[...]
        out[copy, at_mine, :] = mine[QKV_PART:]
        out[copy, at_other, :] = other[QKV_PART:]


def call(kernel, micros, outs, scratch, *args, late=(), semaphores=(), megabytes=16):
    vmem, anywhere = pl.BlockSpec(memory_space=pltpu.VMEM), pl.BlockSpec(memory_space=pl.ANY)
    return pl.pallas_call(
        kernel,
        out_shape=[jax.ShapeDtypeStruct(shape, BF16) for shape in outs],
        in_specs=[vmem] * len(args) + [anywhere] * len(late),
        out_specs=[vmem] * len(outs),
        scratch_shapes=[pltpu.VMEM(shape, dtype) for shape, dtype in scratch]
        + [
            pltpu.SemaphoreType.DMA(count if isinstance(count, tuple) else (count,))
            for count in semaphores
        ],
        compiler_params=pltpu.CompilerParams(vmem_limit_bytes=megabytes * 1024 * 1024),
        cost_estimate=pl.CostEstimate(
            flops=int(micros * 1.1e9), bytes_accessed=0, transcendentals=0
        ),
    )(*args, *late)


def solution(mesh):
    curve, heads = mesh.shape["curve"], mesh.shape["head"]
    shape = (curve // 2, 2, 2, heads // 4, 2)
    deep = shape[0]
    head_axes = ("xh", "y", "c")
    other_core = pairs(shape, lambda z, xl, xh, y, c: (z, xl, xh, y, 1 - c))
    mirror = pairs(shape, lambda z, xl, xh, y, c: (z, 1 - xl, 1 - xh, y, c))
    beside = pairs(shape, lambda z, xl, xh, y, c: (z, 1 - xl, xh, y, c))
    inner = pairs(shape, lambda z, xl, xh, y, c: (z, xl, 1 - xh, y, c))

    def across(z, xl, xh, y, c):
        here = z * 2 + xl
        there = (here + (1 if xh else -1)) % (2 * deep)
        return there // 2, there % 2, 1 - xh, y, c

    outer = pairs(shape, across)

    def over_y(copies):
        return lax.all_to_all(copies, "y", 0, 0, tiled=True)

    def swapped(array):
        return lax.ppermute(array, AXES, other_core)

    def on_device(points, order, scan_ids, ln_gain, w_qkv, w_out):
        w_turned = jnp.swapaxes(w_qkv, 1, 2)
        (copies,) = call(
            order_kernel, 1.2, [(4, FULL, LANES)],
            [
                ((ROWS, D), BF16), ((1, ROWS), jnp.int32), ((1, ROWS), jnp.int32),
                ((HEAD_DIM, D), BF16),
            ],
            late=(points, order, scan_ids.reshape(1, ROWS), w_out), semaphores=(4,), megabytes=56,
        )
        share = 1 - lax.axis_index("xl")
        first = jnp.concatenate(
            [
                w_turned[0],
                lax.dynamic_slice_in_dim(w_turned[1], share * QKV_PART, QKV_PART, 0),
                lax.dynamic_slice_in_dim(w_out[1], share * OUT_PART, OUT_PART, 0),
            ],
            axis=0,
        )
        first_far = lax.ppermute(first, AXES, mirror)
        near = over_y(copies)
        near, first_far = lax.optimization_barrier((near, first_far))
        far = swapped(near)

        projection = [((3 * HEAD_DIM, D), BF16)] * 2
        (o_copies,) = call(
            first_kernel,
            8,
            [(4, PATCH, LANES)],
            [
                ((PATCH, D), BF16),
                ((PATCH, LANES), BF16),
                ((PATCH, 2 * LANES), BF16),
                ((LANES, PATCH), BF16),
                ((2, HEAD_DIM + 16, PATCH), BF16),
                ((PATCH, LANES), BF16),
                ((3 * HEAD_DIM, D), BF16),
            ],
            ln_gain, near, far, w_turned, late=(first_far,), semaphores=(1,), megabytes=16,
        )
        w_own = near[:, EXT:].reshape(4, BLOCKS, HEAD_DIM, LANES)
        share_far = first_far[3 * HEAD_DIM :]
        rest_far = lax.ppermute(share_far, AXES, beside)
        o_copies, w_own, rest_far = lax.optimization_barrier((o_copies, w_own, rest_far))
        w_mir = lax.ppermute(w_own, AXES, mirror)
        (shares,) = call(
            relay_kernel, 1, [(8, ROWS, D)], [], w_out[1], share_far, rest_far, megabytes=4
        )
        o_near, shares = lax.optimization_barrier((over_y(o_copies), shares))
        o_far = swapped(o_near)
        w_mir_far = swapped(w_mir)
        w_last = lax.all_to_all(shares, ("y", "c"), 0, 0, tiled=True).reshape(D, D)
        queries, *kvs, stream = call(
            middle_kernel,
            8,
            [(2, HALF, LANES), (EXT, LANES), (EXT, LANES), (ROWS, D)],
            [
                ((BLOCKS, PATCH, LANES), BF16),
                ((PATCH, D), F32),
                ((PATCH, D), BF16),
                ((PATCH, LANES), BF16),
                ((PATCH, LANES), BF16),
                ((LANES, PATCH), BF16),
                ((BLOCKS, D, LANES), BF16),
                ((2, 4, EXT, LANES), BF16),
                *projection,
            ],
            ln_gain,
            late=(o_near, o_far, near, far, w_mir, w_mir_far, w_turned, share_far, rest_far, shares),
            semaphores=(3, 16, 5), megabytes=52,
        )
        halos = [lax.ppermute(kv, AXES, links) for kv, links in zip(kvs, (inner, outer))]
        parts = None
        for part in range(2):
            kv = kvs[part]
            (parts,) = call(
                functools.partial(second_kernel, part),
                3 if part else 0,
                [(8 if part else 4, ROWS, LANES)],
                [
                    ((PATCH, 2 * LANES), BF16),
                    ((2, HEAD_DIM + 16, PATCH), BF16),
                    ((HALF, LANES), BF16),
                ],
                queries, kv, halos[part], *([parts] if part else []),
                megabytes=8,
            )
        parts, w_last = lax.optimization_barrier((parts, w_last))
        parts = lax.all_to_all(parts, ("y", "c"), 0, 0, tiled=True)
        (result,) = call(
            last_kernel, 1.5, [(ROWS, D)], [((ROWS, D), BF16)],
            parts, w_last, stream, megabytes=8,
        )
        return result

    every = ("z", "xl") + head_axes
    return jax.shard_map(
        on_device,
        mesh=Mesh(mesh.devices.reshape(shape), AXES),
        in_specs=(P(every, None), P(every, None), P(every), P(), P(None, None, head_axes), P(None, head_axes, None)),
        out_specs=P(every, None),
        check_vma=False,
    )
```

```python
import functools

import jax
import jax.numpy as jnp
import numpy as np
from jax import lax
from jax.experimental import pallas as pl
from jax.experimental.pallas import tpu as pltpu
from jax.sharding import Mesh
from jax.sharding import PartitionSpec as P

HEAD_DIM = 64
D = 1024
ROWS = 128
PATCH = 1024
HALF = 512
LANES = 128
BLOCKS = D // LANES
EXT = D + 16
QKV_PART = 3 * HEAD_DIM // 2
OUT_PART = HEAD_DIM // 2
FULL = EXT + BLOCKS * HEAD_DIM
EPSILON = 1e-05
FAR = -1e30
AXES = ("z", "xl", "xh", "y", "c")
F32 = jnp.float32
BF16 = jnp.bfloat16


def pairs(shape, move):
    result = []
    for i in range(int(np.prod(shape))):
        place = tuple(int(v) for v in np.unravel_index(i, shape))
        result.append((i, int(np.ravel_multi_index(move(*place), shape))))
    return result


def dot(a, b):
    return lax.dot_general(a, b, (((1,), (0,)), ((), ())), preferred_element_type=F32)


def dot_nt(a, b):
    return lax.dot_general(a, b, (((1,), (1,)), ((), ())), preferred_element_type=F32)


def layer_norm(values, gain):
    center = values - jnp.mean(values, axis=-1, keepdims=True)
    spread = jnp.mean(center * center, axis=-1, keepdims=True)
    return (center * lax.rsqrt(spread + EPSILON) * gain).astype(BF16)


def side_by_side(ref, index):
    return jnp.concatenate([ref[index, b * LANES : (b + 1) * LANES, :] for b in range(BLOCKS)], axis=1)


def tag_columns(rows):
    return jnp.transpose(jnp.concatenate(rows, axis=0))


def one_hot(columns, block):
    lane = lax.broadcasted_iota(jnp.int32, (ROWS, LANES), 1).astype(F32)
    return columns[:, block : block + 1] == lane


def attend(queries, hot, keys_ref, values_ref):
    lane = lax.broadcasted_iota(jnp.int32, queries.shape, 1)
    pieces = [slice(k * 256, (k + 1) * 256) for k in range(4)]
    scores = []
    for head in range(2):
        own = jnp.where(lane // HEAD_DIM == head, queries, jnp.zeros_like(queries))
        both = jnp.concatenate([own, hot], axis=1)
        scores.append([dot_nt(keys_ref[piece, :], both) for piece in pieces])
    results = []
    for head in range(2):
        tops = [jnp.max(part, axis=0, keepdims=True) for part in scores[head]]
        top = functools.reduce(jnp.maximum, tops)
        sums = sum(
            dot(values_ref[head, :, piece], jnp.exp(part - top).astype(BF16))
            for part, piece in zip(scores[head], pieces)
        )
        results.append(sums[:HEAD_DIM] / sums[HEAD_DIM : HEAD_DIM + 1])
    return jnp.transpose(jnp.concatenate(results, axis=0)).astype(BF16)


def fetch(sources, targets, sems):
    copies = [pltpu.make_async_copy(a, b, sems.at[i]) for i, (a, b) in enumerate(zip(sources, targets))]
    for copy in copies:
        copy.start()
    return copies


def order_kernel(points_at, order_at, tags_at, w_at, out, points, order, tags, w, sems):
    copies = fetch((order_at, points_at, tags_at, w_at.at[0]), (order, points, tags, w), sems)
    for copy in copies:
        copy.wait()
    row = lax.broadcasted_iota(jnp.int32, (ROWS, ROWS), 0)
    picks = jnp.transpose((row == order[...]).astype(F32)).astype(BF16)
    ordered = dot(picks, points[...]).astype(BF16)
    tag_rows = jnp.broadcast_to(tags[...].astype(F32), (16, LANES)).astype(BF16)
    for copy in range(4):
        for b in range(BLOCKS):
            out[copy, b * LANES : (b + 1) * LANES, :] = ordered[:, b * LANES : (b + 1) * LANES]
            out[copy, EXT + b * HEAD_DIM : EXT + (b + 1) * HEAD_DIM, :] = w[:, b * LANES : (b + 1) * LANES]
        out[copy, D:EXT, :] = tag_rows


def joined(own, mirrored, kind):
    cut = slice(kind * HEAD_DIM, (kind + 1) * HEAD_DIM)
    return jnp.concatenate([own[cut, :], mirrored[cut, :]], axis=0)


def project(normed, own, mirrored, queries, keys, turned):
    every = jnp.concatenate([joined(own, mirrored, kind) for kind in range(3)], axis=0)
    found = dot_nt(normed, every)
    queries[...] = found[:, :LANES].astype(BF16) * jnp.asarray(HEAD_DIM**-0.5, BF16)
    keys[...] = found[:, LANES : 2 * LANES].astype(BF16)
    turned[...] = jnp.transpose(found[:, 2 * LANES :]).astype(BF16)


def put_values(values_ref, span, turned, swap):
    for head in range(2):
        from_head = 1 - head if swap else head
        values_ref[head, :HEAD_DIM, span] = turned[from_head * HEAD_DIM : (from_head + 1) * HEAD_DIM]


def first_kernel(
    gain, near, far, own, mirrored_at, out,
    normed, queries, keys, turned, values, hots, mirrored, sems,
):
    (copy,) = fetch((mirrored_at.at[: 3 * HEAD_DIM],), (mirrored,), sems)
    rows = []
    for block in range(8):
        ref, y = (near, far)[block // 4], block % 4
        normed[block * ROWS : (block + 1) * ROWS, :] = layer_norm(
            side_by_side(ref, y).astype(F32), gain[0:1, :]
        )
        rows.append(ref[y, D:EXT, :].astype(F32)[:1])
    columns = tag_columns(rows)
    copy.wait()
    project(normed[...], own.at[0], mirrored, queries, keys.at[:, :LANES], turned)
    put_values(values, slice(0, PATCH), turned, False)
    values[:, HEAD_DIM:, :] = jnp.ones((2, 16, PATCH), BF16)
    for block in range(8):
        hot = one_hot(columns, block)
        span = slice(block * ROWS, (block + 1) * ROWS)
        hots[span, :] = jnp.where(hot, 1.0, 0.0).astype(BF16)
        keys[span, LANES:] = jnp.where(hot, 0.0, FAR).astype(BF16)
    for part in range(4):
        span = slice(part * 256, (part + 1) * 256)
        result = attend(queries[span, :], hots[span, :], keys, values)
        for copy in range(4):
            out[copy, span, :] = result


def half_of(part):
    xh = lax.axis_index("xh")
    return xh if part else 1 - xh


def middle_kernel(
    gain, o_near, o_far, near, far, w_mir, w_mir_far, own_at, mine_at, other_at, ready,
    q_out, kv_p, kv_q, st_out,
    heads, update, normed, queries, keys, turned, w, points, own, mirrored,
    o_sems, w_sems, sems,
):
    my_y = lax.axis_index("y")
    sources, targets = [], []
    for i, ref in enumerate((near, w_mir, far, w_mir_far)):
        for g in range(4):
            row = (i // 2 * 4 + g) * LANES + i % 2 * HEAD_DIM
            if i % 2:
                sources.append(ref.at[g])
            else:
                sources.append(ref.at[g, EXT:FULL, :].reshape(BLOCKS, HEAD_DIM, LANES))
            targets.append(w.at[:, row : row + HEAD_DIM, :])
    w_copies = fetch(sources[:8], targets[:8], w_sems.at[:8])
    o_copies = fetch((o_near,), (heads.at[:4],), o_sems.at[:1])
    w_copies += fetch(sources[8:], targets[8:], w_sems.at[8:])
    xl = lax.axis_index("xl")
    at_mine, at_other = [
        pl.ds(pl.multiple_of(k * QKV_PART, QKV_PART), QKV_PART) for k in (xl, 1 - xl)
    ]
    top, end = slice(0, HALF), slice(HALF, PATCH)
    o_copies += fetch(
        (o_far.at[:, end, :], o_far.at[:, top, :]),
        (heads.at[4:, top, :], heads.at[4:, end, :]),
        o_sems.at[1:],
    )
    x_copies = fetch((near.at[:, :EXT, :], far.at[:, :EXT, :]), (points.at[0], points.at[1]), sems)
    late = fetch(
        (own_at.at[1], mine_at.at[:QKV_PART], other_at.at[:QKV_PART]),
        (own, mirrored.at[at_mine, :], mirrored.at[at_other, :]),
        sems.at[2:5],
    )
    for side in range(2):
        for copy in w_copies[side * 8 : (side + 1) * 8] + (o_copies[1:] if side else o_copies[:1]):
            copy.wait()
        depth = slice(side * HALF, (side + 1) * HALF)
        left = jnp.concatenate([heads[side * 4 + g] for g in range(4)], axis=1)
        for j in range(2):
            both = jnp.concatenate([w[4 * j + i, depth, :] for i in range(4)], axis=1)
            cut = slice(j * HALF, (j + 1) * HALF)
            product = dot(left, both)
            update[:, cut] = update[:, cut] + product if side else product
    rows = []
    for s in range(2):
        x_copies[s].wait()
        for y in range(4):
            there = slice(s * HALF + y * ROWS, s * HALF + (y + 1) * ROWS)
            x = jnp.concatenate(
                [points[s, y, b * LANES : (b + 1) * LANES, :] for b in range(BLOCKS)], axis=1
            )
            stream = (x.astype(F32) + update[there, :]).astype(BF16)
            normed[there, :] = layer_norm(stream.astype(F32), gain[1:2, :])
            rows.append(points[s, y, D:, :].astype(F32)[:1])
            if s == 0:

                @pl.when(y == my_y)
                def _(stream=stream):
                    st_out[...] = stream

    for copy in late:
        copy.wait()
    project(normed[...], own, mirrored, queries, keys, turned)
    for part, kv in enumerate((kv_p, kv_q)):
        half = half_of(part)
        for s in range(2):
            at = pl.multiple_of(s * HALF + half * 256, 256)
            q_out[part, s * 256 : (s + 1) * 256, :] = queries[pl.ds(at, 256), :]
            kv[s * 256 : (s + 1) * 256, :] = keys[pl.ds(at, 256), :]
            for b in range(2):
                cut = slice(HALF + (s * 2 + b) * LANES, HALF + (s * 2 + b + 1) * LANES)
                kv[cut, :] = turned[:, pl.ds(pl.multiple_of(at + b * LANES, LANES), LANES)]
        tags = [jnp.where(half == 0, rows[s * 4 + b], rows[s * 4 + 2 + b]) for s in range(2) for b in range(2)]
        kv[D:, :] = jnp.concatenate(tags + [jnp.zeros((12, LANES), F32)], axis=0).astype(BF16)


def second_kernel(part, *refs):
    if part:
        queries, mine, other, had, out, keys, values, hots = refs
    else:
        queries, mine, other, out, keys, values, hots = refs
    half, c = half_of(part), lax.axis_index("c")
    keys[:HALF, :LANES] = mine[:HALF, :]
    keys[HALF:, :HEAD_DIM] = other[:HALF, HEAD_DIM:]
    keys[HALF:, HEAD_DIM:LANES] = other[:HALF, :HEAD_DIM]
    for b in range(4):
        cut = slice(HALF + b * LANES, HALF + (b + 1) * LANES)
        put_values(values, slice(b * LANES, (b + 1) * LANES), mine[cut, :], False)
        put_values(values, slice(HALF + b * LANES, HALF + (b + 1) * LANES), other[cut, :], True)
    values[:, HEAD_DIM:, :] = jnp.ones((2, 16, PATCH), BF16)
    columns = tag_columns([mine[D:, :].astype(F32)[:4], other[D:, :].astype(F32)[:4]])
    for block in range(8):
        hot = one_hot(columns, block)
        span = slice(block * ROWS, (block + 1) * ROWS)
        if block < 4:
            hots[span, :] = jnp.where(hot, 1.0, 0.0).astype(BF16)
        keys[span, LANES:] = jnp.where(hot, 0.0, FAR).astype(BF16)
    for s in range(2):
        span = slice(s * 256, (s + 1) * 256)
        result = attend(queries[part, span, :], hots[span, :], keys, values)
        core = c if s == 0 else 1 - c
        for yy in range(2):
            block = result[yy * ROWS : (yy + 1) * ROWS]
            if part:
                out[(half * 2 + yy) * 2 + core] = block
                out[((1 - half) * 2 + yy) * 2 + core] = had[s * 2 + yy]
            else:
                out[s * 2 + yy] = block


def last_kernel(parts, w, stream, out, heads):
    for g in range(8):
        heads[:, g * LANES : (g + 1) * LANES] = parts[g]
    update = dot(heads[...], w[...])

    out[...] = (stream[...].astype(F32) + update).astype(BF16)


def relay_kernel(own, mine, other, out):
    xl = lax.axis_index("xl")
    at_mine, at_other = [
        pl.ds(pl.multiple_of(HEAD_DIM + k * OUT_PART, OUT_PART), OUT_PART) for k in (xl, 1 - xl)
    ]
    for copy in range(out.shape[0]):
        out[copy, :HEAD_DIM] = own[...]
        out[copy, at_mine, :] = mine[QKV_PART:]
        out[copy, at_other, :] = other[QKV_PART:]


def call(kernel, micros, outs, scratch, *args, late=(), semaphores=(), megabytes=16):
    vmem, anywhere = pl.BlockSpec(memory_space=pltpu.VMEM), pl.BlockSpec(memory_space=pl.ANY)
    return pl.pallas_call(
        kernel,
        out_shape=[jax.ShapeDtypeStruct(shape, BF16) for shape in outs],
        in_specs=[vmem] * len(args) + [anywhere] * len(late),
        out_specs=[vmem] * len(outs),
        scratch_shapes=[pltpu.VMEM(shape, dtype) for shape, dtype in scratch]
        + [
            pltpu.SemaphoreType.DMA(count if isinstance(count, tuple) else (count,))
            for count in semaphores
        ],
        compiler_params=pltpu.CompilerParams(vmem_limit_bytes=megabytes * 1024 * 1024),
        cost_estimate=pl.CostEstimate(
            flops=int(micros * 1.1e9), bytes_accessed=0, transcendentals=0
        ),
    )(*args, *late)


def solution(mesh):
    curve, heads = mesh.shape["curve"], mesh.shape["head"]
    shape = (curve // 2, 2, 2, heads // 4, 2)
    deep = shape[0]
    head_axes = ("xh", "y", "c")
    other_core = pairs(shape, lambda z, xl, xh, y, c: (z, xl, xh, y, 1 - c))
    mirror = pairs(shape, lambda z, xl, xh, y, c: (z, 1 - xl, 1 - xh, y, c))
    beside = pairs(shape, lambda z, xl, xh, y, c: (z, 1 - xl, xh, y, c))
    inner = pairs(shape, lambda z, xl, xh, y, c: (z, xl, 1 - xh, y, c))

    def across(z, xl, xh, y, c):
        here = z * 2 + xl
        there = (here + (1 if xh else -1)) % (2 * deep)
        return there // 2, there % 2, 1 - xh, y, c

    outer = pairs(shape, across)

    def over_y(copies):
        return lax.all_to_all(copies, "y", 0, 0, tiled=True)

    def swapped(array):
        return lax.ppermute(array, AXES, other_core)

    def on_device(points, order, scan_ids, ln_gain, w_qkv, w_out):
        w_turned = jnp.swapaxes(w_qkv, 1, 2)
        (copies,) = call(
            order_kernel, 1.2, [(4, FULL, LANES)],
            [
                ((ROWS, D), BF16), ((1, ROWS), jnp.int32), ((1, ROWS), jnp.int32),
                ((HEAD_DIM, D), BF16),
            ],
            late=(points, order, scan_ids.reshape(1, ROWS), w_out), semaphores=(4,), megabytes=56,
        )
        share = 1 - lax.axis_index("xl")
        first = jnp.concatenate(
            [
                w_turned[0],
                lax.dynamic_slice_in_dim(w_turned[1], share * QKV_PART, QKV_PART, 0),
                lax.dynamic_slice_in_dim(w_out[1], share * OUT_PART, OUT_PART, 0),
            ],
            axis=0,
        )
        first_far = lax.ppermute(first, AXES, mirror)
        near = over_y(copies)
        near, first_far = lax.optimization_barrier((near, first_far))
        far = swapped(near)

        projection = [((3 * HEAD_DIM, D), BF16)] * 2
        (o_copies,) = call(
            first_kernel,
            8,
            [(4, PATCH, LANES)],
            [
                ((PATCH, D), BF16),
                ((PATCH, LANES), BF16),
                ((PATCH, 2 * LANES), BF16),
                ((LANES, PATCH), BF16),
                ((2, HEAD_DIM + 16, PATCH), BF16),
                ((PATCH, LANES), BF16),
                ((3 * HEAD_DIM, D), BF16),
            ],
            ln_gain, near, far, w_turned, late=(first_far,), semaphores=(1,), megabytes=16,
        )
        w_own = near[:, EXT:].reshape(4, BLOCKS, HEAD_DIM, LANES)
        share_far = first_far[3 * HEAD_DIM :]
        rest_far = lax.ppermute(share_far, AXES, beside)
        o_copies, w_own, rest_far = lax.optimization_barrier((o_copies, w_own, rest_far))
        w_mir = lax.ppermute(w_own, AXES, mirror)
        (shares,) = call(
            relay_kernel, 1, [(8, ROWS, D)], [], w_out[1], share_far, rest_far, megabytes=4
        )
        o_near, shares = lax.optimization_barrier((over_y(o_copies), shares))
        o_far = swapped(o_near)
        w_mir_far = swapped(w_mir)
        w_last = lax.all_to_all(shares, ("y", "c"), 0, 0, tiled=True).reshape(D, D)
        queries, *kvs, stream = call(
            middle_kernel,
            8,
            [(2, HALF, LANES), (EXT, LANES), (EXT, LANES), (ROWS, D)],
            [
                ((BLOCKS, PATCH, LANES), BF16),
                ((PATCH, D), F32),
                ((PATCH, D), BF16),
                ((PATCH, LANES), BF16),
                ((PATCH, LANES), BF16),
                ((LANES, PATCH), BF16),
                ((BLOCKS, D, LANES), BF16),
                ((2, 4, EXT, LANES), BF16),
                *projection,
            ],
            ln_gain,
            late=(o_near, o_far, near, far, w_mir, w_mir_far, w_turned, share_far, rest_far, shares),
            semaphores=(3, 16, 5), megabytes=52,
        )
        halos = [lax.ppermute(kv, AXES, links) for kv, links in zip(kvs, (inner, outer))]
        parts = None
        for part in range(2):
            kv = kvs[part]
            (parts,) = call(
                functools.partial(second_kernel, part),
                3 if part else 0,
                [(8 if part else 4, ROWS, LANES)],
                [
                    ((PATCH, 2 * LANES), BF16),
                    ((2, HEAD_DIM + 16, PATCH), BF16),
                    ((HALF, LANES), BF16),
                ],
                queries, kv, halos[part], *([parts] if part else []),
                megabytes=8,
            )
        parts, w_last = lax.optimization_barrier((parts, w_last))
        parts = lax.all_to_all(parts, ("y", "c"), 0, 0, tiled=True)
        (result,) = call(
            last_kernel, 1.5, [(ROWS, D)], [((ROWS, D), BF16)],
            parts, w_last, stream, megabytes=8,
        )
        return result

    every = ("z", "xl") + head_axes
    return jax.shard_map(
        on_device,
        mesh=Mesh(mesh.devices.reshape(shape), AXES),
        in_specs=(P(every, None), P(every, None), P(every), P(), P(None, None, head_axes), P(None, head_axes, None)),
        out_specs=P(every, None),
        check_vma=False,
    )
```
